32 devices in a mesh: src: 2 (over x), tgt: 4 (over z), feat: 4 (over y, core).
Axes of the slice: x: 2, y: 2, z: 4, core: 2. Of those that a mesh axis runs over, the one named last changes fastest.
Arguments:
- errors: bfloat16 [8, 1024, 2048], P('tgt', 'feat', 'src'), may hold values from -0.796875 to 0.796875
- saved_codes: bfloat16 [8, 1024, 2048], P('src', None, 'feat'), may hold values from 0 to 2
- active_mask: int32 [8, 1024, 2048], P('src', 'tgt', 'feat'), may hold values 0 or 1
- decoder: bfloat16 [8, 8, 2048, 2048], P('src', 'tgt', 'feat'), may hold values from -0.125 to 0.125
Outputs:
- code_grads: bfloat16 [8, 1024, 2048], P('src', 'tgt', 'feat')
- decoder_grads: bfloat16 [8, 8, 2048, 2048], P('src', 'tgt', 'feat')
The draws below stay inside these ranges and needn't reach their ends.
All inputs are finite; a program needn't handle non-finite values. No bound on the sum of `active_mask` on one device may be relied on, other than what follows from the above.
Results may differ from the reference program's by a relative error of at most 0.001.
Values may be sent and summed in bfloat16 or wider, within the bound.
No kernel may reach another device: no remote copies, remote signals or barrier semaphores. Data moves between devices by JAX's collectives and lax.ppermute only.
A program may use at most 128 MiB of HBM per device.

```python
import jax
import jax.numpy as jnp

D = 2048
LAYERS = 8
TOKENS = 1024
FEATS = 2048


def plant(array, own_key, least, high):
    dims = array.shape
    spot = [jax.random.randint(jax.random.fold_in(own_key, axis), (), 0, dims[axis]) for axis in range(len(dims))]
    array = array.at[tuple(spot)].set(least)
    longest = dims.index(max(dims))
    spot[longest] = (spot[longest] + 1) % dims[longest]
    return array.at[tuple(spot)].set(high)


def block_scale(own_key, extent, split, least, high):
    loudness, own = 1.0, jax.random.fold_in(own_key, 6)
    for position, shards_of in split:
        steps = jnp.exp(jax.random.uniform(jax.random.fold_in(own, position), (shards_of,), jnp.float32, least / len(split), high / len(split)))
        loudness = loudness * jnp.repeat(steps, extent[position] // shards_of).reshape([-1 if axis == position else 1 for axis in range(len(extent))])
    return loudness


def bell_draw(key, extent, spread, most, pieces=(), dtype=jnp.bfloat16):
    array = spread * jax.random.normal(key, extent, jnp.float32)
    if pieces:
        array = array * block_scale(key, extent, pieces, -0.22, 0.18)
    return jnp.clip(array, -most, most).astype(dtype)


def setup_inputs(seed: int = 0) -> dict:
    keys = jax.random.split(jax.random.key(seed), 5)
    return {
        "errors": bell_draw(keys[0], (LAYERS, TOKENS, D), 0.1, 0.796875, ((0, 4), (1, 4), (2, 2))),
        "saved_codes": jnp.clip(2.0 * jax.random.uniform(keys[1], (LAYERS, TOKENS, FEATS), jnp.float32) ** block_scale(keys[1], (LAYERS, TOKENS, FEATS), ((0, 2), (2, 4)), -0.2, 0.2), 0.0, 2.0).astype(jnp.bfloat16),
        "active_mask": plant((jax.random.randint(keys[2], (LAYERS, TOKENS, FEATS), 0, 3) < 1).astype(jnp.int32), jax.random.fold_in(keys[2], 1), 0, 1),
        "decoder": bell_draw(keys[3], (LAYERS, LAYERS, FEATS, D), FEATS ** -0.5, 0.125, ((0, 2), (1, 4), (2, 4))),
    }


def reference(errors, saved_codes, active_mask, decoder):
    grad_rows = []
    code_rows = []
    for src_layer in range(LAYERS):
        tile_row = []
        summed = jnp.zeros((TOKENS, FEATS), jnp.float32)
        for tgt_layer in range(LAYERS):
            if tgt_layer >= src_layer:
                tile = jnp.dot(saved_codes[src_layer].T, errors[tgt_layer], preferred_element_type=jnp.float32)
                tile_row.append(tile.astype(jnp.bfloat16))
                summed = summed + jnp.dot(errors[tgt_layer], decoder[src_layer, tgt_layer].T, preferred_element_type=jnp.float32)
            else:
                tile_row.append(jnp.zeros((FEATS, D), jnp.bfloat16))
        grad_rows.append(jnp.stack(tile_row))
        code_rows.append((summed * active_mask[src_layer].astype(jnp.float32)).astype(jnp.bfloat16))
    return jnp.stack(code_rows), jnp.stack(grad_rows)
```

```python
import functools

import jax
import jax.numpy as jnp
from jax import lax
from jax.experimental import pallas as pl
from jax.experimental.pallas import tpu as pltpu
from jax.sharding import PartitionSpec as P

LANES = 128
SUBLANES = 8
STEPS_PER_OCTAVE = 64
TOP = 32760.0
FLOOR = 1e-30
EIGHTHS = (2, 2, 2, 2)
MIB = 1 << 20


def quantize(v, out_ref, lead, layer):
    rows, width = v.shape
    half, tiles = rows // 2, width // LANES
    peak = jnp.maximum(jnp.max(jnp.abs(v), axis=1, keepdims=True), FLOOR)
    scale = jnp.ceil(jnp.log2(peak) * STEPS_PER_OCTAVE)
    gain = jnp.exp2(scale * (-1.0 / STEPS_PER_OCTAVE)) * TOP
    q = jnp.floor(v * gain + 0.5).astype(jnp.int32)
    scale = scale.astype(jnp.int32)
    words = (q[half:] << 16) | (q[:half] & 0xFFFF)
    scale_words = (scale[half:] << 16) | (scale[:half] & 0xFFFF)
    for tile in range(tiles):
        start = (layer * tiles + tile) * half
        if not isinstance(start, int):
            start = pl.multiple_of(start, SUBLANES)
        out_ref[lead, pl.ds(start, half), :] = words[:, tile * LANES : (tile + 1) * LANES]
    end = out_ref.shape[1] - SUBLANES
    lane = lax.broadcasted_iota(jnp.int32, (SUBLANES, LANES), 1)
    tail = out_ref[lead, pl.ds(end, SUBLANES), :]
    for group in range(half // SUBLANES):
        piece = scale_words[group * SUBLANES : (group + 1) * SUBLANES]
        tail = jnp.where(lane == layer * (half // SUBLANES) + group, piece, tail)
    out_ref[lead, pl.ds(end, SUBLANES), :] = tail


def dequantize(in_ref, lead, layer, rows, width):
    half, tiles = rows // 2, width // LANES
    groups = half // SUBLANES
    end = in_ref.shape[1] - SUBLANES
    words = jnp.concatenate(
        [in_ref[lead, pl.ds((layer * tiles + tile) * half, half), :] for tile in range(tiles)], axis=1
    )
    tail = in_ref[lead, pl.ds(end, SUBLANES), :]
    scale_words = jnp.concatenate(
        [tail[:, layer * groups + group : layer * groups + group + 1] for group in range(groups)], axis=0
    )

    def step(scale):
        return jnp.exp2(scale.astype(jnp.float32) * (1.0 / STEPS_PER_OCTAVE)) * (1.0 / TOP)

    low = ((words << 16) >> 16).astype(jnp.float32) * step((scale_words << 16) >> 16)
    high = (words >> 16).astype(jnp.float32) * step(scale_words >> 16)
    return jnp.concatenate([low, high], axis=0)


def payload_rows(layers, rows, width):
    return layers * (width // LANES) * (rows // 2) + SUBLANES


def terms_kernel(n_tgt, n_pieces, place, keep, order, *refs):
    pieces = refs[:n_pieces]
    dec_ref, own_ref, send_ref, err_ref, acc = refs[n_pieces:]
    layer = pl.program_id(0)
    tgt_count, total_rows, _ = err_ref.shape
    rows = total_rows // n_tgt
    width = acc.shape[1]

    @pl.when(layer == 0)
    def _():
        for index, piece in enumerate(pieces):
            _, tokens, columns = piece.shape
            row = pl.multiple_of(place[2 * index] * tokens, tokens)
            column = pl.multiple_of(place[2 * index + 1] * columns, columns)
            for tgt in range(tgt_count):
                err_ref[tgt, pl.ds(row, tokens), pl.ds(column, columns)] = piece[tgt]
        for lead in range(n_tgt - 1):
            send_ref[lead, pl.ds(send_ref.shape[1] - SUBLANES, SUBLANES), :] = jnp.zeros((SUBLANES, LANES), jnp.int32)

    acc[...] = jnp.zeros_like(acc)
    for tgt in range(tgt_count):

        @pl.when(keep[layer * tgt_count + tgt] == 1)
        def _():
            acc[...] += lax.dot_general(
                err_ref[tgt], dec_ref[0, tgt], (((1,), (1,)), ((), ())), preferred_element_type=jnp.float32
            )

    own_ref[0] = acc[...]
    for lead in range(n_tgt - 1):
        start = pl.multiple_of(order[lead] * rows, rows)
        quantize(acc[pl.ds(start, rows), :], send_ref, lead, layer)


def terms_call(pieces, place, keep, order, decoder, n_tgt, total_rows):
    src_count, tgt_count, width, columns = decoder.shape
    rows = total_rows // n_tgt
    payload = (n_tgt - 1, payload_rows(src_count, rows, width), LANES)
    whole = lambda shape: pl.BlockSpec(shape, lambda i, *_: (0,) * len(shape))
    return pl.pallas_call(
        functools.partial(terms_kernel, n_tgt, len(pieces)),
        grid_spec=pltpu.PrefetchScalarGridSpec(
            num_scalar_prefetch=3,
            grid=(src_count,),
            in_specs=[whole(piece.shape) for piece in pieces]
            + [pl.BlockSpec((1, tgt_count, width, columns), lambda i, *_: (i, 0, 0, 0))],
            out_specs=[
                pl.BlockSpec((1, total_rows, width), lambda i, *_: (i, 0, 0)),
                whole(payload),
                whole((tgt_count, total_rows, columns)),
            ],
            scratch_shapes=[pltpu.VMEM((total_rows, width), jnp.float32)],
        ),
        out_shape=[
            jax.ShapeDtypeStruct((src_count, total_rows, width), jnp.float32),
            jax.ShapeDtypeStruct(payload, jnp.int32),
            jax.ShapeDtypeStruct((tgt_count, total_rows, columns), jnp.bfloat16),
        ],
        compiler_params=pltpu.CompilerParams(vmem_limit_bytes=48 * MIB),
        cost_estimate=pl.CostEstimate(
            flops=2 * total_rows * width * columns * src_count * tgt_count,
            bytes_accessed=decoder.size * 2 + src_count * total_rows * width * 4 + 4 * total_rows * columns * tgt_count,
            transcendentals=0,
        ),
        name="terms",
    )(place, keep, order, *pieces, decoder)


def relay_kernel(order, own_ref, got_ref, send_ref):
    src_count, rows, width = own_ref.shape
    send_ref[0, pl.ds(send_ref.shape[1] - SUBLANES, SUBLANES), :] = jnp.zeros((SUBLANES, LANES), jnp.int32)
    for layer in range(src_count):
        quantize(own_ref[layer] + dequantize(got_ref, 0, layer, rows, width), send_ref, 0, layer)


def relay_call(order, own, got, n_tgt):
    src_count, total_rows, width = own.shape
    rows = total_rows // n_tgt
    blocks, length, _ = got.shape
    return pl.pallas_call(
        relay_kernel,
        grid_spec=pltpu.PrefetchScalarGridSpec(
            num_scalar_prefetch=1,
            grid=(blocks - 1,),
            in_specs=[
                pl.BlockSpec((src_count, rows, width), lambda i, order: (0, order[i], 0)),
                pl.BlockSpec((1, length, LANES), lambda i, order: (i, 0, 0)),
            ],
            out_specs=pl.BlockSpec((1, length, LANES), lambda i, order: (i, 0, 0)),
        ),
        out_shape=jax.ShapeDtypeStruct((blocks - 1, length, LANES), jnp.int32),
        compiler_params=pltpu.CompilerParams(vmem_limit_bytes=24 * MIB),
        cost_estimate=pl.CostEstimate(
            flops=20 * src_count * rows * width * (blocks - 1),
            bytes_accessed=(blocks - 1) * (8 * length * LANES + 4 * src_count * rows * width),
            transcendentals=0,
        ),
        name="relay",
    )(order, own, got)


def finish_kernel(n_got, offset, stride, here, own_ref, *refs):
    gots = refs[:n_got]
    mask_ref, out_ref, mask_tile, out_tile, in_sem, out_sem = refs[n_got : n_got + 1] + refs[-5:]
    src_count, rows, width = own_ref.shape
    parts = mask_ref.shape[1] // stride
    tokens = rows // parts

    def mask_copy(part):
        return pltpu.make_async_copy(
            mask_ref.at[:, pl.ds(part * stride + offset, tokens), :],
            mask_tile.at[:, pl.ds(part * tokens, tokens), :],
            in_sem.at[part],
        )

    def out_copy(part):
        return pltpu.make_async_copy(
            out_tile.at[:, pl.ds(part * tokens, tokens), :],
            out_ref.at[:, pl.ds(part * stride + offset, tokens), :],
            out_sem.at[part],
        )

    for part in range(parts):
        mask_copy(part).start()
    for part in range(parts):
        mask_copy(part).wait()
    for layer in range(src_count):
        total = own_ref[layer]
        for got in gots:
            total += dequantize(got, 0, layer, rows, width)
        out_tile[layer] = (total * mask_tile[layer].astype(jnp.float32)).astype(jnp.bfloat16)
    for part in range(parts):
        out_copy(part).start()
    for part in range(parts):
        out_copy(part).wait()


def finish_call(here, own, gots, mask, out, offset, stride, n_tgt):
    src_count, total_rows, width = own.shape
    rows = total_rows // n_tgt
    parts = mask.shape[1] // stride
    length = gots[0].shape[1]
    anywhere = pl.BlockSpec(memory_space=pl.ANY)
    in_specs = [pl.BlockSpec((src_count, rows, width), lambda i, here: (0, here[0], 0))]
    for got in gots:
        last = got.shape[0] - 1
        in_specs.append(pl.BlockSpec((1, length, LANES), lambda i, here, last=last: (last, 0, 0)))
    in_specs.append(anywhere)
    operands = [here, own, *gots, mask]
    aliases = {}
    if out is not None:
        in_specs.append(anywhere)
        aliases = {len(operands): 0}
        operands.append(out)
    return pl.pallas_call(
        functools.partial(finish_kernel, len(gots), offset, stride),
        grid_spec=pltpu.PrefetchScalarGridSpec(
            num_scalar_prefetch=1,
            grid=(1,),
            in_specs=in_specs,
            out_specs=anywhere,
            scratch_shapes=[
                pltpu.VMEM((src_count, rows, width), jnp.int32),
                pltpu.VMEM((src_count, rows, width), jnp.bfloat16),
                pltpu.SemaphoreType.DMA((parts,)),
                pltpu.SemaphoreType.DMA((parts,)),
            ],
        ),
        out_shape=jax.ShapeDtypeStruct(mask.shape, jnp.bfloat16),
        input_output_aliases=aliases,
        compiler_params=pltpu.CompilerParams(vmem_limit_bytes=24 * MIB),
        cost_estimate=pl.CostEstimate(
            flops=20 * src_count * rows * width,
            bytes_accessed=src_count * rows * width * 10 + 4 * length * LANES * len(gots),
            transcendentals=0,
        ),
        name="finish",
    )(*operands)


def turn_kernel(spans, codes_ref, out_ref):
    tokens = codes_ref.shape[1]
    stride = sum(spans)
    blocks = tokens // stride
    offset = column = 0
    for span in spans:
        rows = jnp.concatenate(
            [codes_ref[0, pl.ds(block * stride + offset, span), :] for block in range(blocks)], axis=0
        )
        out_ref[0, :, pl.ds(column, blocks * span)] = rows.T
        offset += span
        column += blocks * span


def turn_call(codes, spans):
    src_count, tokens, width = codes.shape
    return pl.pallas_call(
        functools.partial(turn_kernel, spans),
        grid=(src_count,),
        in_specs=[pl.BlockSpec((1, tokens, width), lambda i: (i, 0, 0))],
        out_specs=pl.BlockSpec((1, width, tokens), lambda i: (i, 0, 0)),
        out_shape=jax.ShapeDtypeStruct((src_count, width, tokens), jnp.bfloat16),
        compiler_params=pltpu.CompilerParams(vmem_limit_bytes=24 * MIB),
        cost_estimate=pl.CostEstimate(flops=codes.size, bytes_accessed=codes.size * 4, transcendentals=0),
        name="turn",
    )(codes)


def grads_kernel(layer, n_chunks, keep, codes_ref, *refs):
    chunks = refs[:n_chunks]
    out_ref = refs[-2]
    acc = refs[-1]
    tgt = pl.program_id(0)
    kept = keep[layer * pl.num_programs(0) + tgt] == 1

    @pl.when(kept)
    def _():
        column = 0
        for index, chunk in enumerate(chunks):
            depth = chunk.shape[1]
            term = jnp.dot(
                codes_ref[0, :, pl.ds(column, depth)], chunk[0], preferred_element_type=jnp.float32
            )
            if index == 0:
                acc[...] = term
            elif index < n_chunks - 1:
                acc[...] += term
            else:
                out_ref[0, 0] = (acc[...] + term).astype(jnp.bfloat16)
            column += depth

    @pl.when(jnp.logical_not(kept))
    def _():
        out_ref[...] = jnp.zeros_like(out_ref)


def grads_call(layer, keep, codes_t, chunks, out, shape):
    src_count, tgt_count, width, columns = shape
    tokens = codes_t.shape[2]
    in_specs = [pl.BlockSpec((1, width, tokens), lambda i, *_: (layer, 0, 0))]
    for chunk in chunks:
        in_specs.append(pl.BlockSpec((1, chunk.shape[1], columns), lambda i, *_: (i, 0, 0)))
    operands = [keep, codes_t, *chunks]
    aliases = {}
    if out is not None:
        in_specs.append(pl.BlockSpec(memory_space=pl.ANY))
        aliases = {len(operands): 0}
        operands.append(out)
    return pl.pallas_call(
        functools.partial(grads_kernel, layer, len(chunks)),
        grid_spec=pltpu.PrefetchScalarGridSpec(
            num_scalar_prefetch=1,
            grid=(tgt_count,),
            in_specs=in_specs,
            out_specs=pl.BlockSpec((1, 1, width, columns), lambda i, *_: (layer, i, 0, 0)),
            scratch_shapes=[pltpu.VMEM((width, columns), jnp.float32)],
        ),
        out_shape=jax.ShapeDtypeStruct(shape, jnp.bfloat16),
        input_output_aliases=aliases,
        compiler_params=pltpu.CompilerParams(vmem_limit_bytes=48 * MIB),
        cost_estimate=pl.CostEstimate(
            flops=2 * tgt_count * width * columns * tokens,
            bytes_accessed=2 * tgt_count * (width * columns + tokens * columns) + 2 * width * tokens,
            transcendentals=0,
        ),
        name="grads",
    )(*operands)


def swap(x, axes, flips, sizes):
    pairs = []
    total = 1
    for size in sizes:
        total *= size
    for index in range(total):
        rest, other, weight = index, 0, 1
        for size, flip in reversed(list(zip(sizes, flips))):
            other += ((rest % size) ^ flip) * weight
            rest //= size
            weight *= size
        pairs.append((index, other))
    return lax.ppermute(x, axes, pairs)


def gather_pieces(part, chunk, n_src, n_feat):
    src, feat = lax.axis_index("src"), lax.axis_index("feat")
    if (n_src, n_feat) != (2, 4):
        columns = lax.all_gather(part, "src", axis=2, tiled=True)
        return [lax.all_gather(columns, "feat", axis=1, tiled=True)], [0, 0]
    over_x = lambda x: swap(x, "src", (1,), (n_src,))
    over_y = lambda x: swap(x, "feat", (2,), (n_feat,))
    over_core = lambda x: swap(x, "feat", (1,), (n_feat,))
    from_x, from_y = over_x(part), over_y(part)
    from_far = over_y(from_x) if chunk % 2 == 0 else over_x(from_y)
    pieces, place = [], []
    for piece, dx, dy in ((part, 0, 0), (from_x, 1, 0), (from_y, 0, 2), (from_far, 1, 2)):
        pieces += [piece, over_core(piece)]
        place += [feat ^ dy, src ^ dx, feat ^ dy ^ 1, src ^ dx]
    return pieces, place


def body(n_src, n_tgt, n_feat, errors, saved_codes, active_mask, decoder):
    src_count, tgt_count, width, _ = decoder.shape
    stride = errors.shape[1]
    src, tgt = lax.axis_index("src"), lax.axis_index("tgt")
    src_ids = src * src_count + jnp.arange(src_count, dtype=jnp.int32)
    tgt_ids = tgt * tgt_count + jnp.arange(tgt_count, dtype=jnp.int32)
    keep = (tgt_ids[None, :] >= src_ids[:, None]).astype(jnp.int32).reshape(-1)
    here = jnp.reshape(tgt, (1,)).astype(jnp.int32)
    lead = jnp.arange(n_tgt, dtype=jnp.int32)
    orders = [jnp.where(tgt == n_tgt - 1 - hop, lead, n_tgt - 1 - lead) for hop in range(n_tgt - 1)]

    spans = [stride * part // 8 for part in EIGHTHS]
    codes_t = turn_call(saved_codes, spans)
    code_grads = None
    chunks = []
    offset = 0
    for index, span in enumerate(spans):
        part = lax.slice_in_dim(errors, offset, offset + span, axis=1)
        pieces, place = gather_pieces(part, index, n_src, n_feat)
        place = jnp.stack([jnp.asarray(p, jnp.int32) for p in place])
        own, send, chunk = terms_call(pieces, place, keep, orders[0], decoder, n_tgt, n_feat * span)
        chunks.append(chunk)
        gots = []
        for hop in range(n_tgt - 1):
            if hop:
                send = relay_call(orders[hop], own, gots[-1], n_tgt)
            pairs = [(n_tgt - 1 - hop, n_tgt - 2 - hop), (hop, hop + 1)]
            gots.append(lax.ppermute(send, "tgt", pairs))
        code_grads = finish_call(here, own, gots, active_mask, code_grads, offset, stride, n_tgt)
        offset += span
    decoder_grads = None
    for layer in range(src_count):
        decoder_grads = grads_call(layer, keep, codes_t, chunks, decoder_grads, decoder.shape)
    return code_grads, decoder_grads


def solution(mesh):
    sizes = [mesh.shape[axis] for axis in ("src", "tgt", "feat")]
    in_specs = (
        P("tgt", "feat", "src"),
        P("src", None, "feat"),
        P("src", "tgt", "feat"),
        P("src", "tgt", "feat", None),
    )
    out_specs = (P("src", "tgt", "feat"), P("src", "tgt", "feat", None))
    return jax.shard_map(
        functools.partial(body, *sizes), mesh=mesh, in_specs=in_specs, out_specs=out_specs, check_vma=False
    )
```

```python
import functools

import jax
import jax.numpy as jnp
from jax import lax
from jax.experimental import pallas as pl
from jax.experimental.pallas import tpu as pltpu
from jax.sharding import PartitionSpec as P

LANES = 128
SUBLANES = 8
STEPS_PER_OCTAVE = 64
TOP = 32760.0
FLOOR = 1e-30
EIGHTHS = (3, 5)
VMEM = 60 << 20


def pair(x):
    half = x.shape[0] // 2
    return (x[half:] << 16) | (x[:half] & 0xFFFF)


def unpair(words):
    return (words << 16) >> 16, words >> 16


def scale_and_gain(peaks):
    scale = jnp.ceil(jnp.log2(jnp.maximum(peaks, FLOOR)) * STEPS_PER_OCTAVE)
    return scale.astype(jnp.int32), jnp.exp2(scale * (-1.0 / STEPS_PER_OCTAVE)) * TOP


def row_peak(v):
    return jnp.max(jnp.abs(v), axis=1, keepdims=True)


def store_words(out_ref, layer, v, gain):
    rows, width = v.shape
    half, tiles = rows // 2, width // LANES
    words = pair(jnp.floor(v * gain + 0.5).astype(jnp.int32))
    for tile in range(tiles):
        start = (layer * tiles + tile) * half
        if not isinstance(start, int):
            start = pl.multiple_of(start, SUBLANES)
        out_ref[pl.ds(start, half), :] = words[:, tile * LANES : (tile + 1) * LANES]


def lanes_of(shape):
    return lax.broadcasted_iota(jnp.int32, shape, 1)


def load_steps(in_ref):
    end = in_ref.shape[0] - SUBLANES
    low, high = unpair(in_ref[pl.ds(end, SUBLANES), :])
    step = lambda scale: jnp.exp2(scale.astype(jnp.float32) * (1.0 / STEPS_PER_OCTAVE)) * (1.0 / TOP)
    return step(low), step(high)


def load_values(in_ref, steps, layer, layers, rows, width):
    half, tiles = rows // 2, width // LANES
    words = jnp.concatenate(
        [in_ref[pl.ds((layer * tiles + tile) * half, half), :] for tile in range(tiles)], axis=1
    )
    values = []
    for part, step in zip(unpair(words), steps):
        column = jnp.concatenate(
            [step[:, group * layers + layer][:, None] for group in range(half // SUBLANES)], axis=0
        )
        values.append(part.astype(jnp.float32) * column)
    return jnp.concatenate(values, axis=0)


def payload_rows(layers, rows, width):
    return layers * (width // LANES) * (rows // 2) + SUBLANES


def terms_kernel(n_tgt, n_pieces, offset, place, keep, order, *refs):
    pieces = refs[:n_pieces]
    dec_ref = refs[n_pieces]
    own_ref = refs[-(n_tgt + 5)]
    sends = refs[-(n_tgt + 4) : -5]
    all_ref, err, acc, in_sem, out_sem = refs[-5:]
    layer, layers = pl.program_id(0), pl.num_programs(0)
    tgt_count, total_rows, _ = err.shape
    rows = total_rows // n_tgt
    half = rows // 2

    def in_copy(index):
        piece = pieces[index]
        _, tokens, columns = piece.shape
        row = pl.multiple_of(place[2 * index] * tokens, tokens)
        column = pl.multiple_of(place[2 * index + 1] * columns, columns)
        return pltpu.make_async_copy(
            piece, err.at[:, pl.ds(row, tokens), pl.ds(column, columns)], in_sem.at[index]
        )

    out_copy = pltpu.make_async_copy(err, all_ref.at[:, pl.ds(offset, total_rows), :], out_sem.at[0])

    @pl.when(layer == 0)
    def _():
        for index in range(n_pieces):
            in_copy(index).start()
        for index in range(n_pieces):
            in_copy(index).wait()
        out_copy.start()
        for send in sends:
            send[pl.ds(send.shape[0] - SUBLANES, SUBLANES), :] = jnp.zeros((SUBLANES, LANES), jnp.int32)

    for tgt in range(tgt_count):
        term = lax.dot_general(
            err[tgt], dec_ref[0, tgt], (((1,), (1,)), ((), ())), preferred_element_type=jnp.float32
        )
        term = term * keep[layer * tgt_count + tgt].astype(jnp.float32)
        acc[...] = term if tgt == 0 else acc[...] + term
    own_ref[0] = acc[...]

    lane = lanes_of((rows, LANES))
    peaks = jnp.zeros((rows, LANES), jnp.float32)
    blocks = []
    for index in range(n_tgt - 1):
        start = pl.multiple_of(order[index] * rows, rows)
        blocks.append(start)
        peaks = jnp.where(lane == index, row_peak(acc[pl.ds(start, rows), :]), peaks)
    scale, gain = scale_and_gain(peaks)
    scale_words = pair(scale)
    small = lanes_of((SUBLANES, LANES))
    for index, send in enumerate(sends):
        store_words(send, layer, acc[pl.ds(blocks[index], rows), :], gain[:, index : index + 1])
        end = pl.ds(send.shape[0] - SUBLANES, SUBLANES)
        tail = send[end, :]
        for group in range(half // SUBLANES):
            piece = scale_words[group * SUBLANES : (group + 1) * SUBLANES, index : index + 1]
            tail = jnp.where(small == group * layers + layer, piece, tail)
        send[end, :] = tail

    @pl.when(layer == layers - 1)
    def _():
        out_copy.wait()


def terms_call(pieces, place, keep, order, decoder, everything, offset, n_tgt, total_rows, tokens):
    src_count, tgt_count, width, columns = decoder.shape
    rows = total_rows // n_tgt
    payload = (payload_rows(src_count, rows, width), LANES)
    anywhere = pl.BlockSpec(memory_space=pl.ANY)
    in_specs = [anywhere] * len(pieces)
    in_specs.append(pl.BlockSpec((1, tgt_count, width, columns), lambda i, *_: (i, 0, 0, 0)))
    operands = [place, keep, order, *pieces, decoder]
    aliases = {}
    if everything is not None:
        in_specs.append(anywhere)
        aliases = {len(operands): n_tgt}
        operands.append(everything)
    out = pl.pallas_call(
        functools.partial(terms_kernel, n_tgt, len(pieces), offset),
        grid_spec=pltpu.PrefetchScalarGridSpec(
            num_scalar_prefetch=3,
            grid=(src_count,),
            in_specs=in_specs,
            out_specs=[pl.BlockSpec((1, total_rows, width), lambda i, *_: (i, 0, 0))]
            + [pl.BlockSpec(payload, lambda i, *_: (0, 0))] * (n_tgt - 1)
            + [anywhere],
            scratch_shapes=[
                pltpu.VMEM((tgt_count, total_rows, columns), jnp.bfloat16),
                pltpu.VMEM((total_rows, width), jnp.float32),
                pltpu.SemaphoreType.DMA((len(pieces),)),
                pltpu.SemaphoreType.DMA((1,)),
            ],
        ),
        out_shape=[jax.ShapeDtypeStruct((src_count, total_rows, width), jnp.float32)]
        + [jax.ShapeDtypeStruct(payload, jnp.int32)] * (n_tgt - 1)
        + [jax.ShapeDtypeStruct((tgt_count, tokens, columns), jnp.bfloat16)],
        input_output_aliases=aliases,
        compiler_params=pltpu.CompilerParams(vmem_limit_bytes=VMEM),
        cost_estimate=pl.CostEstimate(
            flops=2 * total_rows * width * columns * src_count * tgt_count,
            bytes_accessed=decoder.size * 2 + src_count * total_rows * width * 4 + 4 * total_rows * columns * tgt_count,
            transcendentals=0,
        ),
        name="terms",
    )(*operands)
    return out[0], out[1:-1], out[-1]


def relay_kernel(dest, own_ref, got_ref, send_ref, total):
    src_count, rows, width = own_ref.shape
    half = rows // 2
    steps = load_steps(got_ref)
    lane = lanes_of((rows, LANES))
    peaks = jnp.zeros((rows, LANES), jnp.float32)
    for layer in range(src_count):
        v = own_ref[layer] + load_values(got_ref, steps, layer, src_count, rows, width)
        total[layer] = v
        peaks = jnp.where(lane % src_count == layer, row_peak(v), peaks)
    scale, gain = scale_and_gain(peaks)
    for layer in range(src_count):
        store_words(send_ref, layer, total[layer], gain[:, layer : layer + 1])
    scale_words = pair(scale)
    small = lanes_of((SUBLANES, LANES)) // src_count
    tail = jnp.zeros((SUBLANES, LANES), jnp.int32)
    for group in range(half // SUBLANES):
        tail = jnp.where(small == group, scale_words[group * SUBLANES : (group + 1) * SUBLANES], tail)
    send_ref[pl.ds(send_ref.shape[0] - SUBLANES, SUBLANES), :] = tail


def relay_call(dest, own, got, n_tgt):
    src_count, total_rows, width = own.shape
    rows = total_rows // n_tgt
    whole = pl.BlockSpec(got.shape, lambda i, dest: (0, 0))
    return pl.pallas_call(
        relay_kernel,
        grid_spec=pltpu.PrefetchScalarGridSpec(
            num_scalar_prefetch=1,
            grid=(1,),
            in_specs=[pl.BlockSpec((src_count, rows, width), lambda i, dest: (0, dest[0], 0)), whole],
            out_specs=whole,
            scratch_shapes=[pltpu.VMEM((src_count, rows, width), jnp.float32)],
        ),
        out_shape=jax.ShapeDtypeStruct(got.shape, jnp.int32),
        compiler_params=pltpu.CompilerParams(vmem_limit_bytes=VMEM),
        cost_estimate=pl.CostEstimate(
            flops=20 * src_count * rows * width,
            bytes_accessed=8 * got.size + 4 * src_count * rows * width,
            transcendentals=0,
        ),
        name="relay",
    )(dest, own, got)


def finish_kernel(n_got, offset, stride, here, own_ref, *refs):
    gots = refs[:n_got]
    mask_ref = refs[n_got]
    out_ref, mask_tile, out_tile, in_sem, out_sem = refs[-5:]
    src_count, rows, width = own_ref.shape
    parts = mask_ref.shape[1] // stride
    tokens = rows // parts

    def mask_copy(part):
        return pltpu.make_async_copy(
            mask_ref.at[:, pl.ds(part * stride + offset, tokens), :],
            mask_tile.at[:, pl.ds(part * tokens, tokens), :],
            in_sem.at[part],
        )

    def out_copy(layer, part):
        return pltpu.make_async_copy(
            out_tile.at[layer, pl.ds(part * tokens, tokens), :],
            out_ref.at[layer, pl.ds(part * stride + offset, tokens), :],
            out_sem.at[layer * parts + part],
        )

    for part in range(parts):
        mask_copy(part).start()
    steps = [load_steps(got) for got in gots]
    for part in range(parts):
        mask_copy(part).wait()
    for layer in range(src_count):
        total = own_ref[layer]
        for got, step in zip(gots, steps):
            total += load_values(got, step, layer, src_count, rows, width)
        out_tile[layer] = (total * mask_tile[layer].astype(jnp.float32)).astype(jnp.bfloat16)
        for part in range(parts):
            out_copy(layer, part).start()
    for layer in range(src_count):
        for part in range(parts):
            out_copy(layer, part).wait()


def finish_call(here, own, gots, mask, out, offset, stride, n_tgt):
    src_count, total_rows, width = own.shape
    rows = total_rows // n_tgt
    parts = mask.shape[1] // stride
    anywhere = pl.BlockSpec(memory_space=pl.ANY)
    in_specs = [pl.BlockSpec((src_count, rows, width), lambda i, here: (0, here[0], 0))]
    in_specs += [pl.BlockSpec(got.shape, lambda i, here: (0, 0)) for got in gots]
    in_specs.append(anywhere)
    operands = [here, own, *gots, mask]
    aliases = {}
    if out is not None:
        in_specs.append(anywhere)
        aliases = {len(operands): 0}
        operands.append(out)
    return pl.pallas_call(
        functools.partial(finish_kernel, len(gots), offset, stride),
        grid_spec=pltpu.PrefetchScalarGridSpec(
            num_scalar_prefetch=1,
            grid=(1,),
            in_specs=in_specs,
            out_specs=anywhere,
            scratch_shapes=[
                pltpu.VMEM((src_count, rows, width), jnp.int32),
                pltpu.VMEM((src_count, rows, width), jnp.bfloat16),
                pltpu.SemaphoreType.DMA((parts,)),
                pltpu.SemaphoreType.DMA((src_count * parts,)),
            ],
        ),
        out_shape=jax.ShapeDtypeStruct(mask.shape, jnp.bfloat16),
        input_output_aliases=aliases,
        compiler_params=pltpu.CompilerParams(vmem_limit_bytes=VMEM),
        cost_estimate=pl.CostEstimate(
            flops=20 * src_count * rows * width,
            bytes_accessed=src_count * rows * width * 10 + 4 * sum(got.size for got in gots),
            transcendentals=0,
        ),
        name="finish",
    )(*operands)


def turn_kernel(spans, codes_ref, out_ref):
    tokens = codes_ref.shape[1]
    stride = sum(spans)
    blocks = tokens // stride
    offset = column = 0
    for span in spans:
        rows = jnp.concatenate(
            [codes_ref[0, pl.ds(block * stride + offset, span), :] for block in range(blocks)], axis=0
        )
        out_ref[0, :, pl.ds(column, blocks * span)] = rows.T
        offset += span
        column += blocks * span


def turn_call(codes, spans):
    src_count, tokens, width = codes.shape
    return pl.pallas_call(
        functools.partial(turn_kernel, spans),
        grid=(src_count,),
        in_specs=[pl.BlockSpec((1, tokens, width), lambda i: (i, 0, 0))],
        out_specs=pl.BlockSpec((1, width, tokens), lambda i: (i, 0, 0)),
        out_shape=jax.ShapeDtypeStruct((src_count, width, tokens), jnp.bfloat16),
        compiler_params=pltpu.CompilerParams(vmem_limit_bytes=VMEM),
        cost_estimate=pl.CostEstimate(flops=codes.size, bytes_accessed=codes.size * 4, transcendentals=0),
        name="turn",
    )(codes)


def grads_kernel(tgt, tgt_count, keep, codes_ref, err_ref, *refs):
    out_ref = refs[-1]
    kept = keep[pl.program_id(0) * tgt_count + tgt] == 1
    columns = out_ref.shape[3]
    step = min(columns, 512)

    @pl.when(kept)
    def _():
        for column in range(0, columns, step):
            out_ref[0, 0, :, column : column + step] = jnp.dot(
                codes_ref[0], err_ref[0, :, column : column + step], preferred_element_type=jnp.float32
            ).astype(jnp.bfloat16)

    @pl.when(jnp.logical_not(kept))
    def _():
        out_ref[...] = jnp.zeros_like(out_ref)


def grads_call(tgt, keep, codes_t, everything, out, shape):
    src_count, tgt_count, width, columns = shape
    tokens = codes_t.shape[2]
    in_specs = [
        pl.BlockSpec((1, width, tokens), lambda i, *_: (i, 0, 0)),
        pl.BlockSpec((1, tokens, columns), lambda i, *_: (tgt, 0, 0)),
    ]
    operands = [keep, codes_t, everything]
    aliases = {}
    if out is not None:
        in_specs.append(pl.BlockSpec(memory_space=pl.ANY))
        aliases = {len(operands): 0}
        operands.append(out)
    return pl.pallas_call(
        functools.partial(grads_kernel, tgt, tgt_count),
        grid_spec=pltpu.PrefetchScalarGridSpec(
            num_scalar_prefetch=1,
            grid=(src_count,),
            in_specs=in_specs,
            out_specs=pl.BlockSpec((1, 1, width, columns), lambda i, *_: (i, tgt, 0, 0)),
        ),
        out_shape=jax.ShapeDtypeStruct(shape, jnp.bfloat16),
        input_output_aliases=aliases,
        compiler_params=pltpu.CompilerParams(vmem_limit_bytes=VMEM),
        cost_estimate=pl.CostEstimate(
            flops=2 * src_count * width * columns * tokens,
            bytes_accessed=2 * src_count * width * (columns + tokens) + 2 * tokens * columns,
            transcendentals=0,
        ),
        name="grads",
    )(*operands)


def swap(x, axes, flips, sizes):
    pairs = []
    total = 1
    for size in sizes:
        total *= size
    for index in range(total):
        rest, other, weight = index, 0, 1
        for size, flip in reversed(list(zip(sizes, flips))):
            other += ((rest % size) ^ flip) * weight
            rest //= size
            weight *= size
        pairs.append((index, other))
    return lax.ppermute(x, axes, pairs)


def gather_pieces(part, chunk, n_src, n_feat):
    src, feat = lax.axis_index("src"), lax.axis_index("feat")
    if (n_src, n_feat) != (2, 4):
        columns = lax.all_gather(part, "src", axis=2, tiled=True)
        return [lax.all_gather(columns, "feat", axis=1, tiled=True)], [0, 0]
    over_x = lambda x: swap(x, "src", (1,), (n_src,))
    over_y = lambda x: swap(x, "feat", (2,), (n_feat,))
    over_core = lambda x: swap(x, "feat", (1,), (n_feat,))
    from_x, from_y = over_x(part), over_y(part)
    from_far = over_y(from_x) if chunk % 2 == 0 else over_x(from_y)
    pieces, place = [], []
    for piece, dx, dy in ((part, 0, 0), (from_x, 1, 0), (from_y, 0, 2), (from_far, 1, 2)):
        pieces += [piece, over_core(piece)]
        place += [feat ^ dy, src ^ dx, feat ^ dy ^ 1, src ^ dx]
    return pieces, place


def body(n_src, n_tgt, n_feat, errors, saved_codes, active_mask, decoder):
    src_count, tgt_count, width, _ = decoder.shape
    stride = errors.shape[1]
    src, tgt = lax.axis_index("src"), lax.axis_index("tgt")
    src_ids = src * src_count + jnp.arange(src_count, dtype=jnp.int32)
    tgt_ids = tgt * tgt_count + jnp.arange(tgt_count, dtype=jnp.int32)
    keep = (tgt_ids[None, :] >= src_ids[:, None]).astype(jnp.int32).reshape(-1)
    here = jnp.reshape(tgt, (1,)).astype(jnp.int32)
    lead = jnp.arange(n_tgt, dtype=jnp.int32)
    orders = [jnp.where(tgt == n_tgt - 1 - hop, lead, n_tgt - 1 - lead) for hop in range(n_tgt - 1)]

    spans = [stride * part // 8 for part in EIGHTHS]
    codes_t = turn_call(saved_codes, spans)
    code_grads = everything = None
    offset = 0
    for index, span in enumerate(spans):
        part = lax.slice_in_dim(errors, offset, offset + span, axis=1)
        pieces, place = gather_pieces(part, index, n_src, n_feat)
        place = jnp.stack([jnp.asarray(p, jnp.int32) for p in place])
        own, sends, everything = terms_call(
            pieces, place, keep, orders[0], decoder, everything, n_feat * offset, n_tgt, n_feat * span, n_feat * stride
        )
        last = []
        for hop in range(n_tgt - 1):
            pairs = [(n_tgt - 1 - hop, n_tgt - 2 - hop), (hop, hop + 1)]
            if hop:
                sends = [relay_call(orders[hop][i : i + 1], own, got, n_tgt) for i, got in enumerate(gots[:-1])]
            gots = [lax.ppermute(send, "tgt", pairs) for send in sends]
            last.append(gots[-1])
        code_grads = finish_call(here, own, last, active_mask, code_grads, offset, stride, n_tgt)
        offset += span
    decoder_grads = None
    for layer in range(tgt_count):
        decoder_grads = grads_call(layer, keep, codes_t, everything, decoder_grads, decoder.shape)
    return code_grads, decoder_grads


def solution(mesh):
    sizes = [mesh.shape[axis] for axis in ("src", "tgt", "feat")]
    in_specs = (
        P("tgt", "feat", "src"),
        P("src", None, "feat"),
        P("src", "tgt", "feat"),
        P("src", "tgt", "feat", None),
    )
    out_specs = (P("src", "tgt", "feat"), P("src", "tgt", "feat", None))
    return jax.shard_map(
        functools.partial(body, *sizes), mesh=mesh, in_specs=in_specs, out_specs=out_specs, check_vma=False
    )
```

```python
import functools

import jax
import jax.numpy as jnp
from jax import lax
from jax.experimental import pallas as pl
from jax.experimental.pallas import tpu as pltpu
from jax.sharding import PartitionSpec as P

LANES = 128
SUBLANES = 8
STEPS_PER_OCTAVE = 64
TOP = 32760.0
FLOOR = 1e-30
EIGHTHS = (2, 3, 3)
VMEM = 127 << 19
ANYWHERE = pl.BlockSpec(memory_space=pl.ANY)


def pair(x):
    half = x.shape[0] // 2
    return (x[half:] << 16) | (x[:half] & 0xFFFF)


def unpair(words):
    return (words << 16) >> 16, words >> 16


def scale_and_gain(peaks):
    scale = jnp.ceil(jnp.log2(jnp.maximum(peaks, FLOOR)) * STEPS_PER_OCTAVE)
    return scale.astype(jnp.int32), jnp.exp2(scale * (-1.0 / STEPS_PER_OCTAVE)) * TOP


def row_peak(v):
    return jnp.max(jnp.abs(v), axis=1, keepdims=True)


def store_words(out_ref, layer, v, gain, base=0):
    rows, width = v.shape
    half, tiles = rows // 2, width // LANES
    words = pair(jnp.floor(v * gain + 0.5).astype(jnp.int32))
    for tile in range(tiles):
        start = base + (layer * tiles + tile) * half
        out_ref[start : start + half, :] = words[:, tile * LANES : (tile + 1) * LANES]


def lanes_of(shape):
    return lax.broadcasted_iota(jnp.int32, shape, 1)


def load_steps(in_ref):
    end = in_ref.shape[0] - SUBLANES
    low, high = unpair(in_ref[end:, :])
    step = lambda scale: jnp.exp2(scale.astype(jnp.float32) * (1.0 / STEPS_PER_OCTAVE)) * (1.0 / TOP)
    return step(low), step(high)


def load_values(in_ref, steps, layer, layers, rows, width):
    half, tiles = rows // 2, width // LANES
    words = jnp.concatenate(
        [in_ref[(layer * tiles + tile) * half : (layer * tiles + tile + 1) * half, :] for tile in range(tiles)], axis=1
    )
    values = []
    for part, step in zip(unpair(words), steps):
        column = jnp.concatenate(
            [step[:, group * layers + layer][:, None] for group in range(half // SUBLANES)], axis=0
        )
        values.append(part.astype(jnp.float32) * column)
    return jnp.concatenate(values, axis=0)


def payload_rows(layers, rows, width):
    return layers * (width // LANES) * (rows // 2) + SUBLANES


def cost(flops, bytes_accessed):
    return pl.CostEstimate(flops=flops, bytes_accessed=bytes_accessed, transcendentals=0)


def cut_kernel(n_join, offset, errors_ref, *refs):
    sem = refs[-1]
    joined = refs[:n_join]
    outs = refs[-1 - (n_join > 0) - (offset is not None) : -1]
    copies = [(piece, outs[0].at[index]) for index, piece in enumerate(joined)]
    if offset is not None:
        copies.append((errors_ref.at[:, pl.ds(offset, outs[-1].shape[1]), :], outs[-1]))
    copies = [pltpu.make_async_copy(*copy, sem.at[index]) for index, copy in enumerate(copies)]
    for copy in copies:
        copy.start()
    for copy in copies:
        copy.wait()


def cut_call(errors, offset, span, join, after):
    shapes = []
    if join:
        shapes.append(jax.ShapeDtypeStruct((len(join), *join[0].shape), errors.dtype))
    if offset is not None:
        shapes.append(jax.ShapeDtypeStruct((errors.shape[0], span, errors.shape[2]), errors.dtype))
    return pl.pallas_call(
        functools.partial(cut_kernel, len(join), offset),
        in_specs=[ANYWHERE] * (1 + len(join) + len(after)),
        out_specs=[ANYWHERE] * len(shapes),
        out_shape=shapes,
        scratch_shapes=[pltpu.SemaphoreType.DMA((len(join) + 1,))],
        compiler_params=pltpu.CompilerParams(vmem_limit_bytes=VMEM),
        name="cut",
    )(errors, *join, *after)


def terms_kernel(n_tgt, plan, offset, *refs):
    n_pieces = 1 + max(entry[0] for entry in plan)
    pieces = refs[:n_pieces]
    dec_ref = refs[n_pieces]
    own_ref, both_ref, far_ref, all_ref, err, dec, acc, in_sem, dec_sem, own_sem, out_sem = refs[-11:]
    layers, tgt_count, width, columns = dec_ref.shape
    total_rows = err.shape[0]
    rows = total_rows // n_tgt
    half = rows // 2
    src, tgt, feat = (lax.axis_index(axis) for axis in ("src", "tgt", "feat"))

    def piece_copies(index):
        source, lead, skip, tokens, flip_src, flip_feat = plan[index]
        piece = pieces[source] if lead is None else pieces[source].at[lead]
        wide = piece.shape[2]
        row = 0 if flip_feat is None else pl.multiple_of((feat ^ flip_feat) * tokens, tokens)
        column = 0 if flip_src is None else pl.multiple_of((src ^ flip_src) * wide, wide)
        return [
            pltpu.make_async_copy(
                piece.at[t, pl.ds(skip, tokens), :],
                err.at[pl.ds(row, tokens), pl.ds(t * columns + column, wide)],
                in_sem.at[index * tgt_count + t],
            )
            for t in range(tgt_count)
        ]

    def dec_copy(layer, t):
        return pltpu.make_async_copy(
            dec_ref.at[layer, t], dec.at[layer, :, pl.ds(t * columns, columns)], dec_sem.at[layer * tgt_count + t]
        )

    def block(dest):
        return pl.ds(pl.multiple_of(dest * rows, rows), rows)

    def own_copies(layer):
        return [
            pltpu.make_async_copy(
                acc.at[layer, block(tgt ^ flip), :], own_ref.at[index, layer], own_sem.at[layer * 2 + index]
            )
            for index, flip in enumerate((0, 2))
        ]

    out_copy = pltpu.make_async_copy(err, all_ref.at[pl.ds(offset, total_rows), :], out_sem)

    for t in range(tgt_count):
        dec_copy(0, t).start()
    copies = [copy for index in range(len(plan)) for copy in piece_copies(index)]
    for copy in copies:
        copy.start()
    for layer in range(1, layers):
        for t in range(tgt_count):
            dec_copy(layer, t).start()
    for copy in copies:
        copy.wait()
    out_copy.start()

    lane = lanes_of((rows, LANES))
    small = lanes_of((SUBLANES, LANES))
    length = far_ref.shape[0]
    flips = (1, 3)
    tails = [jnp.zeros((SUBLANES, LANES), jnp.int32) for _ in flips]

    def multiply(layer):
        for t in range(tgt_count):
            dec_copy(layer, t).wait()
            kept = tgt * tgt_count + t >= src * layers + layer

            @pl.when(jnp.logical_not(kept))
            def _():
                dec[layer, :, t * columns : (t + 1) * columns] = jnp.zeros((width, columns), jnp.bfloat16)

        acc[layer] = lax.dot_general(
            err[...], dec[layer], (((1,), (1,)), ((), ())), preferred_element_type=jnp.float32
        )
        for copy in own_copies(layer):
            copy.start()

    def encode(layer):
        peaks = jnp.zeros((rows, LANES), jnp.float32)
        for index, flip in enumerate(flips):
            peaks = jnp.where(lane == index, row_peak(acc[layer, block(tgt ^ flip), :]), peaks)
        scale, gain = scale_and_gain(peaks)
        scale_words = pair(scale)
        for index, flip in enumerate(flips):
            v, factor = acc[layer, block(tgt ^ flip), :], gain[:, index : index + 1]
            store_words(both_ref, layer, v, factor, index * length)
            if index:
                store_words(far_ref, layer, v, factor)
            for group in range(half // SUBLANES):
                piece = scale_words[group * SUBLANES : (group + 1) * SUBLANES, index : index + 1]
                tails[index] = jnp.where(small == group * layers + layer, piece, tails[index])

    for layer in range(layers):
        multiply(layer)
        if layer:
            encode(layer - 1)
    encode(layers - 1)
    for index, tail in enumerate(tails):
        both_ref[(index + 1) * length - SUBLANES : (index + 1) * length, :] = tail
    far_ref[length - SUBLANES :, :] = tails[1]
    for layer in range(layers):
        for copy in own_copies(layer):
            copy.wait()
    out_copy.wait()


def terms_call(pieces, plan, decoder, everything, offset, n_tgt, total_rows, tokens, after):
    layers, tgt_count, width, columns = decoder.shape
    rows = total_rows // n_tgt
    payload = (payload_rows(layers, rows, width), LANES)
    whole = pl.BlockSpec(memory_space=pltpu.VMEM)
    operands = [*pieces, decoder]
    aliases = {}
    if everything is not None:
        aliases = {len(operands): 3}
        operands.append(everything)
    operands += after
    return pl.pallas_call(
        functools.partial(terms_kernel, n_tgt, plan, offset),
        in_specs=[ANYWHERE] * len(operands),
        out_specs=[ANYWHERE, whole, whole, ANYWHERE],
        scratch_shapes=[
            pltpu.VMEM((total_rows, tgt_count * columns), jnp.bfloat16),
            pltpu.VMEM((layers, width, tgt_count * columns), jnp.bfloat16),
            pltpu.VMEM((layers, total_rows, width), jnp.float32),
            pltpu.SemaphoreType.DMA((len(plan) * tgt_count,)),
            pltpu.SemaphoreType.DMA((layers * tgt_count,)),
            pltpu.SemaphoreType.DMA((layers * 2,)),
            pltpu.SemaphoreType.DMA,
        ],
        out_shape=[
            jax.ShapeDtypeStruct((2, layers, rows, width), jnp.float32),
            jax.ShapeDtypeStruct((2 * payload[0], LANES), jnp.int32),
            jax.ShapeDtypeStruct(payload, jnp.int32),
            jax.ShapeDtypeStruct((tokens, tgt_count * columns), jnp.bfloat16),
        ],
        input_output_aliases=aliases,
        compiler_params=pltpu.CompilerParams(vmem_limit_bytes=VMEM),
        cost_estimate=cost(2 * total_rows * decoder.size // EASE, decoder.size * 2 // EASE),
        name="terms",
    )(*operands)


def relay_kernel(own_ref, got_ref, *refs):
    send_ref, total = refs[-2:]
    layers, rows, width = total.shape
    half = rows // 2
    tgt = lax.axis_index("tgt")
    inner = jnp.logical_or(tgt == 1, tgt == 2).astype(jnp.float32)
    steps = [step * inner for step in load_steps(got_ref)]
    lane = lanes_of((rows, LANES))
    peaks = jnp.zeros((rows, LANES), jnp.float32)
    for layer in range(layers):
        v = own_ref[0, layer] + load_values(got_ref, steps, layer, layers, rows, width)
        total[layer] = v
        peaks = jnp.where(lane % layers == layer, row_peak(v), peaks)
    scale, gain = scale_and_gain(peaks)
    for layer in range(layers):
        store_words(send_ref, layer, total[layer], gain[:, layer : layer + 1])
    scale_words = pair(scale)
    small = lanes_of((SUBLANES, LANES)) // layers
    tail = jnp.zeros((SUBLANES, LANES), jnp.int32)
    for group in range(half // SUBLANES):
        tail = jnp.where(small == group, scale_words[group * SUBLANES : (group + 1) * SUBLANES], tail)
    send_ref[send_ref.shape[0] - SUBLANES :, :] = tail


def relay_call(own, got, after):
    _, layers, rows, width = own.shape
    shape = (got.shape[0] // 2, LANES)
    return pl.pallas_call(
        relay_kernel,
        grid=(1,),
        in_specs=[
            pl.BlockSpec((1, layers, rows, width), lambda i: (1, 0, 0, 0)),
            pl.BlockSpec(shape, lambda i: (1, 0)),
        ]
        + [ANYWHERE] * len(after),
        out_specs=pl.BlockSpec(shape, lambda i: (0, 0)),
        scratch_shapes=[pltpu.VMEM((layers, rows, width), jnp.float32)],
        out_shape=jax.ShapeDtypeStruct(shape, jnp.int32),
        compiler_params=pltpu.CompilerParams(vmem_limit_bytes=VMEM),
        cost_estimate=cost(20 * layers * rows * width // EASE, 8 * got.size // EASE),
        name="relay",
    )(own, got, *after)


def finish_kernel(n_got, offset, stride, own_ref, *refs):
    gots = refs[:n_got]
    mask_ref = refs[n_got]
    out_ref, mask_tile, out_tile, in_sem, out_sem = refs[-5:]
    layers, rows, width = out_tile.shape
    parts = mask_ref.shape[1] // stride
    tokens = rows // parts

    def mask_copy(part):
        return pltpu.make_async_copy(
            mask_ref.at[:, pl.ds(part * stride + offset, tokens), :],
            mask_tile.at[:, pl.ds(part * tokens, tokens), :],
            in_sem.at[part],
        )

    def out_copy(layer, part):
        return pltpu.make_async_copy(
            out_tile.at[layer, pl.ds(part * tokens, tokens), :],
            out_ref.at[layer, pl.ds(part * stride + offset, tokens), :],
            out_sem.at[layer * parts + part],
        )

    for part in range(parts):
        mask_copy(part).start()
    steps = [load_steps(got) for got in gots]
    for part in range(parts):
        mask_copy(part).wait()
    for layer in range(layers):
        total = own_ref[0, layer]
        for got, step in zip(gots, steps):
            total += load_values(got, step, layer, layers, rows, width)
        out_tile[layer] = (total * mask_tile[layer].astype(jnp.float32)).astype(jnp.bfloat16)
        for part in range(parts):
            out_copy(layer, part).start()
    for layer in range(layers):
        for part in range(parts):
            out_copy(layer, part).wait()


def finish_call(own, gots, mask, out, offset, stride, after):
    _, layers, rows, width = own.shape
    parts = mask.shape[1] // stride
    in_specs = [pl.BlockSpec((1, layers, rows, width), lambda i: (0, 0, 0, 0))]
    in_specs += [pl.BlockSpec(gots[-1].shape, lambda i: (0, 0)) for got in gots]
    in_specs.append(ANYWHERE)
    operands = [own, *gots, mask]
    aliases = {}
    if out is not None:
        in_specs.append(ANYWHERE)
        aliases = {len(operands): 0}
        operands.append(out)
    in_specs += [ANYWHERE] * len(after)
    operands += after
    return pl.pallas_call(
        functools.partial(finish_kernel, len(gots), offset, stride),
        grid=(1,),
        in_specs=in_specs,
        out_specs=ANYWHERE,
        scratch_shapes=[
            pltpu.VMEM((layers, rows, width), jnp.int32),
            pltpu.VMEM((layers, rows, width), jnp.bfloat16),
            pltpu.SemaphoreType.DMA((parts,)),
            pltpu.SemaphoreType.DMA((layers * parts,)),
        ],
        out_shape=jax.ShapeDtypeStruct(mask.shape, jnp.bfloat16),
        input_output_aliases=aliases,
        compiler_params=pltpu.CompilerParams(vmem_limit_bytes=VMEM),
        cost_estimate=cost(20 * layers * rows * width // EASE, layers * rows * width * 16 // EASE),
        name="finish",
    )(*operands)


def turn_kernel(spans, codes_ref, out_ref):
    tokens = codes_ref.shape[1]
    stride = sum(spans)
    blocks = tokens // stride
    offset = column = 0
    for span in spans:
        rows = jnp.concatenate(
            [codes_ref[0, pl.ds(block * stride + offset, span), :] for block in range(blocks)], axis=0
        )
        out_ref[0, :, pl.ds(column, blocks * span)] = rows.T
        offset += span
        column += blocks * span


def turn_call(codes, spans):
    layers, tokens, width = codes.shape
    return pl.pallas_call(
        functools.partial(turn_kernel, spans),
        grid=(layers,),
        in_specs=[pl.BlockSpec((1, tokens, width), lambda i: (i, 0, 0))],
        out_specs=pl.BlockSpec((1, width, tokens), lambda i: (i, 0, 0)),
        out_shape=jax.ShapeDtypeStruct((layers, width, tokens), jnp.bfloat16),
        compiler_params=pltpu.CompilerParams(vmem_limit_bytes=VMEM),
        cost_estimate=cost(codes.size // EASE, codes.size * 4 // EASE),
        name="turn",
    )(codes)


def grads_kernel(t, codes_ref, err_ref, *refs):
    out_ref = refs[-1]
    tgt_count, columns = 1, out_ref.shape[3]
    layer = lax.axis_index("src") * pl.num_programs(0) + pl.program_id(0)
    kept = lax.axis_index("tgt") * t[1] + t[0] >= layer
    step = min(columns, 512)

    @pl.when(kept)
    def _():
        for column in range(0, columns, step):
            out_ref[0, 0, :, column : column + step] = jnp.dot(
                codes_ref[0], err_ref[:, column : column + step], preferred_element_type=jnp.float32
            ).astype(jnp.bfloat16)

    @pl.when(jnp.logical_not(kept))
    def _():
        out_ref[...] = jnp.zeros_like(out_ref)


def grads_call(t, codes_t, everything, out, shape, after):
    layers, tgt_count, width, columns = shape
    tokens = codes_t.shape[2]
    in_specs = [
        pl.BlockSpec((1, width, tokens), lambda i: (i, 0, 0)),
        pl.BlockSpec((tokens, columns), lambda i: (0, t)),
    ]
    operands = [codes_t, everything]
    aliases = {}
    if out is not None:
        aliases = {len(operands): 0}
        operands.append(out)
    operands += after
    in_specs += [ANYWHERE] * (len(operands) - 2)
    return pl.pallas_call(
        functools.partial(grads_kernel, (t, tgt_count)),
        grid=(layers,),
        in_specs=in_specs,
        out_specs=pl.BlockSpec((1, 1, width, columns), lambda i: (i, t, 0, 0)),
        out_shape=jax.ShapeDtypeStruct(shape, jnp.bfloat16),
        input_output_aliases=aliases,
        compiler_params=pltpu.CompilerParams(vmem_limit_bytes=VMEM),
        cost_estimate=cost(
            2 * layers * width * columns * tokens // EASE, 2 * layers * width * (columns + tokens) // EASE
        ),
        name="grads",
    )(*operands)


EASE = 16


def gather_pieces(errors, spans, offsets, n_src, n_feat, codes_t):
    if (n_src, n_feat) != (2, 4):
        for offset, span in zip(offsets, spans):
            part = lax.slice_in_dim(errors, offset, offset + span, axis=1)
            columns = lax.all_gather(part, "src", axis=2, tiled=True)
            piece = lax.all_gather(columns, "feat", axis=1, tiled=True)
            yield [piece], [(0, None, 0, n_feat * span, None, None)]
        return
    axes = ("src", "feat")
    to = lambda x, flip: lax.ppermute(x, axes, [(i, i ^ flip) for i in range(n_src * n_feat)])
    core_own = over_core(errors, n_feat)
    (part,) = cut_call(errors, 0, spans[0], [], [])
    after = [core_own, codes_t]
    for index, (offset, span) in enumerate(zip(offsets, spans)):
        arrived = [to(part, n_feat), to(part, 2), to(part, n_feat + 2)]
        more = index + 1 < len(spans)
        joined, *rest = cut_call(
            errors, offsets[index + 1] if more else None, spans[index + 1] if more else None, arrived, after
        )
        part = rest[0] if more else None
        plan = [(core, None, offset, span, 0, core) for core in (0, 1)]
        for lead, (dx, dy) in enumerate(((1, 0), (0, 2), (1, 2))):
            plan += [(2 + core, lead, 0, span, dx, dy ^ core) for core in (0, 1)]
        after = yield [errors, core_own, joined, over_core(joined, n_feat)], plan


def over_core(x, n_feat):
    return lax.ppermute(x, "feat", [(i, i ^ 1) for i in range(n_feat)])


def body(n_src, n_tgt, n_feat, errors, saved_codes, active_mask, decoder):
    tgt_count = decoder.shape[1]
    stride = errors.shape[1]
    spans = [stride * part // 8 for part in EIGHTHS]
    offsets = [sum(spans[:index]) for index in range(len(spans))]
    near = [(i, i ^ 1) for i in range(n_tgt)]
    middle = [(1, 2), (2, 1)]
    across = [(i, i ^ 2) for i in range(n_tgt)]
    codes_t = turn_call(saved_codes, spans)
    gather = gather_pieces(errors, spans, offsets, n_src, n_feat, codes_t)
    pieces, plan = next(gather)

    last = len(spans) - 1
    owns, gots = [], []
    everything, relayed = None, []
    decoder_grads = None

    def relay(index, after):
        ready = after + gots[index][1:] + [got for group in gots[:index] for got in group]
        sent = relay_call(owns[index], gots[index][0], ready)
        gots[index].append(lax.ppermute(sent, "tgt", across))
        return [sent]

    for index, span in enumerate(spans):
        own, both, far, everything = terms_call(
            pieces,
            plan,
            decoder,
            everything,
            n_feat * offsets[index],
            n_tgt,
            n_feat * span,
            n_feat * stride,
            relayed,
        )
        owns.append(own)
        gots.append([lax.ppermute(both, "tgt", near), lax.ppermute(far, "tgt", middle)])
        if index < last:
            pieces, plan = gather.send([own])
        relayed = relay(index - 1, [own]) if index else gots[0][:2]
    for t in range(tgt_count):
        decoder_grads = grads_call(t, codes_t, everything, decoder_grads, decoder.shape, relayed)
        if t == 0:
            relayed = relay(last, [decoder_grads])
    code_grads = None
    for index in range(len(spans)):
        code_grads = finish_call(
            owns[index], gots[index], active_mask, code_grads, offsets[index], stride, [] if index else [decoder_grads]
        )
    return code_grads, decoder_grads


def plain_body(errors, saved_codes, active_mask, decoder):
    src_count, tgt_count, feat_count, _ = decoder.shape
    src_ids = lax.axis_index("src") * src_count + jnp.arange(src_count, dtype=jnp.int32)
    tgt_ids = lax.axis_index("tgt") * tgt_count + jnp.arange(tgt_count, dtype=jnp.int32)
    kept = (tgt_ids[None, :] >= src_ids[:, None])[:, :, None, None]
    columns = lax.all_gather(errors, "src", axis=2, tiled=True)
    portion = lax.all_gather(columns, "feat", axis=1, tiled=True)
    grads = jnp.einsum("itf,jtd->ijfd", saved_codes, portion, preferred_element_type=jnp.float32)
    decoder = jnp.where(kept, decoder, jnp.zeros_like(decoder))
    term = jnp.einsum("jtd,ijfd->itf", portion, decoder, preferred_element_type=jnp.float32)
    summed = lax.psum_scatter(term, "tgt", scatter_dimension=1, tiled=True)
    code_grads = (summed * active_mask.astype(jnp.float32)).astype(jnp.bfloat16)
    return code_grads, jnp.where(kept, grads, 0.0).astype(jnp.bfloat16)


def solution(mesh):
    sizes = [mesh.shape[axis] for axis in ("src", "tgt", "feat")]
    fits = sizes[1] == 4 and sizes[2] % sizes[1] == 0
    in_specs = (
        P("tgt", "feat", "src"),
        P("src", None, "feat"),
        P("src", "tgt", "feat"),
        P("src", "tgt", "feat", None),
    )
    out_specs = (P("src", "tgt", "feat"), P("src", "tgt", "feat", None))
    return jax.shard_map(
        functools.partial(body, *sizes) if fits else plain_body,
        mesh=mesh,
        in_specs=in_specs,
        out_specs=out_specs,
        check_vma=False,
    )
```

```python
import functools

import jax
import jax.numpy as jnp
from jax import lax
from jax.experimental import pallas as pl
from jax.experimental.pallas import tpu as pltpu
from jax.sharding import PartitionSpec as P

LANES = 128
SUBLANES = 8
STEPS_PER_OCTAVE = 64
TOP = 32760.0
FLOOR = 1e-30
EIGHTHS = (2, 3, 3)
VMEM = 127 << 19
ANYWHERE = pl.BlockSpec(memory_space=pl.ANY)


def pair(x):
    half = x.shape[0] // 2
    return (x[half:] << 16) | (x[:half] & 0xFFFF)


def unpair(words):
    return (words << 16) >> 16, words >> 16


def scale_and_gain(peaks):
    scale = jnp.ceil(jnp.log2(jnp.maximum(peaks, FLOOR)) * STEPS_PER_OCTAVE)
    return scale.astype(jnp.int32), jnp.exp2(scale * (-1.0 / STEPS_PER_OCTAVE)) * TOP


def row_peak(v):
    return jnp.max(jnp.abs(v), axis=1, keepdims=True)


def store_words(out_ref, layer, v, gain, base=0):
    rows, width = v.shape
    half, tiles = rows // 2, width // LANES
    words = pair(jnp.floor(v * gain + 0.5).astype(jnp.int32))
    for tile in range(tiles):
        start = base + (layer * tiles + tile) * half
        out_ref[start : start + half, :] = words[:, tile * LANES : (tile + 1) * LANES]


def lanes_of(shape):
    return lax.broadcasted_iota(jnp.int32, shape, 1)


def load_steps(in_ref):
    end = in_ref.shape[0] - SUBLANES
    low, high = unpair(in_ref[end:, :])
    step = lambda scale: jnp.exp2(scale.astype(jnp.float32) * (1.0 / STEPS_PER_OCTAVE)) * (1.0 / TOP)
    return step(low), step(high)


def load_values(in_ref, steps, layer, layers, rows, width):
    half, tiles = rows // 2, width // LANES
    words = jnp.concatenate(
        [in_ref[(layer * tiles + tile) * half : (layer * tiles + tile + 1) * half, :] for tile in range(tiles)], axis=1
    )
    values = []
    for part, step in zip(unpair(words), steps):
        column = jnp.concatenate(
            [step[:, group * layers + layer][:, None] for group in range(half // SUBLANES)], axis=0
        )
        values.append(part.astype(jnp.float32) * column)
    return jnp.concatenate(values, axis=0)


def payload_rows(layers, rows, width):
    return layers * (width // LANES) * (rows // 2) + SUBLANES


def cost(flops, bytes_accessed):
    return pl.CostEstimate(flops=flops, bytes_accessed=bytes_accessed, transcendentals=0)


def cut_kernel(n_join, offset, errors_ref, *refs):
    sem = refs[-1]
    joined = refs[:n_join]
    outs = refs[-1 - (n_join > 0) - (offset is not None) : -1]
    copies = [(piece, outs[0].at[index]) for index, piece in enumerate(joined)]
    if offset is not None:
        copies.append((errors_ref.at[:, pl.ds(offset, outs[-1].shape[1]), :], outs[-1]))
    copies = [pltpu.make_async_copy(*copy, sem.at[index]) for index, copy in enumerate(copies)]
    for copy in copies:
        copy.start()
    for copy in copies:
        copy.wait()


def cut_call(errors, offset, span, join, after):
    shapes = []
    if join:
        shapes.append(jax.ShapeDtypeStruct((len(join), *join[0].shape), errors.dtype))
    if offset is not None:
        shapes.append(jax.ShapeDtypeStruct((errors.shape[0], span, errors.shape[2]), errors.dtype))
    return pl.pallas_call(
        functools.partial(cut_kernel, len(join), offset),
        in_specs=[ANYWHERE] * (1 + len(join) + len(after)),
        out_specs=[pl.BlockSpec(memory_space=pltpu.VMEM)] * len(shapes),
        out_shape=shapes,
        scratch_shapes=[pltpu.SemaphoreType.DMA((len(join) + 1,))],
        compiler_params=pltpu.CompilerParams(vmem_limit_bytes=VMEM),
        name="cut",
    )(errors, *join, *after)


def terms_kernel(n_tgt, plan, offset, *refs):
    n_pieces = 1 + max(entry[0] for entry in plan)
    pieces = refs[:n_pieces]
    dec_ref = refs[n_pieces]
    own_ref, both_ref, far_ref, all_ref, err, dec, acc, in_sem, dec_sem, own_sem, out_sem = refs[-11:]
    layers, tgt_count, width, columns = dec_ref.shape
    total_rows = err.shape[0]
    rows = total_rows // n_tgt
    half = rows // 2
    src, tgt, feat = (lax.axis_index(axis) for axis in ("src", "tgt", "feat"))

    def piece_copies(index):
        source, lead, skip, tokens, flip_src, flip_feat = plan[index]
        piece = pieces[source] if lead is None else pieces[source].at[lead]
        wide = piece.shape[2]
        row = 0 if flip_feat is None else pl.multiple_of((feat ^ flip_feat) * tokens, tokens)
        column = 0 if flip_src is None else pl.multiple_of((src ^ flip_src) * wide, wide)
        return [
            pltpu.make_async_copy(
                piece.at[t, pl.ds(skip, tokens), :],
                err.at[pl.ds(row, tokens), pl.ds(t * columns + column, wide)],
                in_sem.at[index * tgt_count + t],
            )
            for t in range(tgt_count)
        ]

    def dec_copy(layer, t):
        return pltpu.make_async_copy(
            dec_ref.at[layer, t], dec.at[layer, :, pl.ds(t * columns, columns)], dec_sem.at[layer * tgt_count + t]
        )

    def block(dest):
        return pl.ds(pl.multiple_of(dest * rows, rows), rows)

    def own_copies(layer):
        return [
            pltpu.make_async_copy(
                acc.at[layer, block(tgt ^ flip), :], own_ref.at[index, layer], own_sem.at[layer * 2 + index]
            )
            for index, flip in enumerate((0, 2))
        ]

    out_copy = pltpu.make_async_copy(err, all_ref.at[pl.ds(offset, total_rows), :], out_sem)

    for t in range(tgt_count):
        dec_copy(0, t).start()
    copies = [copy for index in range(len(plan)) for copy in piece_copies(index)]
    for copy in copies:
        copy.start()
    for layer in range(1, layers):
        for t in range(tgt_count):
            dec_copy(layer, t).start()
    for copy in copies:
        copy.wait()
    out_copy.start()

    lane = lanes_of((rows, LANES))
    small = lanes_of((SUBLANES, LANES))
    length = far_ref.shape[0]
    flips = (1, 3)
    tails = [jnp.zeros((SUBLANES, LANES), jnp.int32) for _ in flips]

    def multiply(layer):
        for t in range(tgt_count):
            dec_copy(layer, t).wait()
            kept = tgt * tgt_count + t >= src * layers + layer

            @pl.when(jnp.logical_not(kept))
            def _():
                dec[layer, :, t * columns : (t + 1) * columns] = jnp.zeros((width, columns), jnp.bfloat16)

        acc[layer] = lax.dot_general(
            err[...], dec[layer], (((1,), (1,)), ((), ())), preferred_element_type=jnp.float32
        )
        for copy in own_copies(layer):
            copy.start()

    def encode(layer):
        peaks = jnp.zeros((rows, LANES), jnp.float32)
        for index, flip in enumerate(flips):
            peaks = jnp.where(lane == index, row_peak(acc[layer, block(tgt ^ flip), :]), peaks)
        scale, gain = scale_and_gain(peaks)
        scale_words = pair(scale)
        for index, flip in enumerate(flips):
            v, factor = acc[layer, block(tgt ^ flip), :], gain[:, index : index + 1]
            store_words(both_ref, layer, v, factor, index * length)
            if index:
                store_words(far_ref, layer, v, factor)
            for group in range(half // SUBLANES):
                piece = scale_words[group * SUBLANES : (group + 1) * SUBLANES, index : index + 1]
                tails[index] = jnp.where(small == group * layers + layer, piece, tails[index])

    for layer in range(layers):
        multiply(layer)
        if layer:
            encode(layer - 1)
    encode(layers - 1)
    for index, tail in enumerate(tails):
        both_ref[(index + 1) * length - SUBLANES : (index + 1) * length, :] = tail
    far_ref[length - SUBLANES :, :] = tails[1]
    for layer in range(layers):
        for copy in own_copies(layer):
            copy.wait()
    out_copy.wait()


def terms_call(pieces, plan, decoder, everything, offset, n_tgt, total_rows, tokens, after):
    layers, tgt_count, width, columns = decoder.shape
    rows = total_rows // n_tgt
    payload = (payload_rows(layers, rows, width), LANES)
    whole = pl.BlockSpec(memory_space=pltpu.VMEM)
    operands = [*pieces, decoder]
    aliases = {}
    if everything is not None:
        aliases = {len(operands): 3}
        operands.append(everything)
    operands += after
    return pl.pallas_call(
        functools.partial(terms_kernel, n_tgt, plan, offset),
        in_specs=[ANYWHERE] * len(operands),
        out_specs=[ANYWHERE, whole, whole, ANYWHERE],
        scratch_shapes=[
            pltpu.VMEM((total_rows, tgt_count * columns), jnp.bfloat16),
            pltpu.VMEM((layers, width, tgt_count * columns), jnp.bfloat16),
            pltpu.VMEM((layers, total_rows, width), jnp.float32),
            pltpu.SemaphoreType.DMA((len(plan) * tgt_count,)),
            pltpu.SemaphoreType.DMA((layers * tgt_count,)),
            pltpu.SemaphoreType.DMA((layers * 2,)),
            pltpu.SemaphoreType.DMA,
        ],
        out_shape=[
            jax.ShapeDtypeStruct((2, layers, rows, width), jnp.float32),
            jax.ShapeDtypeStruct((2 * payload[0], LANES), jnp.int32),
            jax.ShapeDtypeStruct(payload, jnp.int32),
            jax.ShapeDtypeStruct((tokens, tgt_count * columns), jnp.bfloat16),
        ],
        input_output_aliases=aliases,
        compiler_params=pltpu.CompilerParams(vmem_limit_bytes=VMEM),
        cost_estimate=cost(2 * total_rows * decoder.size // EASE, decoder.size * 2 // EASE),
        name="terms",
    )(*operands)


def relay_kernel(own_ref, got_ref, *refs):
    send_ref, total = refs[-2:]
    layers, rows, width = total.shape
    half = rows // 2
    tgt = lax.axis_index("tgt")
    inner = jnp.logical_or(tgt == 1, tgt == 2).astype(jnp.float32)
    steps = [step * inner for step in load_steps(got_ref)]
    lane = lanes_of((rows, LANES))
    peaks = jnp.zeros((rows, LANES), jnp.float32)
    for layer in range(layers):
        v = own_ref[0, layer] + load_values(got_ref, steps, layer, layers, rows, width)
        total[layer] = v
        peaks = jnp.where(lane % layers == layer, row_peak(v), peaks)
    scale, gain = scale_and_gain(peaks)
    for layer in range(layers):
        store_words(send_ref, layer, total[layer], gain[:, layer : layer + 1])
    scale_words = pair(scale)
    small = lanes_of((SUBLANES, LANES)) // layers
    tail = jnp.zeros((SUBLANES, LANES), jnp.int32)
    for group in range(half // SUBLANES):
        tail = jnp.where(small == group, scale_words[group * SUBLANES : (group + 1) * SUBLANES], tail)
    send_ref[send_ref.shape[0] - SUBLANES :, :] = tail


def relay_call(own, got, after):
    _, layers, rows, width = own.shape
    shape = (got.shape[0] // 2, LANES)
    return pl.pallas_call(
        relay_kernel,
        grid=(1,),
        in_specs=[
            pl.BlockSpec((1, layers, rows, width), lambda i: (1, 0, 0, 0)),
            pl.BlockSpec(shape, lambda i: (1, 0)),
        ]
        + [ANYWHERE] * len(after),
        out_specs=pl.BlockSpec(shape, lambda i: (0, 0)),
        scratch_shapes=[pltpu.VMEM((layers, rows, width), jnp.float32)],
        out_shape=jax.ShapeDtypeStruct(shape, jnp.int32),
        compiler_params=pltpu.CompilerParams(vmem_limit_bytes=VMEM),
        cost_estimate=cost(20 * layers * rows * width // EASE, 8 * got.size // EASE),
        name="relay",
    )(own, got, *after)


def finish_kernel(n_got, offset, stride, own_ref, *refs):
    gots = refs[:n_got]
    mask_ref = refs[n_got]
    out_ref, mask_tile, out_tile, in_sem, out_sem = refs[-5:]
    layers, rows, width = out_tile.shape
    parts = mask_ref.shape[1] // stride
    tokens = rows // parts

    def mask_copy(part):
        return pltpu.make_async_copy(
            mask_ref.at[:, pl.ds(part * stride + offset, tokens), :],
            mask_tile.at[:, pl.ds(part * tokens, tokens), :],
            in_sem.at[part],
        )

    def out_copy(layer, part):
        return pltpu.make_async_copy(
            out_tile.at[layer, pl.ds(part * tokens, tokens), :],
            out_ref.at[layer, pl.ds(part * stride + offset, tokens), :],
            out_sem.at[layer * parts + part],
        )

    for part in range(parts):
        mask_copy(part).start()
    steps = [load_steps(got) for got in gots]
    for part in range(parts):
        mask_copy(part).wait()
    for layer in range(layers):
        total = own_ref[0, layer]
        for got, step in zip(gots, steps):
            total += load_values(got, step, layer, layers, rows, width)
        out_tile[layer] = (total * mask_tile[layer].astype(jnp.float32)).astype(jnp.bfloat16)
        for part in range(parts):
            out_copy(layer, part).start()
    for layer in range(layers):
        for part in range(parts):
            out_copy(layer, part).wait()


def finish_call(own, gots, mask, out, offset, stride, after):
    _, layers, rows, width = own.shape
    parts = mask.shape[1] // stride
    in_specs = [pl.BlockSpec((1, layers, rows, width), lambda i: (0, 0, 0, 0))]
    in_specs += [pl.BlockSpec(gots[-1].shape, lambda i: (0, 0)) for got in gots]
    in_specs.append(ANYWHERE)
    operands = [own, *gots, mask]
    aliases = {}
    if out is not None:
        in_specs.append(ANYWHERE)
        aliases = {len(operands): 0}
        operands.append(out)
    in_specs += [ANYWHERE] * len(after)
    operands += after
    return pl.pallas_call(
        functools.partial(finish_kernel, len(gots), offset, stride),
        grid=(1,),
        in_specs=in_specs,
        out_specs=ANYWHERE,
        scratch_shapes=[
            pltpu.VMEM((layers, rows, width), jnp.int32),
            pltpu.VMEM((layers, rows, width), jnp.bfloat16),
            pltpu.SemaphoreType.DMA((parts,)),
            pltpu.SemaphoreType.DMA((layers * parts,)),
        ],
        out_shape=jax.ShapeDtypeStruct(mask.shape, jnp.bfloat16),
        input_output_aliases=aliases,
        compiler_params=pltpu.CompilerParams(vmem_limit_bytes=VMEM),
        cost_estimate=cost(20 * layers * rows * width // EASE, layers * rows * width * 16 // EASE),
        name="finish",
    )(*operands)


def turn_kernel(spans, codes_ref, out_ref):
    tokens = codes_ref.shape[1]
    stride = sum(spans)
    blocks = tokens // stride
    offset = column = 0
    for span in spans:
        rows = jnp.concatenate(
            [codes_ref[0, pl.ds(block * stride + offset, span), :] for block in range(blocks)], axis=0
        )
        out_ref[0, :, pl.ds(column, blocks * span)] = rows.T
        offset += span
        column += blocks * span


def turn_call(codes, spans):
    layers, tokens, width = codes.shape
    return pl.pallas_call(
        functools.partial(turn_kernel, spans),
        grid=(layers,),
        in_specs=[pl.BlockSpec((1, tokens, width), lambda i: (i, 0, 0))],
        out_specs=pl.BlockSpec((1, width, tokens), lambda i: (i, 0, 0)),
        out_shape=jax.ShapeDtypeStruct((layers, width, tokens), jnp.bfloat16),
        compiler_params=pltpu.CompilerParams(vmem_limit_bytes=VMEM),
        cost_estimate=cost(codes.size // EASE, codes.size * 4 // EASE),
        name="turn",
    )(codes)


def grads_kernel(t, codes_ref, err_ref, *refs):
    out_ref = refs[-1]
    tgt_count, columns = 1, out_ref.shape[3]
    layer = lax.axis_index("src") * pl.num_programs(0) + pl.program_id(0)
    kept = lax.axis_index("tgt") * t[1] + t[0] >= layer
    step = min(columns, 512)

    @pl.when(kept)
    def _():
        for column in range(0, columns, step):
            out_ref[0, 0, :, column : column + step] = jnp.dot(
                codes_ref[0], err_ref[:, column : column + step], preferred_element_type=jnp.float32
            ).astype(jnp.bfloat16)

    @pl.when(jnp.logical_not(kept))
    def _():
        out_ref[...] = jnp.zeros_like(out_ref)


def grads_call(t, codes_t, everything, out, shape, after):
    layers, tgt_count, width, columns = shape
    tokens = codes_t.shape[2]
    in_specs = [
        pl.BlockSpec((1, width, tokens), lambda i: (i, 0, 0)),
        pl.BlockSpec((tokens, columns), lambda i: (0, t)),
    ]
    operands = [codes_t, everything]
    aliases = {}
    if out is not None:
        aliases = {len(operands): 0}
        operands.append(out)
    operands += after
    in_specs += [ANYWHERE] * (len(operands) - 2)
    return pl.pallas_call(
        functools.partial(grads_kernel, (t, tgt_count)),
        grid=(layers,),
        in_specs=in_specs,
        out_specs=pl.BlockSpec((1, 1, width, columns), lambda i: (i, t, 0, 0)),
        out_shape=jax.ShapeDtypeStruct(shape, jnp.bfloat16),
        input_output_aliases=aliases,
        compiler_params=pltpu.CompilerParams(vmem_limit_bytes=VMEM),
        cost_estimate=cost(
            2 * layers * width * columns * tokens // EASE, 2 * layers * width * (columns + tokens) // EASE
        ),
        name="grads",
    )(*operands)


EASE = 16


def gather_pieces(errors, spans, offsets, n_src, n_feat, codes_t):
    if (n_src, n_feat) != (2, 4):
        for offset, span in zip(offsets, spans):
            part = lax.slice_in_dim(errors, offset, offset + span, axis=1)
            columns = lax.all_gather(part, "src", axis=2, tiled=True)
            piece = lax.all_gather(columns, "feat", axis=1, tiled=True)
            yield [piece], [(0, None, 0, n_feat * span, None, None)]
        return
    axes = ("src", "feat")
    to = lambda x, flip: lax.ppermute(x, axes, [(i, i ^ flip) for i in range(n_src * n_feat)])
    core_own = over_core(errors, n_feat)
    (part,) = cut_call(errors, 0, spans[0], [], [])
    after = [core_own, codes_t]
    for index, (offset, span) in enumerate(zip(offsets, spans)):
        arrived = [to(part, n_feat), to(part, 2), to(part, n_feat + 2)]
        more = index + 1 < len(spans)
        joined, *rest = cut_call(
            errors, offsets[index + 1] if more else None, spans[index + 1] if more else None, arrived, after
        )
        part = rest[0] if more else None
        plan = [(core, None, offset, span, 0, core) for core in (0, 1)]
        for lead, (dx, dy) in enumerate(((1, 0), (0, 2), (1, 2))):
            plan += [(2 + core, lead, 0, span, dx, dy ^ core) for core in (0, 1)]
        after = yield [errors, core_own, joined, over_core(joined, n_feat)], plan


def over_core(x, n_feat):
    return lax.ppermute(x, "feat", [(i, i ^ 1) for i in range(n_feat)])


def body(n_src, n_tgt, n_feat, errors, saved_codes, active_mask, decoder):
    tgt_count = decoder.shape[1]
    stride = errors.shape[1]
    spans = [stride * part // 8 for part in EIGHTHS]
    offsets = [sum(spans[:index]) for index in range(len(spans))]
    near = [(i, i ^ 1) for i in range(n_tgt)]
    middle = [(1, 2), (2, 1)]
    across = [(i, i ^ 2) for i in range(n_tgt)]
    codes_t = turn_call(saved_codes, spans)
    gather = gather_pieces(errors, spans, offsets, n_src, n_feat, codes_t)
    pieces, plan = next(gather)

    last = len(spans) - 1
    owns, gots = [], []
    everything, relayed = None, []
    decoder_grads = None

    def relay(index, after):
        ready = after + gots[index][1:] + [got for group in gots[:index] for got in group]
        sent = relay_call(owns[index], gots[index][0], ready)
        gots[index].append(lax.ppermute(sent, "tgt", across))
        return [sent]

    for index, span in enumerate(spans):
        own, both, far, everything = terms_call(
            pieces,
            plan,
            decoder,
            everything,
            n_feat * offsets[index],
            n_tgt,
            n_feat * span,
            n_feat * stride,
            relayed,
        )
        owns.append(own)
        gots.append([lax.ppermute(both, "tgt", near), lax.ppermute(far, "tgt", middle)])
        if index < last:
            pieces, plan = gather.send([own])
        relayed = relay(index - 1, [own]) if index else gots[0][:2]
    for t in range(tgt_count):
        decoder_grads = grads_call(t, codes_t, everything, decoder_grads, decoder.shape, relayed)
        if t == 0:
            relayed = relay(last, [decoder_grads])
    code_grads = None
    for index in range(len(spans)):
        code_grads = finish_call(
            owns[index], gots[index], active_mask, code_grads, offsets[index], stride, [] if index else [decoder_grads]
        )
    return code_grads, decoder_grads


def plain_body(errors, saved_codes, active_mask, decoder):
    src_count, tgt_count, feat_count, _ = decoder.shape
    src_ids = lax.axis_index("src") * src_count + jnp.arange(src_count, dtype=jnp.int32)
    tgt_ids = lax.axis_index("tgt") * tgt_count + jnp.arange(tgt_count, dtype=jnp.int32)
    kept = (tgt_ids[None, :] >= src_ids[:, None])[:, :, None, None]
    columns = lax.all_gather(errors, "src", axis=2, tiled=True)
    portion = lax.all_gather(columns, "feat", axis=1, tiled=True)
    grads = jnp.einsum("itf,jtd->ijfd", saved_codes, portion, preferred_element_type=jnp.float32)
    decoder = jnp.where(kept, decoder, jnp.zeros_like(decoder))
    term = jnp.einsum("jtd,ijfd->itf", portion, decoder, preferred_element_type=jnp.float32)
    summed = lax.psum_scatter(term, "tgt", scatter_dimension=1, tiled=True)
    code_grads = (summed * active_mask.astype(jnp.float32)).astype(jnp.bfloat16)
    return code_grads, jnp.where(kept, grads, 0.0).astype(jnp.bfloat16)


def solution(mesh):
    sizes = [mesh.shape[axis] for axis in ("src", "tgt", "feat")]
    fits = sizes[1] == 4 and sizes[2] % sizes[1] == 0
    in_specs = (
        P("tgt", "feat", "src"),
        P("src", None, "feat"),
        P("src", "tgt", "feat"),
        P("src", "tgt", "feat", None),
    )
    out_specs = (P("src", "tgt", "feat"), P("src", "tgt", "feat", None))
    return jax.shard_map(
        functools.partial(body, *sizes) if fits else plain_body,
        mesh=mesh,
        in_specs=in_specs,
        out_specs=out_specs,
        check_vma=False,
    )
```

```python
import functools

import jax
import jax.numpy as jnp
from jax import lax
from jax.experimental import pallas as pl
from jax.experimental.pallas import tpu as pltpu
from jax.sharding import PartitionSpec as P

LANES = 128
SUBLANES = 8
STEPS_PER_OCTAVE = 64
TOP = 32760.0
FLOOR = 1e-30
EIGHTHS = (2, 3, 3)
VMEM = 127 << 19
EASE = 2
ANYWHERE = pl.BlockSpec(memory_space=pl.ANY)


def pair(x):
    half = x.shape[0] // 2
    return (x[half:] << 16) | (x[:half] & 0xFFFF)


def unpair(words):
    return (words << 16) >> 16, words >> 16


def scale_and_gain(peaks):
    scale = jnp.ceil(jnp.log2(jnp.maximum(peaks, FLOOR)) * STEPS_PER_OCTAVE)
    return scale.astype(jnp.int32), jnp.exp2(scale * (-1.0 / STEPS_PER_OCTAVE)) * TOP


def row_peak(v):
    return jnp.max(jnp.abs(v), axis=1, keepdims=True)


def store_words(out_ref, layer, v, gain, base=0):
    rows, width = v.shape
    half, tiles = rows // 2, width // LANES
    words = pair(jnp.floor(v * gain + 0.5).astype(jnp.int32))
    for tile in range(tiles):
        start = base + (layer * tiles + tile) * half
        out_ref[start : start + half, :] = words[:, tile * LANES : (tile + 1) * LANES]


def lanes_of(shape):
    return lax.broadcasted_iota(jnp.int32, shape, 1)


def load_steps(in_ref):
    end = in_ref.shape[0] - SUBLANES
    low, high = unpair(in_ref[end:, :])
    step = lambda scale: jnp.exp2(scale.astype(jnp.float32) * (1.0 / STEPS_PER_OCTAVE)) * (1.0 / TOP)
    return step(low), step(high)


def load_values(in_ref, steps, layer, layers, rows, width):
    half, tiles = rows // 2, width // LANES
    words = jnp.concatenate(
        [in_ref[(layer * tiles + tile) * half : (layer * tiles + tile + 1) * half, :] for tile in range(tiles)], axis=1
    )
    values = []
    for part, step in zip(unpair(words), steps):
        column = jnp.concatenate(
            [step[:, group * layers + layer][:, None] for group in range(half // SUBLANES)], axis=0
        )
        values.append(part.astype(jnp.float32) * column)
    return jnp.concatenate(values, axis=0)


def payload_rows(layers, rows, width):
    return layers * (width // LANES) * (rows // 2) + SUBLANES


def cost(flops, bytes_accessed):
    return pl.CostEstimate(flops=flops // EASE, bytes_accessed=bytes_accessed // EASE, transcendentals=0)


def cut_kernel(n_join, offset, errors_ref, *refs):
    sem = refs[-1]
    joined = refs[:n_join]
    outs = refs[-1 - (n_join > 0) - (offset is not None) : -1]
    copies = [(piece, outs[0].at[index]) for index, piece in enumerate(joined)]
    if offset is not None:
        copies.append((errors_ref.at[:, pl.ds(offset, outs[-1].shape[1]), :], outs[-1]))
    copies = [pltpu.make_async_copy(*copy, sem.at[index]) for index, copy in enumerate(copies)]
    for copy in copies:
        copy.start()
    for copy in copies:
        copy.wait()


def cut_call(errors, offset, span, join, after):
    shapes = []
    if join:
        shapes.append(jax.ShapeDtypeStruct((len(join), *join[0].shape), errors.dtype))
    if offset is not None:
        shapes.append(jax.ShapeDtypeStruct((errors.shape[0], span, errors.shape[2]), errors.dtype))
    return pl.pallas_call(
        functools.partial(cut_kernel, len(join), offset),
        in_specs=[ANYWHERE] * (1 + len(join) + len(after)),
        out_specs=[pl.BlockSpec(memory_space=pltpu.VMEM)] * len(shapes),
        out_shape=shapes,
        scratch_shapes=[pltpu.SemaphoreType.DMA((len(join) + 1,))],
        compiler_params=pltpu.CompilerParams(vmem_limit_bytes=VMEM),
        cost_estimate=cost(0, 4 * sum(shape.size for shape in shapes)),
        name="cut",
    )(errors, *join, *after)


def terms_kernel(n_tgt, plan, offset, *refs):
    n_pieces = 1 + max(entry[0] for entry in plan)
    pieces = refs[:n_pieces]
    dec_ref = refs[n_pieces]
    own_ref, both_ref, far_ref, all_ref, err, turned, dec, acc, in_sem, dec_sem, own_sem, out_sem = refs[-12:]
    layers, tgt_count, width, columns = dec_ref.shape
    total_rows = err.shape[0]
    rows = total_rows // n_tgt
    half = rows // 2
    src, tgt, feat = (lax.axis_index(axis) for axis in ("src", "tgt", "feat"))

    def piece_copies(index):
        source, lead, skip, tokens, flip_src, flip_feat = plan[index]
        piece = pieces[source] if lead is None else pieces[source].at[lead]
        wide = piece.shape[2]
        row = 0 if flip_feat is None else pl.multiple_of((feat ^ flip_feat) * tokens, tokens)
        column = 0 if flip_src is None else pl.multiple_of((src ^ flip_src) * wide, wide)
        return [
            pltpu.make_async_copy(
                piece.at[t, pl.ds(skip, tokens), :],
                err.at[pl.ds(row, tokens), pl.ds(t * columns + column, wide)],
                in_sem.at[index * tgt_count + t],
            )
            for t in range(tgt_count)
        ]

    def dec_copy(layer, t):
        return pltpu.make_async_copy(
            dec_ref.at[layer, t], dec.at[layer, :, pl.ds(t * columns, columns)], dec_sem.at[layer * tgt_count + t]
        )

    def block(dest):
        return pl.ds(pl.multiple_of(dest * rows, rows), rows)

    def own_copies(layer):
        return [
            pltpu.make_async_copy(
                acc.at[layer, block(tgt ^ flip), :], own_ref.at[index, layer], own_sem.at[layer * 2 + index]
            )
            for index, flip in enumerate((0, 2))
        ]

    out_copy = pltpu.make_async_copy(err, all_ref.at[pl.ds(offset, total_rows), :], out_sem)

    for t in range(tgt_count):
        dec_copy(0, t).start()
    copies = [copy for index in range(len(plan)) for copy in piece_copies(index)]
    for copy in copies:
        copy.start()
    for layer in range(1, layers):
        for t in range(tgt_count):
            dec_copy(layer, t).start()
    for copy in copies:
        copy.wait()
    out_copy.start()
    for t in range(tgt_count):
        part = slice(t * columns, (t + 1) * columns)
        turned[part, :] = err[:, part].T

    lane = lanes_of((rows, LANES))
    small = lanes_of((SUBLANES, LANES))
    length = far_ref.shape[0]
    flips = (1, 3)
    tails = [jnp.zeros((SUBLANES, LANES), jnp.int32) for _ in flips]

    def multiply(layer):
        for t in range(tgt_count):
            dec_copy(layer, t).wait()
            kept = tgt * tgt_count + t >= src * layers + layer

            @pl.when(jnp.logical_not(kept))
            def _():
                dec[layer, :, t * columns : (t + 1) * columns] = jnp.zeros((width, columns), jnp.bfloat16)

        acc[layer] = jnp.dot(dec[layer], turned[...], preferred_element_type=jnp.float32).T
        for copy in own_copies(layer):
            copy.start()

    def encode(layer):
        peaks = jnp.zeros((rows, LANES), jnp.float32)
        for index, flip in enumerate(flips):
            peaks = jnp.where(lane == index, row_peak(acc[layer, block(tgt ^ flip), :]), peaks)
        scale, gain = scale_and_gain(peaks)
        scale_words = pair(scale)
        for index, flip in enumerate(flips):
            v, factor = acc[layer, block(tgt ^ flip), :], gain[:, index : index + 1]
            store_words(both_ref, layer, v, factor, index * length)
            if index:
                store_words(far_ref, layer, v, factor)
            for group in range(half // SUBLANES):
                piece = scale_words[group * SUBLANES : (group + 1) * SUBLANES, index : index + 1]
                tails[index] = jnp.where(small == group * layers + layer, piece, tails[index])

    for layer in range(layers):
        multiply(layer)
        if layer:
            encode(layer - 1)
    encode(layers - 1)
    for index, tail in enumerate(tails):
        both_ref[(index + 1) * length - SUBLANES : (index + 1) * length, :] = tail
    far_ref[length - SUBLANES :, :] = tails[1]
    for layer in range(layers):
        for copy in own_copies(layer):
            copy.wait()
    out_copy.wait()


def terms_call(pieces, plan, decoder, everything, offset, n_tgt, total_rows, tokens, after):
    layers, tgt_count, width, columns = decoder.shape
    rows = total_rows // n_tgt
    payload = (payload_rows(layers, rows, width), LANES)
    whole = pl.BlockSpec(memory_space=pltpu.VMEM)
    operands = [*pieces, decoder]
    aliases = {}
    if everything is not None:
        aliases = {len(operands): 3}
        operands.append(everything)
    operands += after
    return pl.pallas_call(
        functools.partial(terms_kernel, n_tgt, plan, offset),
        in_specs=[ANYWHERE] * len(operands),
        out_specs=[ANYWHERE, whole, whole, ANYWHERE],
        scratch_shapes=[
            pltpu.VMEM((total_rows, tgt_count * columns), jnp.bfloat16),
            pltpu.VMEM((tgt_count * columns, total_rows), jnp.bfloat16),
            pltpu.VMEM((layers, width, tgt_count * columns), jnp.bfloat16),
            pltpu.VMEM((layers, total_rows, width), jnp.float32),
            pltpu.SemaphoreType.DMA((len(plan) * tgt_count,)),
            pltpu.SemaphoreType.DMA((layers * tgt_count,)),
            pltpu.SemaphoreType.DMA((layers * 2,)),
            pltpu.SemaphoreType.DMA,
        ],
        out_shape=[
            jax.ShapeDtypeStruct((2, layers, rows, width), jnp.float32),
            jax.ShapeDtypeStruct((2 * payload[0], LANES), jnp.int32),
            jax.ShapeDtypeStruct(payload, jnp.int32),
            jax.ShapeDtypeStruct((tokens, tgt_count * columns), jnp.bfloat16),
        ],
        input_output_aliases=aliases,
        compiler_params=pltpu.CompilerParams(vmem_limit_bytes=VMEM),
        cost_estimate=cost(2 * total_rows * decoder.size, decoder.size * 2),
        name="terms",
    )(*operands)


def relay_kernel(own_ref, got_ref, *refs):
    send_ref, total = refs[-2:]
    layers, rows, width = total.shape
    half = rows // 2
    tgt = lax.axis_index("tgt")
    inner = jnp.logical_or(tgt == 1, tgt == 2).astype(jnp.float32)
    steps = [step * inner for step in load_steps(got_ref)]
    lane = lanes_of((rows, LANES))
    peaks = jnp.zeros((rows, LANES), jnp.float32)
    for layer in range(layers):
        v = own_ref[0, layer] + load_values(got_ref, steps, layer, layers, rows, width)
        total[layer] = v
        peaks = jnp.where(lane % layers == layer, row_peak(v), peaks)
    scale, gain = scale_and_gain(peaks)
    for layer in range(layers):
        store_words(send_ref, layer, total[layer], gain[:, layer : layer + 1])
    scale_words = pair(scale)
    small = lanes_of((SUBLANES, LANES)) // layers
    tail = jnp.zeros((SUBLANES, LANES), jnp.int32)
    for group in range(half // SUBLANES):
        tail = jnp.where(small == group, scale_words[group * SUBLANES : (group + 1) * SUBLANES], tail)
    send_ref[send_ref.shape[0] - SUBLANES :, :] = tail


def relay_call(own, got, after):
    _, layers, rows, width = own.shape
    shape = (got.shape[0] // 2, LANES)
    return pl.pallas_call(
        relay_kernel,
        grid=(1,),
        in_specs=[
            pl.BlockSpec((1, layers, rows, width), lambda i: (1, 0, 0, 0)),
            pl.BlockSpec(shape, lambda i: (1, 0)),
        ]
        + [ANYWHERE] * len(after),
        out_specs=pl.BlockSpec(shape, lambda i: (0, 0)),
        scratch_shapes=[pltpu.VMEM((layers, rows, width), jnp.float32)],
        out_shape=jax.ShapeDtypeStruct(shape, jnp.int32),
        compiler_params=pltpu.CompilerParams(vmem_limit_bytes=VMEM),
        cost_estimate=cost(20 * layers * rows * width, 8 * got.size),
        name="relay",
    )(own, got, *after)


def finish_kernel(n_got, offset, stride, own_ref, *refs):
    gots = refs[:n_got]
    mask_ref = refs[n_got]
    out_ref, mask_tile, out_tile, in_sem, out_sem = refs[-5:]
    layers, rows, width = out_tile.shape
    parts = mask_ref.shape[1] // stride
    tokens = rows // parts

    def mask_copy(part):
        return pltpu.make_async_copy(
            mask_ref.at[:, pl.ds(part * stride + offset, tokens), :],
            mask_tile.at[:, pl.ds(part * tokens, tokens), :],
            in_sem.at[part],
        )

    def out_copy(layer, part):
        return pltpu.make_async_copy(
            out_tile.at[layer, pl.ds(part * tokens, tokens), :],
            out_ref.at[layer, pl.ds(part * stride + offset, tokens), :],
            out_sem.at[layer * parts + part],
        )

    for part in range(parts):
        mask_copy(part).start()
    steps = [load_steps(got) for got in gots]
    for part in range(parts):
        mask_copy(part).wait()
    for layer in range(layers):
        total = own_ref[0, layer]
        for got, step in zip(gots, steps):
            total += load_values(got, step, layer, layers, rows, width)
        out_tile[layer] = (total * mask_tile[layer].astype(jnp.float32)).astype(jnp.bfloat16)
        for part in range(parts):
            out_copy(layer, part).start()
    for layer in range(layers):
        for part in range(parts):
            out_copy(layer, part).wait()


def finish_call(own, gots, mask, out, offset, stride, after):
    _, layers, rows, width = own.shape
    parts = mask.shape[1] // stride
    in_specs = [pl.BlockSpec((1, layers, rows, width), lambda i: (0, 0, 0, 0))]
    in_specs += [pl.BlockSpec(gots[-1].shape, lambda i: (0, 0)) for got in gots]
    in_specs.append(ANYWHERE)
    operands = [own, *gots, mask]
    aliases = {}
    if out is not None:
        in_specs.append(ANYWHERE)
        aliases = {len(operands): 0}
        operands.append(out)
    in_specs += [ANYWHERE] * len(after)
    operands += after
    return pl.pallas_call(
        functools.partial(finish_kernel, len(gots), offset, stride),
        grid=(1,),
        in_specs=in_specs,
        out_specs=ANYWHERE,
        scratch_shapes=[
            pltpu.VMEM((layers, rows, width), jnp.int32),
            pltpu.VMEM((layers, rows, width), jnp.bfloat16),
            pltpu.SemaphoreType.DMA((parts,)),
            pltpu.SemaphoreType.DMA((layers * parts,)),
        ],
        out_shape=jax.ShapeDtypeStruct(mask.shape, jnp.bfloat16),
        input_output_aliases=aliases,
        compiler_params=pltpu.CompilerParams(vmem_limit_bytes=VMEM),
        cost_estimate=cost(20 * layers * rows * width, layers * rows * width * 16),
        name="finish",
    )(*operands)


def turn_kernel(spans, codes_ref, out_ref):
    tokens = codes_ref.shape[1]
    stride = sum(spans)
    blocks = tokens // stride
    offset = column = 0
    for span in spans:
        rows = jnp.concatenate(
            [codes_ref[0, pl.ds(block * stride + offset, span), :] for block in range(blocks)], axis=0
        )
        out_ref[0, :, pl.ds(column, blocks * span)] = rows.T
        offset += span
        column += blocks * span


def turn_call(codes, spans):
    layers, tokens, width = codes.shape
    return pl.pallas_call(
        functools.partial(turn_kernel, spans),
        grid=(layers,),
        in_specs=[pl.BlockSpec((1, tokens, width), lambda i: (i, 0, 0))],
        out_specs=pl.BlockSpec((1, width, tokens), lambda i: (i, 0, 0)),
        out_shape=jax.ShapeDtypeStruct((layers, width, tokens), jnp.bfloat16),
        compiler_params=pltpu.CompilerParams(vmem_limit_bytes=VMEM),
        cost_estimate=cost(codes.size, codes.size * 4),
        name="turn",
    )(codes)


def grads_kernel(t, codes_ref, err_ref, *refs):
    out_ref = refs[-1]
    tgt_count, columns = 1, out_ref.shape[3]
    layer = lax.axis_index("src") * pl.num_programs(0) + pl.program_id(0)
    kept = lax.axis_index("tgt") * t[1] + t[0] >= layer
    step = min(columns, 512)

    @pl.when(kept)
    def _():
        for column in range(0, columns, step):
            out_ref[0, 0, :, column : column + step] = jnp.dot(
                codes_ref[0], err_ref[:, column : column + step], preferred_element_type=jnp.float32
            ).astype(jnp.bfloat16)

    @pl.when(jnp.logical_not(kept))
    def _():
        out_ref[...] = jnp.zeros_like(out_ref)


def grads_call(t, codes_t, everything, out, shape, after):
    layers, tgt_count, width, columns = shape
    tokens = codes_t.shape[2]
    in_specs = [
        pl.BlockSpec((1, width, tokens), lambda i: (i, 0, 0)),
        pl.BlockSpec((tokens, columns), lambda i: (0, t)),
    ]
    operands = [codes_t, everything]
    aliases = {}
    if out is not None:
        aliases = {len(operands): 0}
        operands.append(out)
    operands += after
    in_specs += [ANYWHERE] * (len(operands) - 2)
    return pl.pallas_call(
        functools.partial(grads_kernel, (t, tgt_count)),
        grid=(layers,),
        in_specs=in_specs,
        out_specs=pl.BlockSpec((1, 1, width, columns), lambda i: (i, t, 0, 0)),
        out_shape=jax.ShapeDtypeStruct(shape, jnp.bfloat16),
        input_output_aliases=aliases,
        compiler_params=pltpu.CompilerParams(vmem_limit_bytes=VMEM),
        cost_estimate=cost(
            2 * layers * width * columns * tokens, 2 * layers * width * (columns + tokens)
        ),
        name="grads",
    )(*operands)


def gather_pieces(errors, spans, offsets, n_src, n_feat, codes_t):
    if (n_src, n_feat) != (2, 4):
        for offset, span in zip(offsets, spans):
            part = lax.slice_in_dim(errors, offset, offset + span, axis=1)
            columns = lax.all_gather(part, "src", axis=2, tiled=True)
            piece = lax.all_gather(columns, "feat", axis=1, tiled=True)
            yield [piece], [(0, None, 0, n_feat * span, None, None)]
        return
    axes = ("src", "feat")
    to = lambda x, flip: lax.ppermute(x, axes, [(i, i ^ flip) for i in range(n_src * n_feat)])
    core_own = over_core(errors, n_feat)
    (part,) = cut_call(errors, 0, spans[0], [], [])
    after = [core_own, codes_t]
    for index, (offset, span) in enumerate(zip(offsets, spans)):
        arrived = [to(part, n_feat), to(part, 2), to(part, n_feat + 2)]
        more = index + 1 < len(spans)
        joined, *rest = cut_call(
            errors, offsets[index + 1] if more else None, spans[index + 1] if more else None, arrived, after
        )
        part = rest[0] if more else None
        plan = [(core, None, offset, span, 0, core) for core in (0, 1)]
        for lead, (dx, dy) in enumerate(((1, 0), (0, 2), (1, 2))):
            plan += [(2 + core, lead, 0, span, dx, dy ^ core) for core in (0, 1)]
        after = yield [errors, core_own, joined, over_core(joined, n_feat)], plan


def over_core(x, n_feat):
    return lax.ppermute(x, "feat", [(i, i ^ 1) for i in range(n_feat)])


def body(n_src, n_tgt, n_feat, errors, saved_codes, active_mask, decoder):
    tgt_count = decoder.shape[1]
    stride = errors.shape[1]
    spans = [stride * part // 8 for part in EIGHTHS]
    offsets = [sum(spans[:index]) for index in range(len(spans))]
    near = [(i, i ^ 1) for i in range(n_tgt)]
    middle = [(1, 2), (2, 1)]
    across = [(i, i ^ 2) for i in range(n_tgt)]
    codes_t = turn_call(saved_codes, spans)
    gather = gather_pieces(errors, spans, offsets, n_src, n_feat, codes_t)
    pieces, plan = next(gather)

    last = len(spans) - 1
    owns, gots = [], []
    everything, relayed = None, []
    decoder_grads = None

    def relay(index, after):
        ready = after + gots[index][1:]
        sent = relay_call(owns[index], gots[index][0], ready)
        gots[index].append(lax.ppermute(sent, "tgt", across))
        return [sent]

    for index, span in enumerate(spans):
        own, both, far, everything = terms_call(
            pieces,
            plan,
            decoder,
            everything,
            n_feat * offsets[index],
            n_tgt,
            n_feat * span,
            n_feat * stride,
            relayed,
        )
        owns.append(own)
        gots.append([lax.ppermute(both, "tgt", near), lax.ppermute(far, "tgt", middle)])
        if index < last:
            pieces, plan = gather.send([own] + (gots[index - 1][2:] if index else []))
        if index > 1:
            relayed = relay(index - 1, [own])
        if index == 0 and index < last:
            relayed = relay(0, pieces[2:3])
    for t in range(tgt_count):
        decoder_grads = grads_call(t, codes_t, everything, decoder_grads, decoder.shape, relayed)
        if t == 0:
            relayed = relay(last, [decoder_grads])
    code_grads = None
    for index in range(len(spans)):
        code_grads = finish_call(
            owns[index], gots[index], active_mask, code_grads, offsets[index], stride, [] if index else [decoder_grads]
        )
    return code_grads, decoder_grads


def plain_body(errors, saved_codes, active_mask, decoder):
    src_count, tgt_count, feat_count, _ = decoder.shape
    src_ids = lax.axis_index("src") * src_count + jnp.arange(src_count, dtype=jnp.int32)
    tgt_ids = lax.axis_index("tgt") * tgt_count + jnp.arange(tgt_count, dtype=jnp.int32)
    kept = (tgt_ids[None, :] >= src_ids[:, None])[:, :, None, None]
    columns = lax.all_gather(errors, "src", axis=2, tiled=True)
    portion = lax.all_gather(columns, "feat", axis=1, tiled=True)
    grads = jnp.einsum("itf,jtd->ijfd", saved_codes, portion, preferred_element_type=jnp.float32)
    decoder = jnp.where(kept, decoder, jnp.zeros_like(decoder))
    term = jnp.einsum("jtd,ijfd->itf", portion, decoder, preferred_element_type=jnp.float32)
    summed = lax.psum_scatter(term, "tgt", scatter_dimension=1, tiled=True)
    code_grads = (summed * active_mask.astype(jnp.float32)).astype(jnp.bfloat16)
    return code_grads, jnp.where(kept, grads, 0.0).astype(jnp.bfloat16)


def solution(mesh):
    sizes = [mesh.shape[axis] for axis in ("src", "tgt", "feat")]
    fits = sizes[1] == 4 and sizes[2] % sizes[1] == 0
    in_specs = (
        P("tgt", "feat", "src"),
        P("src", None, "feat"),
        P("src", "tgt", "feat"),
        P("src", "tgt", "feat", None),
    )
    out_specs = (P("src", "tgt", "feat"), P("src", "tgt", "feat", None))
    return jax.shard_map(
        functools.partial(body, *sizes) if fits else plain_body,
        mesh=mesh,
        in_specs=in_specs,
        out_specs=out_specs,
        check_vma=False,
    )
```

```python
import functools

import jax
import jax.numpy as jnp
from jax import lax
from jax.experimental import pallas as pl
from jax.experimental.pallas import tpu as pltpu
from jax.sharding import PartitionSpec as P

LANES = 128
SUBLANES = 8
STEPS_PER_OCTAVE = 64
TOP = 32760.0
FLOOR = 1e-30
EIGHTHS = (2, 3, 3)
VMEM = 127 << 19
EASE = 2
ANYWHERE = pl.BlockSpec(memory_space=pl.ANY)


def pair(x):
    half = x.shape[0] // 2
    return (x[half:] << 16) | (x[:half] & 0xFFFF)


def unpair(words):
    return (words << 16) >> 16, words >> 16


def scale_and_gain(peaks):
    scale = jnp.ceil(jnp.log2(jnp.maximum(peaks, FLOOR)) * STEPS_PER_OCTAVE)
    return scale.astype(jnp.int32), jnp.exp2(scale * (-1.0 / STEPS_PER_OCTAVE)) * TOP


def row_peak(v):
    return jnp.max(jnp.abs(v), axis=1, keepdims=True)


def store_words(out_ref, layer, v, gain):
    rows, width = v.shape
    half, tiles = rows // 2, width // LANES
    words = pair(jnp.floor(v * gain + 0.5).astype(jnp.int32))
    for tile in range(tiles):
        start = (layer * tiles + tile) * half
        out_ref[start : start + half, :] = words[:, tile * LANES : (tile + 1) * LANES]


def lanes_of(shape):
    return lax.broadcasted_iota(jnp.int32, shape, 1)


def load_steps(in_ref):
    end = in_ref.shape[0] - SUBLANES
    low, high = unpair(in_ref[end:, :])
    step = lambda scale: jnp.exp2(scale.astype(jnp.float32) * (1.0 / STEPS_PER_OCTAVE)) * (1.0 / TOP)
    return step(low), step(high)


def load_values(in_ref, steps, layer, layers, rows, width):
    half, tiles = rows // 2, width // LANES
    words = jnp.concatenate(
        [in_ref[(layer * tiles + tile) * half : (layer * tiles + tile + 1) * half, :] for tile in range(tiles)], axis=1
    )
    values = []
    for part, step in zip(unpair(words), steps):
        column = jnp.concatenate(
            [step[:, group * layers + layer][:, None] for group in range(half // SUBLANES)], axis=0
        )
        values.append(part.astype(jnp.float32) * column)
    return jnp.concatenate(values, axis=0)


def payload_rows(layers, rows, width):
    return layers * (width // LANES) * (rows // 2) + SUBLANES


def cost(flops, bytes_accessed):
    return pl.CostEstimate(flops=flops // EASE, bytes_accessed=bytes_accessed // EASE, transcendentals=0)


def cut_kernel(n_join, offset, errors_ref, *refs):
    sem = refs[-1]
    joined = refs[:n_join]
    outs = refs[-1 - (n_join > 0) - (offset is not None) : -1]
    copies = [(piece, outs[0].at[index]) for index, piece in enumerate(joined)]
    if offset is not None:
        copies.append((errors_ref.at[:, pl.ds(offset, outs[-1].shape[1]), :], outs[-1]))
    copies = [pltpu.make_async_copy(*copy, sem.at[index]) for index, copy in enumerate(copies)]
    for copy in copies:
        copy.start()
    for copy in copies:
        copy.wait()


def cut_call(errors, offset, span, join, after):
    shapes = []
    if join:
        shapes.append(jax.ShapeDtypeStruct((len(join), *join[0].shape), errors.dtype))
    if offset is not None:
        shapes.append(jax.ShapeDtypeStruct((errors.shape[0], span, errors.shape[2]), errors.dtype))
    return pl.pallas_call(
        functools.partial(cut_kernel, len(join), offset),
        in_specs=[ANYWHERE] * (1 + len(join) + len(after)),
        out_specs=[pl.BlockSpec(memory_space=pltpu.VMEM)] * len(shapes),
        out_shape=shapes,
        scratch_shapes=[pltpu.SemaphoreType.DMA((len(join) + 1,))],
        compiler_params=pltpu.CompilerParams(vmem_limit_bytes=VMEM),
        cost_estimate=cost(0, 4 * sum(shape.size for shape in shapes)),
        name="cut",
    )(errors, *join, *after)


def terms_kernel(n_tgt, plan, offset, *refs):
    n_pieces = 1 + max(entry[0] for entry in plan)
    pieces = refs[:n_pieces]
    dec_ref = refs[n_pieces]
    own_ref, near_ref, across_ref, far_ref, all_ref, err, dec, acc, in_sem, dec_sem, own_sem, out_sem = refs[-12:]
    layers, tgt_count, width, columns = dec_ref.shape
    total_rows = err.shape[0]
    rows = total_rows // n_tgt
    half = rows // 2
    src, tgt, feat = (lax.axis_index(axis) for axis in ("src", "tgt", "feat"))

    def piece_copies(index):
        source, lead, skip, tokens, flip_src, flip_feat = plan[index]
        piece = pieces[source] if lead is None else pieces[source].at[lead]
        wide = piece.shape[2]
        row = 0 if flip_feat is None else pl.multiple_of((feat ^ flip_feat) * tokens, tokens)
        column = 0 if flip_src is None else pl.multiple_of((src ^ flip_src) * wide, wide)
        return [
            pltpu.make_async_copy(
                piece.at[t, pl.ds(skip, tokens), :],
                err.at[pl.ds(row, tokens), pl.ds(t * columns + column, wide)],
                in_sem.at[index * tgt_count + t],
            )
            for t in range(tgt_count)
        ]

    def dec_copy(layer, t):
        return pltpu.make_async_copy(
            dec_ref.at[layer, t], dec.at[layer, :, pl.ds(t * columns, columns)], dec_sem.at[layer * tgt_count + t]
        )

    def block(dest):
        return pl.ds(pl.multiple_of(dest * rows, rows), rows)

    def own_copy(layer):
        return pltpu.make_async_copy(acc.at[layer, block(tgt), :], own_ref.at[layer], own_sem.at[layer])

    out_copy = pltpu.make_async_copy(err, all_ref.at[pl.ds(offset, total_rows), :], out_sem)

    for t in range(tgt_count):
        dec_copy(0, t).start()
    copies = [copy for index in range(len(plan)) for copy in piece_copies(index)]
    for copy in copies:
        copy.start()
    for layer in range(1, layers):
        for t in range(tgt_count):
            dec_copy(layer, t).start()
    for copy in copies:
        copy.wait()
    out_copy.start()

    lane = lanes_of((rows, LANES))
    small = lanes_of((SUBLANES, LANES))
    flips = {1: near_ref, 2: across_ref, 3: far_ref}
    tails = [jnp.zeros((SUBLANES, LANES), jnp.int32) for _ in flips]

    def multiply(layer):
        for t in range(tgt_count):
            dec_copy(layer, t).wait()
            kept = tgt * tgt_count + t >= src * layers + layer

            @pl.when(jnp.logical_not(kept))
            def _():
                dec[layer, :, t * columns : (t + 1) * columns] = jnp.zeros((width, columns), jnp.bfloat16)

        acc[layer] = lax.dot_general(
            err[...], dec[layer], (((1,), (1,)), ((), ())), preferred_element_type=jnp.float32
        )
        own_copy(layer).start()

    def encode(layer):
        peaks = jnp.zeros((rows, LANES), jnp.float32)
        for index, flip in enumerate(flips):
            peaks = jnp.where(lane == index, row_peak(acc[layer, block(tgt ^ flip), :]), peaks)
        scale, gain = scale_and_gain(peaks)
        scale_words = pair(scale)
        for index, flip in enumerate(flips):
            v, factor = acc[layer, block(tgt ^ flip), :], gain[:, index : index + 1]
            store_words(flips[flip], layer, v, factor)
            for group in range(half // SUBLANES):
                piece = scale_words[group * SUBLANES : (group + 1) * SUBLANES, index : index + 1]
                tails[index] = jnp.where(small == group * layers + layer, piece, tails[index])

    for layer in range(layers):
        multiply(layer)
        if layer:
            encode(layer - 1)
    encode(layers - 1)
    for send, tail in zip(flips.values(), tails):
        send[send.shape[0] - SUBLANES :, :] = tail
    for layer in range(layers):
        own_copy(layer).wait()
    out_copy.wait()


def terms_call(pieces, plan, decoder, everything, offset, n_tgt, total_rows, tokens, after):
    layers, tgt_count, width, columns = decoder.shape
    rows = total_rows // n_tgt
    payload = (payload_rows(layers, rows, width), LANES)
    whole = pl.BlockSpec(memory_space=pltpu.VMEM)
    operands = [*pieces, decoder]
    aliases = {}
    if everything is not None:
        aliases = {len(operands): 4}
        operands.append(everything)
    operands += after
    return pl.pallas_call(
        functools.partial(terms_kernel, n_tgt, plan, offset),
        in_specs=[ANYWHERE] * len(operands),
        out_specs=[ANYWHERE, whole, whole, whole, ANYWHERE],
        scratch_shapes=[
            pltpu.VMEM((total_rows, tgt_count * columns), jnp.bfloat16),
            pltpu.VMEM((layers, width, tgt_count * columns), jnp.bfloat16),
            pltpu.VMEM((layers, total_rows, width), jnp.float32),
            pltpu.SemaphoreType.DMA((len(plan) * tgt_count,)),
            pltpu.SemaphoreType.DMA((layers * tgt_count,)),
            pltpu.SemaphoreType.DMA((layers,)),
            pltpu.SemaphoreType.DMA,
        ],
        out_shape=[
            jax.ShapeDtypeStruct((layers, rows, width), jnp.float32),
            jax.ShapeDtypeStruct(payload, jnp.int32),
            jax.ShapeDtypeStruct(payload, jnp.int32),
            jax.ShapeDtypeStruct(payload, jnp.int32),
            jax.ShapeDtypeStruct((tokens, tgt_count * columns), jnp.bfloat16),
        ],
        input_output_aliases=aliases,
        compiler_params=pltpu.CompilerParams(vmem_limit_bytes=VMEM),
        cost_estimate=cost(2 * total_rows * decoder.size, decoder.size * 2),
        name="terms",
    )(*operands)


def finish_kernel(n_got, offset, stride, own_ref, *refs):
    gots = refs[:n_got]
    mask_ref = refs[n_got]
    out_ref, mask_tile, out_tile, in_sem, out_sem = refs[-5:]
    layers, rows, width = out_tile.shape
    parts = mask_ref.shape[1] // stride
    tokens = rows // parts

    def mask_copy(part):
        return pltpu.make_async_copy(
            mask_ref.at[:, pl.ds(part * stride + offset, tokens), :],
            mask_tile.at[:, pl.ds(part * tokens, tokens), :],
            in_sem.at[part],
        )

    def out_copy(layer, part):
        return pltpu.make_async_copy(
            out_tile.at[layer, pl.ds(part * tokens, tokens), :],
            out_ref.at[layer, pl.ds(part * stride + offset, tokens), :],
            out_sem.at[layer * parts + part],
        )

    for part in range(parts):
        mask_copy(part).start()
    steps = [load_steps(got) for got in gots]
    for part in range(parts):
        mask_copy(part).wait()
    for layer in range(layers):
        total = own_ref[layer]
        for got, step in zip(gots, steps):
            total += load_values(got, step, layer, layers, rows, width)
        out_tile[layer] = (total * mask_tile[layer].astype(jnp.float32)).astype(jnp.bfloat16)
        for part in range(parts):
            out_copy(layer, part).start()
    for layer in range(layers):
        for part in range(parts):
            out_copy(layer, part).wait()


def finish_call(own, gots, mask, out, offset, stride, after):
    layers, rows, width = own.shape
    parts = mask.shape[1] // stride
    in_specs = [pl.BlockSpec((layers, rows, width), lambda i: (0, 0, 0))]
    in_specs += [pl.BlockSpec(gots[-1].shape, lambda i: (0, 0)) for got in gots]
    in_specs.append(ANYWHERE)
    operands = [own, *gots, mask]
    aliases = {}
    if out is not None:
        in_specs.append(ANYWHERE)
        aliases = {len(operands): 0}
        operands.append(out)
    in_specs += [ANYWHERE] * len(after)
    operands += after
    return pl.pallas_call(
        functools.partial(finish_kernel, len(gots), offset, stride),
        grid=(1,),
        in_specs=in_specs,
        out_specs=ANYWHERE,
        scratch_shapes=[
            pltpu.VMEM((layers, rows, width), jnp.int32),
            pltpu.VMEM((layers, rows, width), jnp.bfloat16),
            pltpu.SemaphoreType.DMA((parts,)),
            pltpu.SemaphoreType.DMA((layers * parts,)),
        ],
        out_shape=jax.ShapeDtypeStruct(mask.shape, jnp.bfloat16),
        input_output_aliases=aliases,
        compiler_params=pltpu.CompilerParams(vmem_limit_bytes=VMEM),
        cost_estimate=cost(20 * layers * rows * width, layers * rows * width * 16),
        name="finish",
    )(*operands)


def turn_kernel(spans, codes_ref, out_ref):
    tokens = codes_ref.shape[1]
    stride = sum(spans)
    blocks = tokens // stride
    offset = column = 0
    for span in spans:
        rows = jnp.concatenate(
            [codes_ref[0, pl.ds(block * stride + offset, span), :] for block in range(blocks)], axis=0
        )
        out_ref[0, :, pl.ds(column, blocks * span)] = rows.T
        offset += span
        column += blocks * span


def turn_call(codes, spans):
    layers, tokens, width = codes.shape
    return pl.pallas_call(
        functools.partial(turn_kernel, spans),
        grid=(layers,),
        in_specs=[pl.BlockSpec((1, tokens, width), lambda i: (i, 0, 0))],
        out_specs=pl.BlockSpec((1, width, tokens), lambda i: (i, 0, 0)),
        out_shape=jax.ShapeDtypeStruct((layers, width, tokens), jnp.bfloat16),
        compiler_params=pltpu.CompilerParams(vmem_limit_bytes=VMEM),
        cost_estimate=cost(codes.size, codes.size * 4),
        name="turn",
    )(codes)


def grads_kernel(codes_ref, err_ref, *refs):
    out_ref = refs[-1]
    t, layer = pl.program_id(0), pl.program_id(1)
    columns = out_ref.shape[3]
    first_t, first_layer = (lax.axis_index(axis) * pl.num_programs(i) for i, axis in enumerate(("tgt", "src")))
    kept = first_t + t >= first_layer + layer
    step = min(columns, 512)

    @pl.when(kept)
    def _():
        for column in range(0, columns, step):
            out_ref[0, 0, :, column : column + step] = jnp.dot(
                codes_ref[0], err_ref[:, column : column + step], preferred_element_type=jnp.float32
            ).astype(jnp.bfloat16)

    @pl.when(jnp.logical_not(kept))
    def _():
        out_ref[...] = jnp.zeros_like(out_ref)


def grads_call(codes_t, everything, shape, after):
    layers, tgt_count, width, columns = shape
    tokens = codes_t.shape[2]
    in_specs = [
        pl.BlockSpec((1, width, tokens), lambda t, i: (i, 0, 0)),
        pl.BlockSpec((tokens, columns), lambda t, i: (0, t)),
    ]
    return pl.pallas_call(
        grads_kernel,
        grid=(tgt_count, layers),
        in_specs=in_specs + [ANYWHERE] * len(after),
        out_specs=pl.BlockSpec((1, 1, width, columns), lambda t, i: (i, t, 0, 0)),
        out_shape=jax.ShapeDtypeStruct(shape, jnp.bfloat16),
        compiler_params=pltpu.CompilerParams(vmem_limit_bytes=VMEM),
        cost_estimate=cost(
            2 * tgt_count * layers * width * columns * tokens, 2 * tgt_count * layers * width * (columns + tokens)
        ),
        name="grads",
    )(codes_t, everything, *after)


def gather_pieces(errors, spans, offsets, n_src, n_feat, codes_t):
    if (n_src, n_feat) != (2, 4):
        for offset, span in zip(offsets, spans):
            part = lax.slice_in_dim(errors, offset, offset + span, axis=1)
            columns = lax.all_gather(part, "src", axis=2, tiled=True)
            piece = lax.all_gather(columns, "feat", axis=1, tiled=True)
            yield [piece], [(0, None, 0, n_feat * span, None, None)]
        return
    axes = ("src", "feat")
    to = lambda x, flip: lax.ppermute(x, axes, [(i, i ^ flip) for i in range(n_src * n_feat)])
    core_own = over_core(errors, n_feat)
    (part,) = cut_call(errors, 0, spans[0], [], [])
    after = [core_own, codes_t]
    for index, (offset, span) in enumerate(zip(offsets, spans)):
        arrived = [to(part, n_feat), to(part, 2), to(part, n_feat + 2)]
        more = index + 1 < len(spans)
        joined, *rest = cut_call(
            errors, offsets[index + 1] if more else None, spans[index + 1] if more else None, arrived, after
        )
        part = rest[0] if more else None
        plan = [(core, None, offset, span, 0, core) for core in (0, 1)]
        for lead, (dx, dy) in enumerate(((1, 0), (0, 2), (1, 2))):
            plan += [(2 + core, lead, 0, span, dx, dy ^ core) for core in (0, 1)]
        after = yield [errors, core_own, joined, over_core(joined, n_feat)], plan


def over_core(x, n_feat):
    return lax.ppermute(x, "feat", [(i, i ^ 1) for i in range(n_feat)])


def body(n_src, n_tgt, n_feat, errors, saved_codes, active_mask, decoder):
    tgt_count = decoder.shape[1]
    stride = errors.shape[1]
    spans = [stride * part // 8 for part in EIGHTHS]
    offsets = [sum(spans[:index]) for index in range(len(spans))]
    codes_t = turn_call(saved_codes, spans)
    gather = gather_pieces(errors, spans, offsets, n_src, n_feat, codes_t)
    pieces, plan = next(gather)
    last = len(spans) - 1
    owns, gots = [], []
    everything = None
    for index, span in enumerate(spans):
        own, near, across, far, everything = terms_call(
            pieces,
            plan,
            decoder,
            everything,
            n_feat * offsets[index],
            n_tgt,
            n_feat * span,
            n_feat * stride,
            [],
        )
        owns.append(own)
        send = lambda x, flip: lax.ppermute(x, "tgt", [(i, i ^ flip) for i in range(n_tgt)])
        gots.append([send(far, 3), send(across, 2), send(near, 1)])
        if index < last:
            pieces, plan = gather.send([own] + (gots[index - 1] if index else []))
    decoder_grads = grads_call(codes_t, everything, decoder.shape, gots[-2] if last else [])
    code_grads = None
    for index in range(len(spans)):
        after = [decoder_grads, *gots[last]] if index == 0 else []
        code_grads = finish_call(owns[index], gots[index], active_mask, code_grads, offsets[index], stride, after)
    return code_grads, decoder_grads


def plain_body(errors, saved_codes, active_mask, decoder):
    src_count, tgt_count, feat_count, _ = decoder.shape
    src_ids = lax.axis_index("src") * src_count + jnp.arange(src_count, dtype=jnp.int32)
    tgt_ids = lax.axis_index("tgt") * tgt_count + jnp.arange(tgt_count, dtype=jnp.int32)
    kept = (tgt_ids[None, :] >= src_ids[:, None])[:, :, None, None]
    columns = lax.all_gather(errors, "src", axis=2, tiled=True)
    portion = lax.all_gather(columns, "feat", axis=1, tiled=True)
    grads = jnp.einsum("itf,jtd->ijfd", saved_codes, portion, preferred_element_type=jnp.float32)
    decoder = jnp.where(kept, decoder, jnp.zeros_like(decoder))
    term = jnp.einsum("jtd,ijfd->itf", portion, decoder, preferred_element_type=jnp.float32)
    summed = lax.psum_scatter(term, "tgt", scatter_dimension=1, tiled=True)
    code_grads = (summed * active_mask.astype(jnp.float32)).astype(jnp.bfloat16)
    return code_grads, jnp.where(kept, grads, 0.0).astype(jnp.bfloat16)


def solution(mesh):
    sizes = [mesh.shape[axis] for axis in ("src", "tgt", "feat")]
    fits = sizes[1] == 4 and sizes[2] % sizes[1] == 0
    in_specs = (
        P("tgt", "feat", "src"),
        P("src", None, "feat"),
        P("src", "tgt", "feat"),
        P("src", "tgt", "feat", None),
    )
    out_specs = (P("src", "tgt", "feat"), P("src", "tgt", "feat", None))
    return jax.shard_map(
        functools.partial(body, *sizes) if fits else plain_body,
        mesh=mesh,
        in_specs=in_specs,
        out_specs=out_specs,
        check_vma=False,
    )
```

```python
import functools

import jax
import jax.numpy as jnp
from jax import lax
from jax.experimental import pallas as pl
from jax.experimental.pallas import tpu as pltpu
from jax.sharding import PartitionSpec as P

LANES = 128
SUBLANES = 8
STEPS_PER_OCTAVE = 64
TOP = 32760.0
FLOOR = 1e-30
EIGHTHS = (2, 3, 3)
VMEM = 127 << 19
EASE = 2
ANYWHERE = pl.BlockSpec(memory_space=pl.ANY)


def pair(x):
    half = x.shape[0] // 2
    return (x[half:] << 16) | (x[:half] & 0xFFFF)


def unpair(words):
    return (words << 16) >> 16, words >> 16


def scale_and_gain(peaks):
    scale = jnp.ceil(jnp.log2(jnp.maximum(peaks, FLOOR)) * STEPS_PER_OCTAVE)
    return scale.astype(jnp.int32), jnp.exp2(scale * (-1.0 / STEPS_PER_OCTAVE)) * TOP


def row_peak(v):
    return jnp.max(jnp.abs(v), axis=1, keepdims=True)


def store_words(out_ref, layer, v, gain):
    rows, width = v.shape
    half, tiles = rows // 2, width // LANES
    words = pair(jnp.floor(v * gain + 0.5).astype(jnp.int32))
    for tile in range(tiles):
        start = (layer * tiles + tile) * half
        out_ref[start : start + half, :] = words[:, tile * LANES : (tile + 1) * LANES]


def lanes_of(shape):
    return lax.broadcasted_iota(jnp.int32, shape, 1)


def load_steps(in_ref):
    end = in_ref.shape[0] - SUBLANES
    low, high = unpair(in_ref[end:, :])
    step = lambda scale: jnp.exp2(scale.astype(jnp.float32) * (1.0 / STEPS_PER_OCTAVE)) * (1.0 / TOP)
    return step(low), step(high)


def load_values(in_ref, steps, layer, layers, rows, width):
    half, tiles = rows // 2, width // LANES
    words = jnp.concatenate(
        [in_ref[(layer * tiles + tile) * half : (layer * tiles + tile + 1) * half, :] for tile in range(tiles)], axis=1
    )
    values = []
    for part, step in zip(unpair(words), steps):
        column = jnp.concatenate(
            [step[:, group * layers + layer][:, None] for group in range(half // SUBLANES)], axis=0
        )
        values.append(part.astype(jnp.float32) * column)
    return jnp.concatenate(values, axis=0)


def payload_rows(layers, rows, width):
    return layers * (width // LANES) * (rows // 2) + SUBLANES


def cost(flops, bytes_accessed):
    return pl.CostEstimate(flops=flops // EASE, bytes_accessed=bytes_accessed // EASE, transcendentals=0)


def cut_kernel(n_join, offset, errors_ref, *refs):
    sem = refs[-1]
    joined = refs[:n_join]
    outs = refs[-1 - (n_join > 0) - (offset is not None) : -1]
    copies = [(piece, outs[0].at[index]) for index, piece in enumerate(joined)]
    if offset is not None:
        copies.append((errors_ref.at[:, pl.ds(offset, outs[-1].shape[1]), :], outs[-1]))
    copies = [pltpu.make_async_copy(*copy, sem.at[index]) for index, copy in enumerate(copies)]
    for copy in copies:
        copy.start()
    for copy in copies:
        copy.wait()


def cut_call(errors, offset, span, join, after):
    shapes = []
    if join:
        shapes.append(jax.ShapeDtypeStruct((len(join), *join[0].shape), errors.dtype))
    if offset is not None:
        shapes.append(jax.ShapeDtypeStruct((errors.shape[0], span, errors.shape[2]), errors.dtype))
    return pl.pallas_call(
        functools.partial(cut_kernel, len(join), offset),
        in_specs=[ANYWHERE] * (1 + len(join) + len(after)),
        out_specs=[pl.BlockSpec(memory_space=pltpu.VMEM)] * len(shapes),
        out_shape=shapes,
        scratch_shapes=[pltpu.SemaphoreType.DMA((len(join) + 1,))],
        compiler_params=pltpu.CompilerParams(vmem_limit_bytes=VMEM),
        cost_estimate=cost(0, 4 * sum(shape.size for shape in shapes)),
        name="cut",
    )(errors, *join, *after)


def terms_kernel(n_tgt, plan, offset, *refs):
    n_pieces = 1 + max(entry[0] for entry in plan)
    pieces = refs[:n_pieces]
    dec_ref = refs[n_pieces]
    own_ref, near_ref, across_ref, far_ref, all_ref, err, dec, acc, in_sem, dec_sem, own_sem, out_sem = refs[-12:]
    layers, tgt_count, width, columns = dec_ref.shape
    total_rows = err.shape[0]
    rows = total_rows // n_tgt
    half = rows // 2
    src, tgt, feat = (lax.axis_index(axis) for axis in ("src", "tgt", "feat"))

    def piece_copies(index):
        source, lead, skip, tokens, flip_src, flip_feat = plan[index]
        piece = pieces[source] if lead is None else pieces[source].at[lead]
        wide = piece.shape[2]
        row = 0 if flip_feat is None else pl.multiple_of((feat ^ flip_feat) * tokens, tokens)
        column = 0 if flip_src is None else pl.multiple_of((src ^ flip_src) * wide, wide)
        return [
            pltpu.make_async_copy(
                piece.at[t, pl.ds(skip, tokens), :],
                err.at[pl.ds(row, tokens), pl.ds(t * columns + column, wide)],
                in_sem.at[index * tgt_count + t],
            )
            for t in range(tgt_count)
        ]

    def dec_copy(layer, t):
        return pltpu.make_async_copy(
            dec_ref.at[layer, t], dec.at[layer, :, pl.ds(t * columns, columns)], dec_sem.at[layer * tgt_count + t]
        )

    def block(dest):
        return pl.ds(pl.multiple_of(dest * rows, rows), rows)

    def own_copy(layer):
        return pltpu.make_async_copy(acc.at[layer, block(tgt), :], own_ref.at[layer], own_sem.at[layer])

    out_copy = pltpu.make_async_copy(err, all_ref.at[pl.ds(offset, total_rows), :], out_sem)

    for t in range(tgt_count):
        dec_copy(0, t).start()
    copies = [copy for index in range(len(plan)) for copy in piece_copies(index)]
    for copy in copies:
        copy.start()
    for layer in range(1, layers):
        for t in range(tgt_count):
            dec_copy(layer, t).start()
    for copy in copies:
        copy.wait()
    out_copy.start()

    lane = lanes_of((rows, LANES))
    small = lanes_of((SUBLANES, LANES))
    flips = {1: near_ref, 2: across_ref, 3: far_ref}
    tails = [jnp.zeros((SUBLANES, LANES), jnp.int32) for _ in flips]

    def multiply(layer):
        for t in range(tgt_count):
            dec_copy(layer, t).wait()
            kept = tgt * tgt_count + t >= src * layers + layer

            @pl.when(jnp.logical_not(kept))
            def _():
                dec[layer, :, t * columns : (t + 1) * columns] = jnp.zeros((width, columns), jnp.bfloat16)

        acc[layer] = lax.dot_general(
            err[...], dec[layer], (((1,), (1,)), ((), ())), preferred_element_type=jnp.float32
        )
        own_copy(layer).start()

    def encode(layer):
        peaks = jnp.zeros((rows, LANES), jnp.float32)
        for index, flip in enumerate(flips):
            peaks = jnp.where(lane == index, row_peak(acc[layer, block(tgt ^ flip), :]), peaks)
        scale, gain = scale_and_gain(peaks)
        scale_words = pair(scale)
        for index, flip in enumerate(flips):
            v, factor = acc[layer, block(tgt ^ flip), :], gain[:, index : index + 1]
            store_words(flips[flip], layer, v, factor)
            for group in range(half // SUBLANES):
                piece = scale_words[group * SUBLANES : (group + 1) * SUBLANES, index : index + 1]
                tails[index] = jnp.where(small == group * layers + layer, piece, tails[index])

    for layer in range(layers):
        multiply(layer)
        if layer:
            encode(layer - 1)
    encode(layers - 1)
    for send, tail in zip(flips.values(), tails):
        send[send.shape[0] - SUBLANES :, :] = tail
    for layer in range(layers):
        own_copy(layer).wait()
    out_copy.wait()


def terms_call(pieces, plan, decoder, everything, offset, n_tgt, total_rows, tokens, after):
    layers, tgt_count, width, columns = decoder.shape
    rows = total_rows // n_tgt
    payload = (payload_rows(layers, rows, width), LANES)
    whole = pl.BlockSpec(memory_space=pltpu.VMEM)
    operands = [*pieces, decoder]
    aliases = {}
    if everything is not None:
        aliases = {len(operands): 4}
        operands.append(everything)
    operands += after
    return pl.pallas_call(
        functools.partial(terms_kernel, n_tgt, plan, offset),
        in_specs=[ANYWHERE] * len(operands),
        out_specs=[ANYWHERE, whole, whole, whole, ANYWHERE],
        scratch_shapes=[
            pltpu.VMEM((total_rows, tgt_count * columns), jnp.bfloat16),
            pltpu.VMEM((layers, width, tgt_count * columns), jnp.bfloat16),
            pltpu.VMEM((layers, total_rows, width), jnp.float32),
            pltpu.SemaphoreType.DMA((len(plan) * tgt_count,)),
            pltpu.SemaphoreType.DMA((layers * tgt_count,)),
            pltpu.SemaphoreType.DMA((layers,)),
            pltpu.SemaphoreType.DMA,
        ],
        out_shape=[
            jax.ShapeDtypeStruct((layers, rows, width), jnp.float32),
            jax.ShapeDtypeStruct(payload, jnp.int32),
            jax.ShapeDtypeStruct(payload, jnp.int32),
            jax.ShapeDtypeStruct(payload, jnp.int32),
            jax.ShapeDtypeStruct((tokens, tgt_count * columns), jnp.bfloat16),
        ],
        input_output_aliases=aliases,
        compiler_params=pltpu.CompilerParams(vmem_limit_bytes=VMEM),
        cost_estimate=cost(2 * total_rows * decoder.size, decoder.size * 2),
        name="terms",
    )(*operands)


def finish_kernel(n_got, offset, stride, own_ref, *refs):
    gots = refs[:n_got]
    mask_ref = refs[n_got]
    out_ref, mask_tile, out_tile, in_sem, out_sem = refs[-5:]
    layers, rows, width = out_tile.shape
    parts = mask_ref.shape[1] // stride
    tokens = rows // parts

    def mask_copy(part):
        return pltpu.make_async_copy(
            mask_ref.at[:, pl.ds(part * stride + offset, tokens), :],
            mask_tile.at[:, pl.ds(part * tokens, tokens), :],
            in_sem.at[part],
        )

    def out_copy(layer, part):
        return pltpu.make_async_copy(
            out_tile.at[layer, pl.ds(part * tokens, tokens), :],
            out_ref.at[layer, pl.ds(part * stride + offset, tokens), :],
            out_sem.at[layer * parts + part],
        )

    for part in range(parts):
        mask_copy(part).start()
    steps = [load_steps(got) for got in gots]
    for part in range(parts):
        mask_copy(part).wait()
    for layer in range(layers):
        total = own_ref[layer]
        for got, step in zip(gots, steps):
            total += load_values(got, step, layer, layers, rows, width)
        out_tile[layer] = (total * mask_tile[layer].astype(jnp.float32)).astype(jnp.bfloat16)
        for part in range(parts):
            out_copy(layer, part).start()
    for layer in range(layers):
        for part in range(parts):
            out_copy(layer, part).wait()


def finish_call(own, gots, mask, out, offset, stride, after):
    layers, rows, width = own.shape
    parts = mask.shape[1] // stride
    in_specs = [pl.BlockSpec((layers, rows, width), lambda i: (0, 0, 0))]
    in_specs += [pl.BlockSpec(gots[-1].shape, lambda i: (0, 0)) for got in gots]
    in_specs.append(ANYWHERE)
    operands = [own, *gots, mask]
    aliases = {}
    if out is not None:
        in_specs.append(ANYWHERE)
        aliases = {len(operands): 0}
        operands.append(out)
    in_specs += [ANYWHERE] * len(after)
    operands += after
    return pl.pallas_call(
        functools.partial(finish_kernel, len(gots), offset, stride),
        grid=(1,),
        in_specs=in_specs,
        out_specs=ANYWHERE,
        scratch_shapes=[
            pltpu.VMEM((layers, rows, width), jnp.int32),
            pltpu.VMEM((layers, rows, width), jnp.bfloat16),
            pltpu.SemaphoreType.DMA((parts,)),
            pltpu.SemaphoreType.DMA((layers * parts,)),
        ],
        out_shape=jax.ShapeDtypeStruct(mask.shape, jnp.bfloat16),
        input_output_aliases=aliases,
        compiler_params=pltpu.CompilerParams(vmem_limit_bytes=VMEM),
        cost_estimate=cost(20 * layers * rows * width, layers * rows * width * 16),
        name="finish",
    )(*operands)


def turn_kernel(spans, codes_ref, out_ref):
    tokens = codes_ref.shape[1]
    stride = sum(spans)
    blocks = tokens // stride
    offset = column = 0
    for span in spans:
        rows = jnp.concatenate(
            [codes_ref[0, pl.ds(block * stride + offset, span), :] for block in range(blocks)], axis=0
        )
        out_ref[0, :, pl.ds(column, blocks * span)] = rows.T
        offset += span
        column += blocks * span


def turn_call(codes, spans):
    layers, tokens, width = codes.shape
    return pl.pallas_call(
        functools.partial(turn_kernel, spans),
        grid=(layers,),
        in_specs=[pl.BlockSpec((1, tokens, width), lambda i: (i, 0, 0))],
        out_specs=pl.BlockSpec((1, width, tokens), lambda i: (i, 0, 0)),
        out_shape=jax.ShapeDtypeStruct((layers, width, tokens), jnp.bfloat16),
        compiler_params=pltpu.CompilerParams(vmem_limit_bytes=VMEM),
        cost_estimate=cost(codes.size, codes.size * 4),
        name="turn",
    )(codes)


def grads_kernel(codes_ref, err_ref, *refs):
    out_ref = refs[-1]
    t, layer = pl.program_id(0), pl.program_id(1)
    columns = out_ref.shape[3]
    first_t, first_layer = (lax.axis_index(axis) * pl.num_programs(i) for i, axis in enumerate(("tgt", "src")))
    kept = first_t + t >= first_layer + layer
    step = min(columns, 512)

    @pl.when(kept)
    def _():
        for column in range(0, columns, step):
            out_ref[0, 0, :, column : column + step] = jnp.dot(
                codes_ref[0], err_ref[:, column : column + step], preferred_element_type=jnp.float32
            ).astype(jnp.bfloat16)

    @pl.when(jnp.logical_not(kept))
    def _():
        out_ref[...] = jnp.zeros_like(out_ref)


def grads_call(codes_t, everything, shape, after):
    layers, tgt_count, width, columns = shape
    tokens = codes_t.shape[2]
    in_specs = [
        pl.BlockSpec((1, width, tokens), lambda t, i: (i, 0, 0)),
        pl.BlockSpec((tokens, columns), lambda t, i: (0, t)),
    ]
    return pl.pallas_call(
        grads_kernel,
        grid=(tgt_count, layers),
        in_specs=in_specs + [ANYWHERE] * len(after),
        out_specs=pl.BlockSpec((1, 1, width, columns), lambda t, i: (i, t, 0, 0)),
        out_shape=jax.ShapeDtypeStruct(shape, jnp.bfloat16),
        compiler_params=pltpu.CompilerParams(vmem_limit_bytes=VMEM),
        cost_estimate=cost(
            2 * tgt_count * layers * width * columns * tokens, 2 * tgt_count * layers * width * (columns + tokens)
        ),
        name="grads",
    )(codes_t, everything, *after)


def gather_pieces(errors, spans, offsets, n_src, n_feat, codes_t):
    if (n_src, n_feat) != (2, 4):
        for offset, span in zip(offsets, spans):
            part = lax.slice_in_dim(errors, offset, offset + span, axis=1)
            columns = lax.all_gather(part, "src", axis=2, tiled=True)
            piece = lax.all_gather(columns, "feat", axis=1, tiled=True)
            yield [piece], [(0, None, 0, n_feat * span, None, None)]
        return
    axes = ("src", "feat")
    to = lambda x, flip: lax.ppermute(x, axes, [(i, i ^ flip) for i in range(n_src * n_feat)])
    core_own = over_core(errors, n_feat)
    (part,) = cut_call(errors, 0, spans[0], [], [])
    after = [core_own, codes_t]
    for index, (offset, span) in enumerate(zip(offsets, spans)):
        arrived = [to(part, n_feat), to(part, 2), to(part, n_feat + 2)]
        more = index + 1 < len(spans)
        joined, *rest = cut_call(
            errors, offsets[index + 1] if more else None, spans[index + 1] if more else None, arrived, after
        )
        part = rest[0] if more else None
        plan = [(core, None, offset, span, 0, core) for core in (0, 1)]
        for lead, (dx, dy) in enumerate(((1, 0), (0, 2), (1, 2))):
            plan += [(2 + core, lead, 0, span, dx, dy ^ core) for core in (0, 1)]
        after = yield [errors, core_own, joined, over_core(joined, n_feat)], plan


def over_core(x, n_feat):
    return lax.ppermute(x, "feat", [(i, i ^ 1) for i in range(n_feat)])


def body(n_src, n_tgt, n_feat, errors, saved_codes, active_mask, decoder):
    tgt_count = decoder.shape[1]
    stride = errors.shape[1]
    spans = [stride * part // 8 for part in EIGHTHS]
    offsets = [sum(spans[:index]) for index in range(len(spans))]
    codes_t = turn_call(saved_codes, spans)
    gather = gather_pieces(errors, spans, offsets, n_src, n_feat, codes_t)
    pieces, plan = next(gather)
    last = len(spans) - 1
    owns, gots = [], []
    everything = None
    for index, span in enumerate(spans):
        own, near, across, far, everything = terms_call(
            pieces,
            plan,
            decoder,
            everything,
            n_feat * offsets[index],
            n_tgt,
            n_feat * span,
            n_feat * stride,
            gots[index - 1][:1] if index > 1 else [],
        )
        owns.append(own)
        send = lambda x, flip: lax.ppermute(x, "tgt", [(i, i ^ flip) for i in range(n_tgt)])
        gots.append([send(far, 3), send(across, 2), send(near, 1)])
        if index < last:
            pieces, plan = gather.send([own] + (gots[index - 1] if index else gots[0][:1]))
    decoder_grads = grads_call(codes_t, everything, decoder.shape, [])
    code_grads = None
    for index in range(len(spans)):
        after = [] if index else [decoder_grads]
        code_grads = finish_call(owns[index], gots[index], active_mask, code_grads, offsets[index], stride, after)
    return code_grads, decoder_grads


def plain_body(errors, saved_codes, active_mask, decoder):
    src_count, tgt_count, feat_count, _ = decoder.shape
    src_ids = lax.axis_index("src") * src_count + jnp.arange(src_count, dtype=jnp.int32)
    tgt_ids = lax.axis_index("tgt") * tgt_count + jnp.arange(tgt_count, dtype=jnp.int32)
    kept = (tgt_ids[None, :] >= src_ids[:, None])[:, :, None, None]
    columns = lax.all_gather(errors, "src", axis=2, tiled=True)
    portion = lax.all_gather(columns, "feat", axis=1, tiled=True)
    grads = jnp.einsum("itf,jtd->ijfd", saved_codes, portion, preferred_element_type=jnp.float32)
    decoder = jnp.where(kept, decoder, jnp.zeros_like(decoder))
    term = jnp.einsum("jtd,ijfd->itf", portion, decoder, preferred_element_type=jnp.float32)
    summed = lax.psum_scatter(term, "tgt", scatter_dimension=1, tiled=True)
    code_grads = (summed * active_mask.astype(jnp.float32)).astype(jnp.bfloat16)
    return code_grads, jnp.where(kept, grads, 0.0).astype(jnp.bfloat16)


def solution(mesh):
    sizes = [mesh.shape[axis] for axis in ("src", "tgt", "feat")]
    fits = sizes[1] == 4 and sizes[2] % sizes[1] == 0
    in_specs = (
        P("tgt", "feat", "src"),
        P("src", None, "feat"),
        P("src", "tgt", "feat"),
        P("src", "tgt", "feat", None),
    )
    out_specs = (P("src", "tgt", "feat"), P("src", "tgt", "feat", None))
    return jax.shard_map(
        functools.partial(body, *sizes) if fits else plain_body,
        mesh=mesh,
        in_specs=in_specs,
        out_specs=out_specs,
        check_vma=False,
    )
```

```python
import functools

import jax
import jax.numpy as jnp
from jax import lax
from jax.experimental import pallas as pl
from jax.experimental.pallas import tpu as pltpu
from jax.sharding import PartitionSpec as P

LANES = 128
SUBLANES = 8
STEPS_PER_OCTAVE = 64
TOP = 32760.0
FLOOR = 1e-30
EIGHTHS = (2, 3, 3)
VMEM = 127 << 19
EASE = 2
ANYWHERE = pl.BlockSpec(memory_space=pl.ANY)


def pair(x):
    half = x.shape[0] // 2
    return (x[half:] << 16) | (x[:half] & 0xFFFF)


def unpair(words):
    return (words << 16) >> 16, words >> 16


def scale_and_gain(peaks):
    scale = jnp.ceil(jnp.log2(jnp.maximum(peaks, FLOOR)) * STEPS_PER_OCTAVE)
    return scale.astype(jnp.int32), jnp.exp2(scale * (-1.0 / STEPS_PER_OCTAVE)) * TOP


def row_peak(v):
    return jnp.max(jnp.abs(v), axis=1, keepdims=True)


def store_words(out_ref, layer, v, gain, base=0):
    rows, width = v.shape
    half, tiles = rows // 2, width // LANES
    words = pair(jnp.floor(v * gain + 0.5).astype(jnp.int32))
    for tile in range(tiles):
        start = base + (layer * tiles + tile) * half
        out_ref[start : start + half, :] = words[:, tile * LANES : (tile + 1) * LANES]


def lanes_of(shape):
    return lax.broadcasted_iota(jnp.int32, shape, 1)


def load_steps(in_ref):
    end = in_ref.shape[0] - SUBLANES
    low, high = unpair(in_ref[end:, :])
    step = lambda scale: jnp.exp2(scale.astype(jnp.float32) * (1.0 / STEPS_PER_OCTAVE)) * (1.0 / TOP)
    return step(low), step(high)


def load_values(in_ref, steps, layer, layers, rows, width):
    half, tiles = rows // 2, width // LANES
    words = jnp.concatenate(
        [in_ref[(layer * tiles + tile) * half : (layer * tiles + tile + 1) * half, :] for tile in range(tiles)], axis=1
    )
    values = []
    for part, step in zip(unpair(words), steps):
        column = jnp.concatenate(
            [step[:, group * layers + layer][:, None] for group in range(half // SUBLANES)], axis=0
        )
        values.append(part.astype(jnp.float32) * column)
    return jnp.concatenate(values, axis=0)


def payload_rows(layers, rows, width):
    return layers * (width // LANES) * (rows // 2) + SUBLANES


def cost(flops, bytes_accessed):
    return pl.CostEstimate(flops=flops // EASE, bytes_accessed=bytes_accessed // EASE, transcendentals=0)


def cut_kernel(n_join, offset, errors_ref, *refs):
    sem = refs[-1]
    joined = refs[:n_join]
    outs = refs[-1 - (n_join > 0) - (offset is not None) : -1]
    copies = [(piece, outs[0].at[index]) for index, piece in enumerate(joined)]
    if offset is not None:
        copies.append((errors_ref.at[:, pl.ds(offset, outs[-1].shape[1]), :], outs[-1]))
    copies = [pltpu.make_async_copy(*copy, sem.at[index]) for index, copy in enumerate(copies)]
    for copy in copies:
        copy.start()
    for copy in copies:
        copy.wait()


def cut_call(errors, offset, span, join, after):
    shapes = []
    if join:
        shapes.append(jax.ShapeDtypeStruct((len(join), *join[0].shape), errors.dtype))
    if offset is not None:
        shapes.append(jax.ShapeDtypeStruct((errors.shape[0], span, errors.shape[2]), errors.dtype))
    return pl.pallas_call(
        functools.partial(cut_kernel, len(join), offset),
        in_specs=[ANYWHERE] * (1 + len(join) + len(after)),
        out_specs=[pl.BlockSpec(memory_space=pltpu.VMEM)] * len(shapes),
        out_shape=shapes,
        scratch_shapes=[pltpu.SemaphoreType.DMA((len(join) + 1,))],
        compiler_params=pltpu.CompilerParams(vmem_limit_bytes=VMEM),
        cost_estimate=cost(0, 4 * sum(shape.size for shape in shapes)),
        name="cut",
    )(errors, *join, *after)


def terms_kernel(n_tgt, plan, offset, carried, *refs):
    n_pieces = 1 + max(entry[0] for entry in plan)
    pieces = refs[:n_pieces]
    dec_ref = refs[n_pieces]
    own_ref, near_ref, across_ref, far_ref, all_ref, err, dec, acc, in_sem, dec_sem, own_sem, out_sem, carry_sem = refs[-13:]
    layers, tgt_count, width, columns = dec_ref.shape
    total_rows = err.shape[0]
    rows = total_rows // n_tgt
    half = rows // 2
    src, tgt, feat = (lax.axis_index(axis) for axis in ("src", "tgt", "feat"))

    def piece_copies(index):
        source, lead, skip, tokens, flip_src, flip_feat = plan[index]
        piece = pieces[source] if lead is None else pieces[source].at[lead]
        wide = piece.shape[2]
        row = 0 if flip_feat is None else pl.multiple_of((feat ^ flip_feat) * tokens, tokens)
        column = 0 if flip_src is None else pl.multiple_of((src ^ flip_src) * wide, wide)
        return [
            pltpu.make_async_copy(
                piece.at[t, pl.ds(skip, tokens), :],
                err.at[pl.ds(row, tokens), pl.ds(t * columns + column, wide)],
                in_sem.at[index * tgt_count + t],
            )
            for t in range(tgt_count)
        ]

    def dec_copy(layer, t):
        return pltpu.make_async_copy(
            dec_ref.at[layer, t], dec.at[layer, :, pl.ds(t * columns, columns)], dec_sem.at[layer * tgt_count + t]
        )

    def block(dest):
        return pl.ds(pl.multiple_of(dest * rows, rows), rows)

    def own_copy(layer):
        return pltpu.make_async_copy(acc.at[layer, block(tgt), :], own_ref.at[layer], own_sem.at[layer])

    carry = pltpu.make_async_copy(refs[n_pieces + 1], near_ref.at[pl.ds(0, carried), :], carry_sem) if carried else None
    out_copy = pltpu.make_async_copy(err, all_ref.at[pl.ds(offset, total_rows), :], out_sem)

    for t in range(tgt_count):
        dec_copy(0, t).start()
    copies = [copy for index in range(len(plan)) for copy in piece_copies(index)]
    for copy in copies:
        copy.start()
    if carried:
        carry.start()
    for layer in range(1, layers):
        for t in range(tgt_count):
            dec_copy(layer, t).start()
    for copy in copies:
        copy.wait()
    out_copy.start()

    lane = lanes_of((rows, LANES))
    small = lanes_of((SUBLANES, LANES))
    flips = {1: near_ref, 2: across_ref, 3: far_ref}
    tails = [jnp.zeros((SUBLANES, LANES), jnp.int32) for _ in flips]

    def multiply(layer):
        for t in range(tgt_count):
            dec_copy(layer, t).wait()
            kept = tgt * tgt_count + t >= src * layers + layer

            @pl.when(jnp.logical_not(kept))
            def _():
                dec[layer, :, t * columns : (t + 1) * columns] = jnp.zeros((width, columns), jnp.bfloat16)

        acc[layer] = lax.dot_general(
            err[...], dec[layer], (((1,), (1,)), ((), ())), preferred_element_type=jnp.float32
        )
        own_copy(layer).start()

    def encode(layer):
        peaks = jnp.zeros((rows, LANES), jnp.float32)
        for index, flip in enumerate(flips):
            peaks = jnp.where(lane == index, row_peak(acc[layer, block(tgt ^ flip), :]), peaks)
        scale, gain = scale_and_gain(peaks)
        scale_words = pair(scale)
        for index, flip in enumerate(flips):
            v, factor = acc[layer, block(tgt ^ flip), :], gain[:, index : index + 1]
            store_words(flips[flip], layer, v, factor, carried if flip == 1 else 0)
            for group in range(half // SUBLANES):
                piece = scale_words[group * SUBLANES : (group + 1) * SUBLANES, index : index + 1]
                tails[index] = jnp.where(small == group * layers + layer, piece, tails[index])

    for layer in range(layers):
        multiply(layer)
        if layer:
            encode(layer - 1)
    encode(layers - 1)
    for send, tail in zip(flips.values(), tails):
        send[send.shape[0] - SUBLANES :, :] = tail
    for layer in range(layers):
        own_copy(layer).wait()
    out_copy.wait()
    if carried:
        carry.wait()


def terms_call(pieces, plan, decoder, carry, everything, offset, n_tgt, total_rows, tokens, after):
    layers, tgt_count, width, columns = decoder.shape
    rows = total_rows // n_tgt
    payload = (payload_rows(layers, rows, width), LANES)
    whole = pl.BlockSpec(memory_space=pltpu.VMEM)
    operands = [*pieces, decoder, *carry]
    carried = sum(x.shape[0] for x in carry)
    aliases = {}
    if everything is not None:
        aliases = {len(operands): 4}
        operands.append(everything)
    operands += after
    return pl.pallas_call(
        functools.partial(terms_kernel, n_tgt, plan, offset, carried),
        in_specs=[ANYWHERE] * len(operands),
        out_specs=[ANYWHERE, whole, whole, whole, ANYWHERE],
        scratch_shapes=[
            pltpu.VMEM((total_rows, tgt_count * columns), jnp.bfloat16),
            pltpu.VMEM((layers, width, tgt_count * columns), jnp.bfloat16),
            pltpu.VMEM((layers, total_rows, width), jnp.float32),
            pltpu.SemaphoreType.DMA((len(plan) * tgt_count,)),
            pltpu.SemaphoreType.DMA((layers * tgt_count,)),
            pltpu.SemaphoreType.DMA((layers,)),
            pltpu.SemaphoreType.DMA,
            pltpu.SemaphoreType.DMA,
        ],
        out_shape=[
            jax.ShapeDtypeStruct((layers, rows, width), jnp.float32),
            jax.ShapeDtypeStruct((carried + payload[0], LANES), jnp.int32),
            jax.ShapeDtypeStruct(payload, jnp.int32),
            jax.ShapeDtypeStruct(payload, jnp.int32),
            jax.ShapeDtypeStruct((tokens, tgt_count * columns), jnp.bfloat16),
        ],
        input_output_aliases=aliases,
        compiler_params=pltpu.CompilerParams(vmem_limit_bytes=VMEM),
        cost_estimate=cost(2 * total_rows * decoder.size, decoder.size * 2),
        name="terms",
    )(*operands)


def finish_kernel(n_got, offset, stride, own_ref, *refs):
    gots = refs[:n_got]
    mask_ref = refs[n_got]
    out_ref, mask_tile, out_tile, in_sem, out_sem = refs[-5:]
    layers, rows, width = out_tile.shape
    parts = mask_ref.shape[1] // stride
    tokens = rows // parts

    def mask_copy(part):
        return pltpu.make_async_copy(
            mask_ref.at[:, pl.ds(part * stride + offset, tokens), :],
            mask_tile.at[:, pl.ds(part * tokens, tokens), :],
            in_sem.at[part],
        )

    def out_copy(layer, part):
        return pltpu.make_async_copy(
            out_tile.at[layer, pl.ds(part * tokens, tokens), :],
            out_ref.at[layer, pl.ds(part * stride + offset, tokens), :],
            out_sem.at[layer * parts + part],
        )

    for part in range(parts):
        mask_copy(part).start()
    steps = [load_steps(got) for got in gots]
    for part in range(parts):
        mask_copy(part).wait()
    for layer in range(layers):
        total = own_ref[layer]
        for got, step in zip(gots, steps):
            total += load_values(got, step, layer, layers, rows, width)
        out_tile[layer] = (total * mask_tile[layer].astype(jnp.float32)).astype(jnp.bfloat16)
        for part in range(parts):
            out_copy(layer, part).start()
    for layer in range(layers):
        for part in range(parts):
            out_copy(layer, part).wait()


def finish_call(own, gots, mask, out, offset, stride, after):
    layers, rows, width = own.shape
    parts = mask.shape[1] // stride
    in_specs = [pl.BlockSpec((layers, rows, width), lambda i: (0, 0, 0))]
    in_specs += [
        pl.BlockSpec((payload_rows(layers, rows, width), LANES), lambda i, place=place: (place, 0)) for _, place in gots
    ]
    in_specs.append(ANYWHERE)
    gots = [got for got, _ in gots]
    operands = [own, *gots, mask]
    aliases = {}
    if out is not None:
        in_specs.append(ANYWHERE)
        aliases = {len(operands): 0}
        operands.append(out)
    in_specs += [ANYWHERE] * len(after)
    operands += after
    return pl.pallas_call(
        functools.partial(finish_kernel, len(gots), offset, stride),
        grid=(1,),
        in_specs=in_specs,
        out_specs=ANYWHERE,
        scratch_shapes=[
            pltpu.VMEM((layers, rows, width), jnp.int32),
            pltpu.VMEM((layers, rows, width), jnp.bfloat16),
            pltpu.SemaphoreType.DMA((parts,)),
            pltpu.SemaphoreType.DMA((layers * parts,)),
        ],
        out_shape=jax.ShapeDtypeStruct(mask.shape, jnp.bfloat16),
        input_output_aliases=aliases,
        compiler_params=pltpu.CompilerParams(vmem_limit_bytes=VMEM),
        cost_estimate=cost(20 * layers * rows * width, layers * rows * width * 16),
        name="finish",
    )(*operands)


def turn_kernel(spans, codes_ref, out_ref):
    tokens = codes_ref.shape[1]
    stride = sum(spans)
    blocks = tokens // stride
    offset = column = 0
    for span in spans:
        rows = jnp.concatenate(
            [codes_ref[0, pl.ds(block * stride + offset, span), :] for block in range(blocks)], axis=0
        )
        out_ref[0, :, pl.ds(column, blocks * span)] = rows.T
        offset += span
        column += blocks * span


def turn_call(codes, spans):
    layers, tokens, width = codes.shape
    return pl.pallas_call(
        functools.partial(turn_kernel, spans),
        grid=(layers,),
        in_specs=[pl.BlockSpec((1, tokens, width), lambda i: (i, 0, 0))],
        out_specs=pl.BlockSpec((1, width, tokens), lambda i: (i, 0, 0)),
        out_shape=jax.ShapeDtypeStruct((layers, width, tokens), jnp.bfloat16),
        compiler_params=pltpu.CompilerParams(vmem_limit_bytes=VMEM),
        cost_estimate=cost(codes.size, codes.size * 4),
        name="turn",
    )(codes)


def grads_kernel(codes_ref, err_ref, *refs):
    out_ref = refs[-1]
    t, layer = pl.program_id(0), pl.program_id(1)
    columns = out_ref.shape[3]
    first_t, first_layer = (lax.axis_index(axis) * pl.num_programs(i) for i, axis in enumerate(("tgt", "src")))
    kept = first_t + t >= first_layer + layer
    step = min(columns, 512)

    @pl.when(kept)
    def _():
        for column in range(0, columns, step):
            out_ref[0, 0, :, column : column + step] = jnp.dot(
                codes_ref[0], err_ref[:, column : column + step], preferred_element_type=jnp.float32
            ).astype(jnp.bfloat16)

    @pl.when(jnp.logical_not(kept))
    def _():
        out_ref[...] = jnp.zeros_like(out_ref)


def grads_call(codes_t, everything, shape, after):
    layers, tgt_count, width, columns = shape
    tokens = codes_t.shape[2]
    in_specs = [
        pl.BlockSpec((1, width, tokens), lambda t, i: (i, 0, 0)),
        pl.BlockSpec((tokens, columns), lambda t, i: (0, t)),
    ]
    return pl.pallas_call(
        grads_kernel,
        grid=(tgt_count, layers),
        in_specs=in_specs + [ANYWHERE] * len(after),
        out_specs=pl.BlockSpec((1, 1, width, columns), lambda t, i: (i, t, 0, 0)),
        out_shape=jax.ShapeDtypeStruct(shape, jnp.bfloat16),
        compiler_params=pltpu.CompilerParams(vmem_limit_bytes=VMEM),
        cost_estimate=cost(
            2 * tgt_count * layers * width * columns * tokens, 2 * tgt_count * layers * width * (columns + tokens)
        ),
        name="grads",
    )(codes_t, everything, *after)


def gather_pieces(errors, spans, offsets, n_src, n_feat, codes_t):
    if (n_src, n_feat) != (2, 4):
        for offset, span in zip(offsets, spans):
            part = lax.slice_in_dim(errors, offset, offset + span, axis=1)
            columns = lax.all_gather(part, "src", axis=2, tiled=True)
            piece = lax.all_gather(columns, "feat", axis=1, tiled=True)
            yield [piece], [(0, None, 0, n_feat * span, None, None)]
        return
    axes = ("src", "feat")
    to = lambda x, flip: lax.ppermute(x, axes, [(i, i ^ flip) for i in range(n_src * n_feat)])
    core_own = over_core(errors, n_feat)
    (part,) = cut_call(errors, 0, spans[0], [], [])
    after = [core_own, codes_t]
    for index, (offset, span) in enumerate(zip(offsets, spans)):
        arrived = [to(part, n_feat), to(part, 2), to(part, n_feat + 2)]
        more = index + 1 < len(spans)
        joined, *rest = cut_call(
            errors, offsets[index + 1] if more else None, spans[index + 1] if more else None, arrived, after
        )
        part = rest[0] if more else None
        plan = [(core, None, offset, span, 0, core) for core in (0, 1)]
        for lead, (dx, dy) in enumerate(((1, 0), (0, 2), (1, 2))):
            plan += [(2 + core, lead, 0, span, dx, dy ^ core) for core in (0, 1)]
        after = yield [errors, core_own, joined, over_core(joined, n_feat)], plan


def over_core(x, n_feat):
    return lax.ppermute(x, "feat", [(i, i ^ 1) for i in range(n_feat)])


def body(n_src, n_tgt, n_feat, errors, saved_codes, active_mask, decoder):
    tgt_count = decoder.shape[1]
    stride = errors.shape[1]
    spans = [stride * part // 8 for part in EIGHTHS]
    offsets = [sum(spans[:index]) for index in range(len(spans))]
    codes_t = turn_call(saved_codes, spans)
    gather = gather_pieces(errors, spans, offsets, n_src, n_feat, codes_t)
    pieces, plan = next(gather)
    last = len(spans) - 1
    join_near = last > 0 and spans[-1] == spans[-2]
    owns, gots = [], []
    carry, everything = [], None
    send = lambda x, flip: lax.ppermute(x, "tgt", [(i, i ^ flip) for i in range(n_tgt)])
    for index, span in enumerate(spans):
        own, near, across, far, everything = terms_call(
            pieces,
            plan,
            decoder,
            carry,
            everything,
            n_feat * offsets[index],
            n_tgt,
            n_feat * span,
            n_feat * stride,
            [],
        )
        owns.append(own)
        gots.append([(send(far, 3), 0), (send(across, 2), 0)])
        if join_near and index == last - 1:
            carry = [near]
        else:
            got_near = send(near, 1)
            if join_near and index == last:
                gots[last - 1].append((got_near, 0))
            gots[index].append((got_near, len(carry)))
        if index < last:
            before = [gots[0][2]] if index == 0 else gots[index - 1][:2]
            pieces, plan = gather.send([own] + [got for got, _ in before])
    decoder_grads = grads_call(codes_t, everything, decoder.shape, [])
    code_grads = None
    for index in range(len(spans)):
        after = [] if index else [decoder_grads] + [got for group in gots[1:last] for got, _ in group[:2]]
        code_grads = finish_call(owns[index], gots[index], active_mask, code_grads, offsets[index], stride, after)
    return code_grads, decoder_grads


def plain_body(errors, saved_codes, active_mask, decoder):
    src_count, tgt_count, feat_count, _ = decoder.shape
    src_ids = lax.axis_index("src") * src_count + jnp.arange(src_count, dtype=jnp.int32)
    tgt_ids = lax.axis_index("tgt") * tgt_count + jnp.arange(tgt_count, dtype=jnp.int32)
    kept = (tgt_ids[None, :] >= src_ids[:, None])[:, :, None, None]
    columns = lax.all_gather(errors, "src", axis=2, tiled=True)
    portion = lax.all_gather(columns, "feat", axis=1, tiled=True)
    grads = jnp.einsum("itf,jtd->ijfd", saved_codes, portion, preferred_element_type=jnp.float32)
    decoder = jnp.where(kept, decoder, jnp.zeros_like(decoder))
    term = jnp.einsum("jtd,ijfd->itf", portion, decoder, preferred_element_type=jnp.float32)
    summed = lax.psum_scatter(term, "tgt", scatter_dimension=1, tiled=True)
    code_grads = (summed * active_mask.astype(jnp.float32)).astype(jnp.bfloat16)
    return code_grads, jnp.where(kept, grads, 0.0).astype(jnp.bfloat16)


def solution(mesh):
    sizes = [mesh.shape[axis] for axis in ("src", "tgt", "feat")]
    fits = sizes[1] == 4 and sizes[2] % sizes[1] == 0
    in_specs = (
        P("tgt", "feat", "src"),
        P("src", None, "feat"),
        P("src", "tgt", "feat"),
        P("src", "tgt", "feat", None),
    )
    out_specs = (P("src", "tgt", "feat"), P("src", "tgt", "feat", None))
    return jax.shard_map(
        functools.partial(body, *sizes) if fits else plain_body,
        mesh=mesh,
        in_specs=in_specs,
        out_specs=out_specs,
        check_vma=False,
    )
```

```python
import functools

import jax
import jax.numpy as jnp
from jax import lax
from jax.experimental import pallas as pl
from jax.experimental.pallas import tpu as pltpu
from jax.sharding import PartitionSpec as P

LANES = 128
SUBLANES = 8
STEPS_PER_OCTAVE = 64
TOP = 32760.0
FLOOR = 1e-30
EIGHTHS = (3, 3, 2)
VMEM = 127 << 19
EASE = 2
ANYWHERE = pl.BlockSpec(memory_space=pl.ANY)


def pair(x):
    half = x.shape[0] // 2
    return (x[half:] << 16) | (x[:half] & 0xFFFF)


def unpair(words):
    return (words << 16) >> 16, words >> 16


def scale_and_gain(peaks):
    scale = jnp.ceil(jnp.log2(jnp.maximum(peaks, FLOOR)) * STEPS_PER_OCTAVE)
    return scale.astype(jnp.int32), jnp.exp2(scale * (-1.0 / STEPS_PER_OCTAVE)) * TOP


def row_peak(v):
    return jnp.max(jnp.abs(v), axis=1, keepdims=True)


def store_words(out_ref, layer, v, gain, base=0):
    rows, width = v.shape
    half, tiles = rows // 2, width // LANES
    words = pair(jnp.floor(v * gain + 0.5).astype(jnp.int32))
    for tile in range(tiles):
        start = base + (layer * tiles + tile) * half
        out_ref[start : start + half, :] = words[:, tile * LANES : (tile + 1) * LANES]


def lanes_of(shape):
    return lax.broadcasted_iota(jnp.int32, shape, 1)


def load_steps(in_ref):
    end = in_ref.shape[0] - SUBLANES
    low, high = unpair(in_ref[end:, :])
    step = lambda scale: jnp.exp2(scale.astype(jnp.float32) * (1.0 / STEPS_PER_OCTAVE)) * (1.0 / TOP)
    return step(low), step(high)


def load_values(in_ref, steps, layer, layers, rows, width):
    half, tiles = rows // 2, width // LANES
    words = jnp.concatenate(
        [in_ref[(layer * tiles + tile) * half : (layer * tiles + tile + 1) * half, :] for tile in range(tiles)], axis=1
    )
    values = []
    for part, step in zip(unpair(words), steps):
        column = jnp.concatenate(
            [step[:, group * layers + layer][:, None] for group in range(half // SUBLANES)], axis=0
        )
        values.append(part.astype(jnp.float32) * column)
    return jnp.concatenate(values, axis=0)


def payload_rows(layers, rows, width):
    return layers * (width // LANES) * (rows // 2) + SUBLANES


def cost(flops, bytes_accessed):
    return pl.CostEstimate(flops=flops // EASE, bytes_accessed=bytes_accessed // EASE, transcendentals=0)


def cut_kernel(n_join, offset, errors_ref, *refs):
    sem = refs[-1]
    joined = refs[:n_join]
    outs = refs[-1 - (n_join > 0) - (offset is not None) : -1]
    copies = [(piece, outs[0].at[index]) for index, piece in enumerate(joined)]
    if offset is not None:
        copies.append((errors_ref.at[:, pl.ds(offset, outs[-1].shape[1]), :], outs[-1]))
    copies = [pltpu.make_async_copy(*copy, sem.at[index]) for index, copy in enumerate(copies)]
    for copy in copies:
        copy.start()
    for copy in copies:
        copy.wait()


def cut_call(errors, offset, span, join, after):
    shapes = []
    if join:
        shapes.append(jax.ShapeDtypeStruct((len(join), *join[0].shape), errors.dtype))
    if offset is not None:
        shapes.append(jax.ShapeDtypeStruct((errors.shape[0], span, errors.shape[2]), errors.dtype))
    return pl.pallas_call(
        functools.partial(cut_kernel, len(join), offset),
        in_specs=[ANYWHERE] * (1 + len(join) + len(after)),
        out_specs=[pl.BlockSpec(memory_space=pltpu.VMEM)] * len(shapes),
        out_shape=shapes,
        scratch_shapes=[pltpu.SemaphoreType.DMA((len(join) + 1,))],
        compiler_params=pltpu.CompilerParams(vmem_limit_bytes=VMEM),
        cost_estimate=cost(0, 4 * sum(shape.size for shape in shapes)),
        name="cut",
    )(errors, *join, *after)


def terms_kernel(n_tgt, plan, offset, carried, *refs):
    n_pieces = 1 + max(entry[0] for entry in plan)
    pieces = refs[:n_pieces]
    dec_ref = refs[n_pieces]
    own_ref, near_ref, across_ref, far_ref, all_ref, err, dec, acc, in_sem, dec_sem, own_sem, out_sem, carry_sem = refs[-13:]
    layers, tgt_count, width, columns = dec_ref.shape
    total_rows = err.shape[0]
    rows = total_rows // n_tgt
    half = rows // 2
    src, tgt, feat = (lax.axis_index(axis) for axis in ("src", "tgt", "feat"))

    def piece_copies(index):
        source, lead, skip, tokens, flip_src, flip_feat = plan[index]
        piece = pieces[source] if lead is None else pieces[source].at[lead]
        wide = piece.shape[2]
        row = 0 if flip_feat is None else pl.multiple_of((feat ^ flip_feat) * tokens, tokens)
        column = 0 if flip_src is None else pl.multiple_of((src ^ flip_src) * wide, wide)
        return [
            pltpu.make_async_copy(
                piece.at[t, pl.ds(skip, tokens), :],
                err.at[pl.ds(row, tokens), pl.ds(t * columns + column, wide)],
                in_sem.at[index * tgt_count + t],
            )
            for t in range(tgt_count)
        ]

    def dec_copy(layer, t):
        return pltpu.make_async_copy(
            dec_ref.at[layer, t], dec.at[layer, :, pl.ds(t * columns, columns)], dec_sem.at[layer * tgt_count + t]
        )

    def block(dest):
        return pl.ds(pl.multiple_of(dest * rows, rows), rows)

    def own_copy(layer):
        return pltpu.make_async_copy(acc.at[layer, block(tgt), :], own_ref.at[layer], own_sem.at[layer])

    carry = pltpu.make_async_copy(refs[n_pieces + 1], near_ref.at[pl.ds(0, carried), :], carry_sem) if carried else None
    out_copy = pltpu.make_async_copy(err, all_ref.at[pl.ds(offset, total_rows), :], out_sem)

    for t in range(tgt_count):
        dec_copy(0, t).start()
    copies = [copy for index in range(len(plan)) for copy in piece_copies(index)]
    for copy in copies:
        copy.start()
    if carried:
        carry.start()
    for layer in range(1, layers):
        for t in range(tgt_count):
            dec_copy(layer, t).start()
    for copy in copies:
        copy.wait()
    out_copy.start()

    lane = lanes_of((rows, LANES))
    small = lanes_of((SUBLANES, LANES))
    flips = {1: near_ref, 2: across_ref, 3: far_ref}
    tails = [jnp.zeros((SUBLANES, LANES), jnp.int32) for _ in flips]

    def multiply(layer):
        for t in range(tgt_count):
            dec_copy(layer, t).wait()
            kept = tgt * tgt_count + t >= src * layers + layer

            @pl.when(jnp.logical_not(kept))
            def _():
                dec[layer, :, t * columns : (t + 1) * columns] = jnp.zeros((width, columns), jnp.bfloat16)

        acc[layer] = lax.dot_general(
            err[...], dec[layer], (((1,), (1,)), ((), ())), preferred_element_type=jnp.float32
        )
        own_copy(layer).start()

    def encode(layer):
        peaks = jnp.zeros((rows, LANES), jnp.float32)
        for index, flip in enumerate(flips):
            peaks = jnp.where(lane == index, row_peak(acc[layer, block(tgt ^ flip), :]), peaks)
        scale, gain = scale_and_gain(peaks)
        scale_words = pair(scale)
        for index, flip in enumerate(flips):
            v, factor = acc[layer, block(tgt ^ flip), :], gain[:, index : index + 1]
            store_words(flips[flip], layer, v, factor, carried if flip == 1 else 0)
            for group in range(half // SUBLANES):
                piece = scale_words[group * SUBLANES : (group + 1) * SUBLANES, index : index + 1]
                tails[index] = jnp.where(small == group * layers + layer, piece, tails[index])

    for layer in range(layers):
        multiply(layer)
        if layer:
            encode(layer - 1)
    encode(layers - 1)
    for send, tail in zip(flips.values(), tails):
        send[send.shape[0] - SUBLANES :, :] = tail
    for layer in range(layers):
        own_copy(layer).wait()
    out_copy.wait()
    if carried:
        carry.wait()


def terms_call(pieces, plan, decoder, carry, everything, offset, n_tgt, total_rows, tokens, after):
    layers, tgt_count, width, columns = decoder.shape
    rows = total_rows // n_tgt
    payload = (payload_rows(layers, rows, width), LANES)
    whole = pl.BlockSpec(memory_space=pltpu.VMEM)
    operands = [*pieces, decoder, *carry]
    carried = sum(x.shape[0] for x in carry)
    aliases = {}
    if everything is not None:
        aliases = {len(operands): 4}
        operands.append(everything)
    operands += after
    return pl.pallas_call(
        functools.partial(terms_kernel, n_tgt, plan, offset, carried),
        in_specs=[ANYWHERE] * len(operands),
        out_specs=[ANYWHERE, whole, whole, whole, ANYWHERE],
        scratch_shapes=[
            pltpu.VMEM((total_rows, tgt_count * columns), jnp.bfloat16),
            pltpu.VMEM((layers, width, tgt_count * columns), jnp.bfloat16),
            pltpu.VMEM((layers, total_rows, width), jnp.float32),
            pltpu.SemaphoreType.DMA((len(plan) * tgt_count,)),
            pltpu.SemaphoreType.DMA((layers * tgt_count,)),
            pltpu.SemaphoreType.DMA((layers,)),
            pltpu.SemaphoreType.DMA,
            pltpu.SemaphoreType.DMA,
        ],
        out_shape=[
            jax.ShapeDtypeStruct((layers, rows, width), jnp.float32),
            jax.ShapeDtypeStruct((carried + payload[0], LANES), jnp.int32),
            jax.ShapeDtypeStruct(payload, jnp.int32),
            jax.ShapeDtypeStruct(payload, jnp.int32),
            jax.ShapeDtypeStruct((tokens, tgt_count * columns), jnp.bfloat16),
        ],
        input_output_aliases=aliases,
        compiler_params=pltpu.CompilerParams(vmem_limit_bytes=VMEM),
        cost_estimate=cost(2 * total_rows * decoder.size, decoder.size * 2),
        name="terms",
    )(*operands)


def finish_kernel(n_got, offset, stride, own_ref, *refs):
    gots = refs[:n_got]
    mask_ref = refs[n_got]
    out_ref, mask_tile, out_tile, in_sem, out_sem = refs[-5:]
    layers, rows, width = out_tile.shape
    parts = mask_ref.shape[1] // stride
    tokens = rows // parts

    def mask_copy(part):
        return pltpu.make_async_copy(
            mask_ref.at[:, pl.ds(part * stride + offset, tokens), :],
            mask_tile.at[:, pl.ds(part * tokens, tokens), :],
            in_sem.at[part],
        )

    def out_copy(layer, part):
        return pltpu.make_async_copy(
            out_tile.at[layer, pl.ds(part * tokens, tokens), :],
            out_ref.at[layer, pl.ds(part * stride + offset, tokens), :],
            out_sem.at[layer * parts + part],
        )

    for part in range(parts):
        mask_copy(part).start()
    steps = [load_steps(got) for got in gots]
    for part in range(parts):
        mask_copy(part).wait()
    for layer in range(layers):
        total = own_ref[layer]
        for got, step in zip(gots, steps):
            total += load_values(got, step, layer, layers, rows, width)
        out_tile[layer] = (total * mask_tile[layer].astype(jnp.float32)).astype(jnp.bfloat16)
        for part in range(parts):
            out_copy(layer, part).start()
    for layer in range(layers):
        for part in range(parts):
            out_copy(layer, part).wait()


def finish_call(own, gots, mask, out, offset, stride, after):
    layers, rows, width = own.shape
    parts = mask.shape[1] // stride
    in_specs = [pl.BlockSpec((layers, rows, width), lambda i: (0, 0, 0))]
    in_specs += [
        pl.BlockSpec((payload_rows(layers, rows, width), LANES), lambda i, place=place: (place, 0)) for _, place in gots
    ]
    in_specs.append(ANYWHERE)
    gots = [got for got, _ in gots]
    operands = [own, *gots, mask]
    aliases = {}
    if out is not None:
        in_specs.append(ANYWHERE)
        aliases = {len(operands): 0}
        operands.append(out)
    in_specs += [ANYWHERE] * len(after)
    operands += after
    return pl.pallas_call(
        functools.partial(finish_kernel, len(gots), offset, stride),
        grid=(1,),
        in_specs=in_specs,
        out_specs=ANYWHERE,
        scratch_shapes=[
            pltpu.VMEM((layers, rows, width), jnp.int32),
            pltpu.VMEM((layers, rows, width), jnp.bfloat16),
            pltpu.SemaphoreType.DMA((parts,)),
            pltpu.SemaphoreType.DMA((layers * parts,)),
        ],
        out_shape=jax.ShapeDtypeStruct(mask.shape, jnp.bfloat16),
        input_output_aliases=aliases,
        compiler_params=pltpu.CompilerParams(vmem_limit_bytes=VMEM),
        cost_estimate=cost(20 * layers * rows * width, layers * rows * width * 16),
        name="finish",
    )(*operands)


def turn_kernel(spans, codes_ref, out_ref):
    tokens = codes_ref.shape[1]
    stride = sum(spans)
    blocks = tokens // stride
    offset = column = 0
    for span in spans:
        rows = jnp.concatenate(
            [codes_ref[0, pl.ds(block * stride + offset, span), :] for block in range(blocks)], axis=0
        )
        out_ref[0, :, pl.ds(column, blocks * span)] = rows.T
        offset += span
        column += blocks * span


def turn_call(codes, spans):
    layers, tokens, width = codes.shape
    return pl.pallas_call(
        functools.partial(turn_kernel, spans),
        grid=(layers,),
        in_specs=[pl.BlockSpec((1, tokens, width), lambda i: (i, 0, 0))],
        out_specs=pl.BlockSpec((1, width, tokens), lambda i: (i, 0, 0)),
        out_shape=jax.ShapeDtypeStruct((layers, width, tokens), jnp.bfloat16),
        compiler_params=pltpu.CompilerParams(vmem_limit_bytes=VMEM),
        cost_estimate=cost(codes.size, codes.size * 4),
        name="turn",
    )(codes)


def grads_kernel(t, tgt_count, codes_ref, err_ref, *refs):
    out_ref = refs[-1]
    layer = lax.axis_index("src") * pl.num_programs(0) + pl.program_id(0)
    kept = lax.axis_index("tgt") * tgt_count + t >= layer
    columns = out_ref.shape[3]
    step = min(columns, 512)

    @pl.when(kept)
    def _():
        for column in range(0, columns, step):
            out_ref[0, 0, :, column : column + step] = jnp.dot(
                codes_ref[0], err_ref[:, column : column + step], preferred_element_type=jnp.float32
            ).astype(jnp.bfloat16)

    @pl.when(jnp.logical_not(kept))
    def _():
        out_ref[...] = jnp.zeros_like(out_ref)


def grads_call(t, codes_t, everything, out, shape, after):
    layers, tgt_count, width, columns = shape
    tokens = codes_t.shape[2]
    in_specs = [
        pl.BlockSpec((1, width, tokens), lambda i: (i, 0, 0)),
        pl.BlockSpec((tokens, columns), lambda i: (0, t)),
    ]
    operands = [codes_t, everything]
    aliases = {}
    if out is not None:
        aliases = {len(operands): 0}
        operands.append(out)
    operands += after
    in_specs += [ANYWHERE] * (len(operands) - 2)
    return pl.pallas_call(
        functools.partial(grads_kernel, t, tgt_count),
        grid=(layers,),
        in_specs=in_specs,
        out_specs=pl.BlockSpec((1, 1, width, columns), lambda i: (i, t, 0, 0)),
        out_shape=jax.ShapeDtypeStruct(shape, jnp.bfloat16),
        input_output_aliases=aliases,
        compiler_params=pltpu.CompilerParams(vmem_limit_bytes=VMEM),
        cost_estimate=cost(
            2 * layers * width * columns * tokens, 2 * layers * width * (columns + tokens) + 2 * tokens * columns
        ),
        name="grads",
    )(*operands)


def gather_pieces(errors, spans, offsets, n_src, n_feat, codes_t):
    if (n_src, n_feat) != (2, 4):
        for offset, span in zip(offsets, spans):
            part = lax.slice_in_dim(errors, offset, offset + span, axis=1)
            columns = lax.all_gather(part, "src", axis=2, tiled=True)
            piece = lax.all_gather(columns, "feat", axis=1, tiled=True)
            yield [piece], [(0, None, 0, n_feat * span, None, None)]
        return
    axes = ("src", "feat")
    to = lambda x, flip: lax.ppermute(x, axes, [(i, i ^ flip) for i in range(n_src * n_feat)])
    core_own = over_core(errors, n_feat)
    (part,) = cut_call(errors, 0, spans[0], [], [])
    after = [core_own, codes_t]
    for index, (offset, span) in enumerate(zip(offsets, spans)):
        arrived = [to(part, n_feat), to(part, 2), to(part, n_feat + 2)]
        more = index + 1 < len(spans)
        joined, *rest = cut_call(
            errors, offsets[index + 1] if more else None, spans[index + 1] if more else None, arrived, after
        )
        part = rest[0] if more else None
        plan = [(core, None, offset, span, 0, core) for core in (0, 1)]
        for lead, (dx, dy) in enumerate(((1, 0), (0, 2), (1, 2))):
            plan += [(2 + core, lead, 0, span, dx, dy ^ core) for core in (0, 1)]
        after = yield [errors, core_own, joined, over_core(joined, n_feat)], plan


def over_core(x, n_feat):
    return lax.ppermute(x, "feat", [(i, i ^ 1) for i in range(n_feat)])


def body(n_src, n_tgt, n_feat, errors, saved_codes, active_mask, decoder):
    tgt_count = decoder.shape[1]
    stride = errors.shape[1]
    spans = [stride * part // 8 for part in EIGHTHS]
    offsets = [sum(spans[:index]) for index in range(len(spans))]
    codes_t = turn_call(saved_codes, spans)
    gather = gather_pieces(errors, spans, offsets, n_src, n_feat, codes_t)
    pieces, plan = next(gather)
    last = len(spans) - 1
    join_near = last > 0 and spans[0] == spans[1]
    owns, gots = [], []
    carry, everything = [], None
    send = lambda x, flip: lax.ppermute(x, "tgt", [(i, i ^ flip) for i in range(n_tgt)])
    for index, span in enumerate(spans):
        own, near, across, far, everything = terms_call(
            pieces,
            plan,
            decoder,
            carry,
            everything,
            n_feat * offsets[index],
            n_tgt,
            n_feat * span,
            n_feat * stride,
            [],
        )
        owns.append(own)
        gots.append([(send(far, 3), 0), (send(across, 2), 0)])
        if join_near and index == 0:
            carry = [near]
        else:
            got_near = send(near, 1)
            if carry:
                gots[0].append((got_near, 0))
            gots[index].append((got_near, len(carry)))
            carry = []
        if index < last:
            before = gots[index - 1][:2] if index else []
            pieces, plan = gather.send([own] + [got for got, _ in before])
    decoder_grads = None
    for t in range(tgt_count):
        after = [gots[0][2][0]] if t else []
        decoder_grads = grads_call(t, codes_t, everything, decoder_grads, decoder.shape, after)
    code_grads = None
    for index in range(len(spans)):
        after = [] if index else [decoder_grads] + [got for group in gots[1:last] for got, _ in group[:2]]
        code_grads = finish_call(owns[index], gots[index], active_mask, code_grads, offsets[index], stride, after)
    return code_grads, decoder_grads


def plain_body(errors, saved_codes, active_mask, decoder):
    src_count, tgt_count, feat_count, _ = decoder.shape
    src_ids = lax.axis_index("src") * src_count + jnp.arange(src_count, dtype=jnp.int32)
    tgt_ids = lax.axis_index("tgt") * tgt_count + jnp.arange(tgt_count, dtype=jnp.int32)
    kept = (tgt_ids[None, :] >= src_ids[:, None])[:, :, None, None]
    columns = lax.all_gather(errors, "src", axis=2, tiled=True)
    portion = lax.all_gather(columns, "feat", axis=1, tiled=True)
    grads = jnp.einsum("itf,jtd->ijfd", saved_codes, portion, preferred_element_type=jnp.float32)
    decoder = jnp.where(kept, decoder, jnp.zeros_like(decoder))
    term = jnp.einsum("jtd,ijfd->itf", portion, decoder, preferred_element_type=jnp.float32)
    summed = lax.psum_scatter(term, "tgt", scatter_dimension=1, tiled=True)
    code_grads = (summed * active_mask.astype(jnp.float32)).astype(jnp.bfloat16)
    return code_grads, jnp.where(kept, grads, 0.0).astype(jnp.bfloat16)


def solution(mesh):
    sizes = [mesh.shape[axis] for axis in ("src", "tgt", "feat")]
    fits = sizes[1] == 4 and sizes[2] % sizes[1] == 0
    in_specs = (
        P("tgt", "feat", "src"),
        P("src", None, "feat"),
        P("src", "tgt", "feat"),
        P("src", "tgt", "feat", None),
    )
    out_specs = (P("src", "tgt", "feat"), P("src", "tgt", "feat", None))
    return jax.shard_map(
        functools.partial(body, *sizes) if fits else plain_body,
        mesh=mesh,
        in_specs=in_specs,
        out_specs=out_specs,
        check_vma=False,
    )
```

```python
import functools

import jax
import jax.numpy as jnp
from jax import lax
from jax.experimental import pallas as pl
from jax.experimental.pallas import tpu as pltpu
from jax.sharding import PartitionSpec as P

LANES = 128
SUBLANES = 8
STEPS_PER_OCTAVE = 64
TOP = 32760.0
FLOOR = 1e-30
EIGHTHS = (2, 3, 3)
VMEM = 127 << 19
EASE = 2
ANYWHERE = pl.BlockSpec(memory_space=pl.ANY)


def pair(x):
    half = x.shape[0] // 2
    return (x[half:] << 16) | (x[:half] & 0xFFFF)


def unpair(words):
    return (words << 16) >> 16, words >> 16


def scale_and_gain(peaks):
    scale = jnp.ceil(jnp.log2(jnp.maximum(peaks, FLOOR)) * STEPS_PER_OCTAVE)
    return scale.astype(jnp.int32), jnp.exp2(scale * (-1.0 / STEPS_PER_OCTAVE)) * TOP


def row_peak(v):
    return jnp.max(jnp.abs(v), axis=1, keepdims=True)


def store_words(out_ref, layer, v, gain, base=0):
    rows, width = v.shape
    half, tiles = rows // 2, width // LANES
    words = pair(jnp.floor(v * gain + 0.5).astype(jnp.int32))
    for tile in range(tiles):
        start = base + (layer * tiles + tile) * half
        out_ref[start : start + half, :] = words[:, tile * LANES : (tile + 1) * LANES]


def lanes_of(shape):
    return lax.broadcasted_iota(jnp.int32, shape, 1)


def load_steps(in_ref):
    end = in_ref.shape[0] - SUBLANES
    low, high = unpair(in_ref[end:, :])
    step = lambda scale: jnp.exp2(scale.astype(jnp.float32) * (1.0 / STEPS_PER_OCTAVE)) * (1.0 / TOP)
    return step(low), step(high)


def load_values(in_ref, steps, layer, layers, rows, width):
    half, tiles = rows // 2, width // LANES
    words = jnp.concatenate(
        [in_ref[(layer * tiles + tile) * half : (layer * tiles + tile + 1) * half, :] for tile in range(tiles)], axis=1
    )
    values = []
    for part, step in zip(unpair(words), steps):
        column = jnp.concatenate(
            [step[:, group * layers + layer][:, None] for group in range(half // SUBLANES)], axis=0
        )
        values.append(part.astype(jnp.float32) * column)
    return jnp.concatenate(values, axis=0)


def payload_rows(layers, rows, width):
    return layers * (width // LANES) * (rows // 2) + SUBLANES


def cost(flops, bytes_accessed):
    return pl.CostEstimate(flops=flops // EASE, bytes_accessed=bytes_accessed // EASE, transcendentals=0)


def cut_kernel(n_join, offset, errors_ref, *refs):
    sem = refs[-1]
    joined = refs[:n_join]
    outs = refs[-1 - (n_join > 0) - (offset is not None) : -1]
    copies = [(piece, outs[0].at[index]) for index, piece in enumerate(joined)]
    if offset is not None:
        copies.append((errors_ref.at[:, pl.ds(offset, outs[-1].shape[1]), :], outs[-1]))
    copies = [pltpu.make_async_copy(*copy, sem.at[index]) for index, copy in enumerate(copies)]
    for copy in copies:
        copy.start()
    for copy in copies:
        copy.wait()


def cut_call(errors, offset, span, join, after):
    shapes = []
    if join:
        shapes.append(jax.ShapeDtypeStruct((len(join), *join[0].shape), errors.dtype))
    if offset is not None:
        shapes.append(jax.ShapeDtypeStruct((errors.shape[0], span, errors.shape[2]), errors.dtype))
    return pl.pallas_call(
        functools.partial(cut_kernel, len(join), offset),
        in_specs=[ANYWHERE] * (1 + len(join) + len(after)),
        out_specs=[pl.BlockSpec(memory_space=pltpu.VMEM)] * len(shapes),
        out_shape=shapes,
        scratch_shapes=[pltpu.SemaphoreType.DMA((len(join) + 1,))],
        compiler_params=pltpu.CompilerParams(vmem_limit_bytes=VMEM),
        cost_estimate=cost(0, 4 * sum(shape.size for shape in shapes)),
        name="cut",
    )(errors, *join, *after)


def terms_kernel(n_tgt, plan, offset, carried, *refs):
    n_pieces = 1 + max(entry[0] for entry in plan)
    pieces = refs[:n_pieces]
    dec_ref = refs[n_pieces]
    own_ref, near_ref, across_ref, far_ref, all_ref, err, dec, acc, in_sem, dec_sem, own_sem, out_sem, carry_sem = refs[-13:]
    layers, tgt_count, width, columns = dec_ref.shape
    total_rows = err.shape[0]
    rows = total_rows // n_tgt
    half = rows // 2
    src, tgt, feat = (lax.axis_index(axis) for axis in ("src", "tgt", "feat"))

    def piece_copies(index):
        source, lead, skip, tokens, flip_src, flip_feat = plan[index]
        piece = pieces[source] if lead is None else pieces[source].at[lead]
        wide = piece.shape[2]
        row = 0 if flip_feat is None else pl.multiple_of((feat ^ flip_feat) * tokens, tokens)
        column = 0 if flip_src is None else pl.multiple_of((src ^ flip_src) * wide, wide)
        return [
            pltpu.make_async_copy(
                piece.at[t, pl.ds(skip, tokens), :],
                err.at[pl.ds(row, tokens), pl.ds(t * columns + column, wide)],
                in_sem.at[index * tgt_count + t],
            )
            for t in range(tgt_count)
        ]

    def dec_copy(layer, t):
        return pltpu.make_async_copy(
            dec_ref.at[layer, t], dec.at[layer, :, pl.ds(t * columns, columns)], dec_sem.at[layer * tgt_count + t]
        )

    def block(dest):
        return pl.ds(pl.multiple_of(dest * rows, rows), rows)

    def own_copy(layer):
        return pltpu.make_async_copy(acc.at[layer, block(tgt), :], own_ref.at[layer], own_sem.at[layer])

    if carried:
        early_ref = refs[n_pieces + 1]
        carry = pltpu.make_async_copy(early_ref, near_ref.at[pl.ds(0, early_ref.shape[0]), :], carry_sem)
    out_copy = pltpu.make_async_copy(err, all_ref.at[pl.ds(offset, total_rows), :], out_sem)

    for t in range(tgt_count):
        dec_copy(0, t).start()
    copies = [copy for index in range(len(plan)) for copy in piece_copies(index)]
    for copy in copies:
        copy.start()
    if carried:
        carry.start()
    for layer in range(1, layers):
        for t in range(tgt_count):
            dec_copy(layer, t).start()
    for copy in copies:
        copy.wait()
    out_copy.start()

    lane = lanes_of((rows, LANES))
    small = lanes_of((SUBLANES, LANES))
    flips = {1: near_ref, 2: across_ref, 3: far_ref}
    tails = [jnp.zeros((SUBLANES, LANES), jnp.int32) for _ in flips]

    def multiply(layer):
        for t in range(tgt_count):
            dec_copy(layer, t).wait()
            kept = tgt * tgt_count + t >= src * layers + layer

            @pl.when(jnp.logical_not(kept))
            def _():
                dec[layer, :, t * columns : (t + 1) * columns] = jnp.zeros((width, columns), jnp.bfloat16)

        acc[layer] = lax.dot_general(
            err[...], dec[layer], (((1,), (1,)), ((), ())), preferred_element_type=jnp.float32
        )
        own_copy(layer).start()

    def encode(layer):
        peaks = jnp.zeros((rows, LANES), jnp.float32)
        for index, flip in enumerate(flips):
            peaks = jnp.where(lane == index, row_peak(acc[layer, block(tgt ^ flip), :]), peaks)
        scale, gain = scale_and_gain(peaks)
        scale_words = pair(scale)
        for index, flip in enumerate(flips):
            v, factor = acc[layer, block(tgt ^ flip), :], gain[:, index : index + 1]
            store_words(flips[flip], layer, v, factor, carried if flip == 1 else 0)
            for group in range(half // SUBLANES):
                piece = scale_words[group * SUBLANES : (group + 1) * SUBLANES, index : index + 1]
                tails[index] = jnp.where(small == group * layers + layer, piece, tails[index])

    for layer in range(layers):
        multiply(layer)
        if layer:
            encode(layer - 1)
    encode(layers - 1)
    for send, tail in zip(flips.values(), tails):
        send[send.shape[0] - SUBLANES :, :] = tail
    for layer in range(layers):
        own_copy(layer).wait()
    out_copy.wait()
    if carried:
        carry.wait()


def terms_call(pieces, plan, decoder, carry, everything, offset, n_tgt, total_rows, tokens, after):
    layers, tgt_count, width, columns = decoder.shape
    rows = total_rows // n_tgt
    payload = (payload_rows(layers, rows, width), LANES)
    whole = pl.BlockSpec(memory_space=pltpu.VMEM)
    operands = [*pieces, decoder, *carry]
    carried = payload[0] if carry else 0
    aliases = {}
    if everything is not None:
        aliases = {len(operands): 4}
        operands.append(everything)
    operands += after
    return pl.pallas_call(
        functools.partial(terms_kernel, n_tgt, plan, offset, carried),
        in_specs=[ANYWHERE] * len(operands),
        out_specs=[ANYWHERE, whole, whole, whole, ANYWHERE],
        scratch_shapes=[
            pltpu.VMEM((total_rows, tgt_count * columns), jnp.bfloat16),
            pltpu.VMEM((layers, width, tgt_count * columns), jnp.bfloat16),
            pltpu.VMEM((layers, total_rows, width), jnp.float32),
            pltpu.SemaphoreType.DMA((len(plan) * tgt_count,)),
            pltpu.SemaphoreType.DMA((layers * tgt_count,)),
            pltpu.SemaphoreType.DMA((layers,)),
            pltpu.SemaphoreType.DMA,
            pltpu.SemaphoreType.DMA,
        ],
        out_shape=[
            jax.ShapeDtypeStruct((layers, rows, width), jnp.float32),
            jax.ShapeDtypeStruct((carried + payload[0], LANES), jnp.int32),
            jax.ShapeDtypeStruct(payload, jnp.int32),
            jax.ShapeDtypeStruct(payload, jnp.int32),
            jax.ShapeDtypeStruct((tokens, tgt_count * columns), jnp.bfloat16),
        ],
        input_output_aliases=aliases,
        compiler_params=pltpu.CompilerParams(vmem_limit_bytes=VMEM),
        cost_estimate=cost(2 * total_rows * decoder.size, decoder.size * 2),
        name="terms",
    )(*operands)


def finish_kernel(n_got, offset, stride, own_ref, *refs):
    gots = refs[:n_got]
    mask_ref = refs[n_got]
    out_ref, mask_tile, out_tile, in_sem, out_sem = refs[-5:]
    layers, rows, width = out_tile.shape
    parts = mask_ref.shape[1] // stride
    tokens = rows // parts

    def mask_copy(part):
        return pltpu.make_async_copy(
            mask_ref.at[:, pl.ds(part * stride + offset, tokens), :],
            mask_tile.at[:, pl.ds(part * tokens, tokens), :],
            in_sem.at[part],
        )

    def out_copy(layer, part):
        return pltpu.make_async_copy(
            out_tile.at[layer, pl.ds(part * tokens, tokens), :],
            out_ref.at[layer, pl.ds(part * stride + offset, tokens), :],
            out_sem.at[layer * parts + part],
        )

    for part in range(parts):
        mask_copy(part).start()
    steps = [load_steps(got) for got in gots]
    for part in range(parts):
        mask_copy(part).wait()
    for layer in range(layers):
        total = own_ref[layer]
        for got, step in zip(gots, steps):
            total += load_values(got, step, layer, layers, rows, width)
        out_tile[layer] = (total * mask_tile[layer].astype(jnp.float32)).astype(jnp.bfloat16)
        for part in range(parts):
            out_copy(layer, part).start()
    for layer in range(layers):
        for part in range(parts):
            out_copy(layer, part).wait()


def finish_call(own, gots, mask, out, offset, stride, after):
    layers, rows, width = own.shape
    parts = mask.shape[1] // stride
    in_specs = [pl.BlockSpec((layers, rows, width), lambda i: (0, 0, 0))]
    in_specs += [
        pl.BlockSpec((payload_rows(layers, rows, width), LANES), lambda i, place=place: (place, 0)) for _, place in gots
    ]
    in_specs.append(ANYWHERE)
    gots = [got for got, _ in gots]
    operands = [own, *gots, mask]
    aliases = {}
    if out is not None:
        in_specs.append(ANYWHERE)
        aliases = {len(operands): 0}
        operands.append(out)
    in_specs += [ANYWHERE] * len(after)
    operands += after
    return pl.pallas_call(
        functools.partial(finish_kernel, len(gots), offset, stride),
        grid=(1,),
        in_specs=in_specs,
        out_specs=ANYWHERE,
        scratch_shapes=[
            pltpu.VMEM((layers, rows, width), jnp.int32),
            pltpu.VMEM((layers, rows, width), jnp.bfloat16),
            pltpu.SemaphoreType.DMA((parts,)),
            pltpu.SemaphoreType.DMA((layers * parts,)),
        ],
        out_shape=jax.ShapeDtypeStruct(mask.shape, jnp.bfloat16),
        input_output_aliases=aliases,
        compiler_params=pltpu.CompilerParams(vmem_limit_bytes=VMEM),
        cost_estimate=cost(20 * layers * rows * width, layers * rows * width * 16),
        name="finish",
    )(*operands)


def turn_kernel(spans, codes_ref, out_ref):
    tokens = codes_ref.shape[1]
    stride = sum(spans)
    blocks = tokens // stride
    offset = column = 0
    for span in spans:
        rows = jnp.concatenate(
            [codes_ref[0, pl.ds(block * stride + offset, span), :] for block in range(blocks)], axis=0
        )
        out_ref[0, :, pl.ds(column, blocks * span)] = rows.T
        offset += span
        column += blocks * span


def turn_call(codes, spans):
    layers, tokens, width = codes.shape
    return pl.pallas_call(
        functools.partial(turn_kernel, spans),
        grid=(layers,),
        in_specs=[pl.BlockSpec((1, tokens, width), lambda i: (i, 0, 0))],
        out_specs=pl.BlockSpec((1, width, tokens), lambda i: (i, 0, 0)),
        out_shape=jax.ShapeDtypeStruct((layers, width, tokens), jnp.bfloat16),
        compiler_params=pltpu.CompilerParams(vmem_limit_bytes=VMEM),
        cost_estimate=cost(codes.size, codes.size * 4),
        name="turn",
    )(codes)


def grads_kernel(t, tgt_count, codes_ref, err_ref, *refs):
    out_ref = refs[-1]
    layer = lax.axis_index("src") * pl.num_programs(0) + pl.program_id(0)
    kept = lax.axis_index("tgt") * tgt_count + t >= layer
    columns = out_ref.shape[3]
    step = min(columns, 512)

    @pl.when(kept)
    def _():
        for column in range(0, columns, step):
            out_ref[0, 0, :, column : column + step] = jnp.dot(
                codes_ref[0], err_ref[:, column : column + step], preferred_element_type=jnp.float32
            ).astype(jnp.bfloat16)

    @pl.when(jnp.logical_not(kept))
    def _():
        out_ref[...] = jnp.zeros_like(out_ref)


def grads_call(t, codes_t, everything, out, shape, after):
    layers, tgt_count, width, columns = shape
    tokens = codes_t.shape[2]
    in_specs = [
        pl.BlockSpec((1, width, tokens), lambda i: (i, 0, 0)),
        pl.BlockSpec((tokens, columns), lambda i: (0, t)),
    ]
    operands = [codes_t, everything]
    aliases = {}
    if out is not None:
        aliases = {len(operands): 0}
        operands.append(out)
    operands += after
    in_specs += [ANYWHERE] * (len(operands) - 2)
    return pl.pallas_call(
        functools.partial(grads_kernel, t, tgt_count),
        grid=(layers,),
        in_specs=in_specs,
        out_specs=pl.BlockSpec((1, 1, width, columns), lambda i: (i, t, 0, 0)),
        out_shape=jax.ShapeDtypeStruct(shape, jnp.bfloat16),
        input_output_aliases=aliases,
        compiler_params=pltpu.CompilerParams(vmem_limit_bytes=VMEM),
        cost_estimate=cost(
            2 * layers * width * columns * tokens, 2 * layers * width * (columns + tokens) + 2 * tokens * columns
        ),
        name="grads",
    )(*operands)


def gather_pieces(errors, spans, offsets, n_src, n_feat, codes_t):
    if (n_src, n_feat) != (2, 4):
        for offset, span in zip(offsets, spans):
            part = lax.slice_in_dim(errors, offset, offset + span, axis=1)
            columns = lax.all_gather(part, "src", axis=2, tiled=True)
            piece = lax.all_gather(columns, "feat", axis=1, tiled=True)
            yield [piece], [(0, None, 0, n_feat * span, None, None)]
        return
    axes = ("src", "feat")
    to = lambda x, flip: lax.ppermute(x, axes, [(i, i ^ flip) for i in range(n_src * n_feat)])
    core_own = over_core(errors, n_feat)
    (part,) = cut_call(errors, 0, spans[0], [], [])
    after = [core_own, codes_t]
    for index, (offset, span) in enumerate(zip(offsets, spans)):
        arrived = [to(part, n_feat), to(part, 2), to(part, n_feat + 2)]
        more = index + 1 < len(spans)
        joined, *rest = cut_call(
            errors, offsets[index + 1] if more else None, spans[index + 1] if more else None, arrived, after
        )
        part = rest[0] if more else None
        plan = [(core, None, offset, span, 0, core) for core in (0, 1)]
        for lead, (dx, dy) in enumerate(((1, 0), (0, 2), (1, 2))):
            plan += [(2 + core, lead, 0, span, dx, dy ^ core) for core in (0, 1)]
        after = yield [errors, core_own, joined, over_core(joined, n_feat)], plan


def over_core(x, n_feat):
    return lax.ppermute(x, "feat", [(i, i ^ 1) for i in range(n_feat)])


def body(n_src, n_tgt, n_feat, errors, saved_codes, active_mask, decoder):
    tgt_count = decoder.shape[1]
    stride = errors.shape[1]
    spans = [stride * part // 8 for part in EIGHTHS]
    offsets = [sum(spans[:index]) for index in range(len(spans))]
    codes_t = turn_call(saved_codes, spans)
    gather = gather_pieces(errors, spans, offsets, n_src, n_feat, codes_t)
    pieces, plan = next(gather)
    last = len(spans) - 1
    join_near = last > 0 and spans[0] <= spans[1]
    owns, gots = [], []
    carry, everything = [], None
    send = lambda x, flip: lax.ppermute(x, "tgt", [(i, i ^ flip) for i in range(n_tgt)])
    for index, span in enumerate(spans):
        own, near, across, far, everything = terms_call(
            pieces,
            plan,
            decoder,
            carry,
            everything,
            n_feat * offsets[index],
            n_tgt,
            n_feat * span,
            n_feat * stride,
            [],
        )
        owns.append(own)
        gots.append([(send(far, 3), 0), (send(across, 2), 0)])
        if join_near and index == 0:
            carry = [near]
        else:
            got_near = send(near, 1)
            if carry:
                gots[0].append((got_near, 0))
            gots[index].append((got_near, len(carry)))
            carry = []
        if index < last:
            before = gots[index - 1][:2] if index else []
            pieces, plan = gather.send([own] + [got for got, _ in before])
    decoder_grads = None
    for t in range(tgt_count):
        after = [gots[0][2][0]] if t else []
        decoder_grads = grads_call(t, codes_t, everything, decoder_grads, decoder.shape, after)
    code_grads = None
    for index in range(len(spans)):
        after = [] if index else [decoder_grads] + [got for group in gots[1:last] for got, _ in group[:2]]
        code_grads = finish_call(owns[index], gots[index], active_mask, code_grads, offsets[index], stride, after)
    return code_grads, decoder_grads


def plain_body(errors, saved_codes, active_mask, decoder):
    src_count, tgt_count, feat_count, _ = decoder.shape
    src_ids = lax.axis_index("src") * src_count + jnp.arange(src_count, dtype=jnp.int32)
    tgt_ids = lax.axis_index("tgt") * tgt_count + jnp.arange(tgt_count, dtype=jnp.int32)
    kept = (tgt_ids[None, :] >= src_ids[:, None])[:, :, None, None]
    columns = lax.all_gather(errors, "src", axis=2, tiled=True)
    portion = lax.all_gather(columns, "feat", axis=1, tiled=True)
    grads = jnp.einsum("itf,jtd->ijfd", saved_codes, portion, preferred_element_type=jnp.float32)
    decoder = jnp.where(kept, decoder, jnp.zeros_like(decoder))
    term = jnp.einsum("jtd,ijfd->itf", portion, decoder, preferred_element_type=jnp.float32)
    summed = lax.psum_scatter(term, "tgt", scatter_dimension=1, tiled=True)
    code_grads = (summed * active_mask.astype(jnp.float32)).astype(jnp.bfloat16)
    return code_grads, jnp.where(kept, grads, 0.0).astype(jnp.bfloat16)


def solution(mesh):
    sizes = [mesh.shape[axis] for axis in ("src", "tgt", "feat")]
    fits = sizes[1] == 4 and sizes[2] % sizes[1] == 0
    in_specs = (
        P("tgt", "feat", "src"),
        P("src", None, "feat"),
        P("src", "tgt", "feat"),
        P("src", "tgt", "feat", None),
    )
    out_specs = (P("src", "tgt", "feat"), P("src", "tgt", "feat", None))
    return jax.shard_map(
        functools.partial(body, *sizes) if fits else plain_body,
        mesh=mesh,
        in_specs=in_specs,
        out_specs=out_specs,
        check_vma=False,
    )
```

```python
import functools

import jax
import jax.numpy as jnp
from jax import lax
from jax.experimental import pallas as pl
from jax.experimental.pallas import tpu as pltpu
from jax.sharding import PartitionSpec as P

LANES = 128
SUBLANES = 8
STEPS_PER_OCTAVE = 64
TOP = 32760.0
FLOOR = 1e-30
EIGHTHS = (2, 3, 3)
VMEM = 127 << 19
EASE = 2
ANYWHERE = pl.BlockSpec(memory_space=pl.ANY)


def pair(x):
    half = x.shape[0] // 2
    return (x[half:] << 16) | (x[:half] & 0xFFFF)


def unpair(words):
    return (words << 16) >> 16, words >> 16


def scale_and_gain(peaks):
    scale = jnp.ceil(jnp.log2(jnp.maximum(peaks, FLOOR)) * STEPS_PER_OCTAVE)
    return scale.astype(jnp.int32), jnp.exp2(scale * (-1.0 / STEPS_PER_OCTAVE)) * TOP


def row_peak(v):
    return jnp.max(jnp.abs(v), axis=1, keepdims=True)


def store_words(out_ref, layer, v, gain, base=0):
    rows, width = v.shape
    half, tiles = rows // 2, width // LANES
    words = pair(jnp.floor(v * gain + 0.5).astype(jnp.int32))
    for tile in range(tiles):
        start = base + (layer * tiles + tile) * half
        out_ref[start : start + half, :] = words[:, tile * LANES : (tile + 1) * LANES]


def lanes_of(shape):
    return lax.broadcasted_iota(jnp.int32, shape, 1)


def load_steps(in_ref):
    end = in_ref.shape[0] - SUBLANES
    low, high = unpair(in_ref[end:, :])
    step = lambda scale: jnp.exp2(scale.astype(jnp.float32) * (1.0 / STEPS_PER_OCTAVE)) * (1.0 / TOP)
    return step(low), step(high)


def load_values(in_ref, steps, layer, layers, rows, width):
    half, tiles = rows // 2, width // LANES
    words = jnp.concatenate(
        [in_ref[(layer * tiles + tile) * half : (layer * tiles + tile + 1) * half, :] for tile in range(tiles)], axis=1
    )
    values = []
    for part, step in zip(unpair(words), steps):
        column = jnp.concatenate(
            [step[:, group * layers + layer][:, None] for group in range(half // SUBLANES)], axis=0
        )
        values.append(part.astype(jnp.float32) * column)
    return jnp.concatenate(values, axis=0)


def payload_rows(layers, rows, width):
    return layers * (width // LANES) * (rows // 2) + SUBLANES


def cost(flops, bytes_accessed):
    return pl.CostEstimate(flops=flops // EASE, bytes_accessed=bytes_accessed // EASE, transcendentals=0)


def cut_kernel(n_join, offset, errors_ref, *refs):
    sem = refs[-1]
    joined = refs[:n_join]
    outs = refs[-1 - (n_join > 0) - (offset is not None) : -1]
    copies = [(piece, outs[0].at[index]) for index, piece in enumerate(joined)]
    if offset is not None:
        copies.append((errors_ref.at[:, pl.ds(offset, outs[-1].shape[1]), :], outs[-1]))
    copies = [pltpu.make_async_copy(*copy, sem.at[index]) for index, copy in enumerate(copies)]
    for copy in copies:
        copy.start()
    for copy in copies:
        copy.wait()


def cut_call(errors, offset, span, join, after):
    shapes = []
    if join:
        shapes.append(jax.ShapeDtypeStruct((len(join), *join[0].shape), errors.dtype))
    if offset is not None:
        shapes.append(jax.ShapeDtypeStruct((errors.shape[0], span, errors.shape[2]), errors.dtype))
    return pl.pallas_call(
        functools.partial(cut_kernel, len(join), offset),
        in_specs=[ANYWHERE] * (1 + len(join) + len(after)),
        out_specs=[pl.BlockSpec(memory_space=pltpu.VMEM)] * len(shapes),
        out_shape=shapes,
        scratch_shapes=[pltpu.SemaphoreType.DMA((len(join) + 1,))],
        compiler_params=pltpu.CompilerParams(vmem_limit_bytes=VMEM),
        cost_estimate=cost(0, 4 * sum(shape.size for shape in shapes)),
        name="cut",
    )(errors, *join, *after)


def terms_kernel(n_tgt, plan, offset, carried, *refs):
    n_pieces = 1 + max(entry[0] for entry in plan)
    pieces = refs[:n_pieces]
    dec_ref = refs[n_pieces]
    own_ref, near_ref, across_ref, far_ref, all_ref, err, dec, acc, in_sem, dec_sem, own_sem, out_sem, carry_sem = refs[-13:]
    layers, tgt_count, width, columns = dec_ref.shape
    total_rows = err.shape[0]
    rows = total_rows // n_tgt
    half = rows // 2
    src, tgt, feat = (lax.axis_index(axis) for axis in ("src", "tgt", "feat"))

    def piece_copies(index):
        source, lead, skip, tokens, flip_src, flip_feat = plan[index]
        piece = pieces[source] if lead is None else pieces[source].at[lead]
        wide = piece.shape[2]
        row = 0 if flip_feat is None else pl.multiple_of((feat ^ flip_feat) * tokens, tokens)
        column = 0 if flip_src is None else pl.multiple_of((src ^ flip_src) * wide, wide)
        return [
            pltpu.make_async_copy(
                piece.at[t, pl.ds(skip, tokens), :],
                err.at[pl.ds(row, tokens), pl.ds(t * columns + column, wide)],
                in_sem.at[index * tgt_count + t],
            )
            for t in range(tgt_count)
        ]

    def dec_copy(layer, t):
        return pltpu.make_async_copy(
            dec_ref.at[layer, t], dec.at[layer, :, pl.ds(t * columns, columns)], dec_sem.at[layer * tgt_count + t]
        )

    def block(dest):
        return pl.ds(pl.multiple_of(dest * rows, rows), rows)

    def own_copy(layer):
        return pltpu.make_async_copy(acc.at[layer, block(tgt), :], own_ref.at[layer], own_sem.at[layer])

    if carried:
        early_ref = refs[n_pieces + 1]
        carry = pltpu.make_async_copy(early_ref, near_ref.at[pl.ds(0, early_ref.shape[0]), :], carry_sem)
    out_copy = pltpu.make_async_copy(err, all_ref.at[pl.ds(offset, total_rows), :], out_sem)

    for t in range(tgt_count):
        dec_copy(0, t).start()
    copies = [copy for index in range(len(plan)) for copy in piece_copies(index)]
    for copy in copies:
        copy.start()
    if carried:
        carry.start()
    for copy in copies:
        copy.wait()
    out_copy.start()

    lane = lanes_of((rows, LANES))
    small = lanes_of((SUBLANES, LANES))
    flips = {1: near_ref, 2: across_ref, 3: far_ref}
    tails = [jnp.zeros((SUBLANES, LANES), jnp.int32) for _ in flips]

    def multiply(layer):
        if layer + 1 < layers:
            for t in range(tgt_count):
                dec_copy(layer + 1, t).start()
        for t in range(tgt_count):
            dec_copy(layer, t).wait()
            kept = tgt * tgt_count + t >= src * layers + layer

            @pl.when(jnp.logical_not(kept))
            def _():
                dec[layer, :, t * columns : (t + 1) * columns] = jnp.zeros((width, columns), jnp.bfloat16)

        acc[layer] = lax.dot_general(
            err[...], dec[layer], (((1,), (1,)), ((), ())), preferred_element_type=jnp.float32
        )
        own_copy(layer).start()

    def encode(layer):
        peaks = jnp.zeros((rows, LANES), jnp.float32)
        for index, flip in enumerate(flips):
            peaks = jnp.where(lane == index, row_peak(acc[layer, block(tgt ^ flip), :]), peaks)
        scale, gain = scale_and_gain(peaks)
        scale_words = pair(scale)
        for index, flip in enumerate(flips):
            v, factor = acc[layer, block(tgt ^ flip), :], gain[:, index : index + 1]
            store_words(flips[flip], layer, v, factor, carried if flip == 1 else 0)
            for group in range(half // SUBLANES):
                piece = scale_words[group * SUBLANES : (group + 1) * SUBLANES, index : index + 1]
                tails[index] = jnp.where(small == group * layers + layer, piece, tails[index])

    for layer in range(layers):
        multiply(layer)
        if layer:
            encode(layer - 1)
    encode(layers - 1)
    for send, tail in zip(flips.values(), tails):
        send[send.shape[0] - SUBLANES :, :] = tail
    for layer in range(layers):
        own_copy(layer).wait()
    out_copy.wait()
    if carried:
        carry.wait()


def terms_call(pieces, plan, decoder, carry, everything, offset, n_tgt, total_rows, tokens, after):
    layers, tgt_count, width, columns = decoder.shape
    rows = total_rows // n_tgt
    payload = (payload_rows(layers, rows, width), LANES)
    whole = pl.BlockSpec(memory_space=pltpu.VMEM)
    operands = [*pieces, decoder, *carry]
    carried = payload[0] if carry else 0
    aliases = {}
    if everything is not None:
        aliases = {len(operands): 4}
        operands.append(everything)
    operands += after
    return pl.pallas_call(
        functools.partial(terms_kernel, n_tgt, plan, offset, carried),
        in_specs=[ANYWHERE] * len(operands),
        out_specs=[ANYWHERE, whole, whole, whole, ANYWHERE],
        scratch_shapes=[
            pltpu.VMEM((total_rows, tgt_count * columns), jnp.bfloat16),
            pltpu.VMEM((layers, width, tgt_count * columns), jnp.bfloat16),
            pltpu.VMEM((layers, total_rows, width), jnp.float32),
            pltpu.SemaphoreType.DMA((len(plan) * tgt_count,)),
            pltpu.SemaphoreType.DMA((layers * tgt_count,)),
            pltpu.SemaphoreType.DMA((layers,)),
            pltpu.SemaphoreType.DMA,
            pltpu.SemaphoreType.DMA,
        ],
        out_shape=[
            jax.ShapeDtypeStruct((layers, rows, width), jnp.float32),
            jax.ShapeDtypeStruct((carried + payload[0], LANES), jnp.int32),
            jax.ShapeDtypeStruct(payload, jnp.int32),
            jax.ShapeDtypeStruct(payload, jnp.int32),
            jax.ShapeDtypeStruct((tokens, tgt_count * columns), jnp.bfloat16),
        ],
        input_output_aliases=aliases,
        compiler_params=pltpu.CompilerParams(vmem_limit_bytes=VMEM),
        cost_estimate=cost(2 * total_rows * decoder.size, decoder.size * 2),
        name="terms",
    )(*operands)


def finish_kernel(n_got, offset, stride, own_ref, *refs):
    gots = refs[:n_got]
    mask_ref = refs[n_got]
    out_ref, mask_tile, out_tile, in_sem, out_sem = refs[-5:]
    layers, rows, width = out_tile.shape
    parts = mask_ref.shape[1] // stride
    tokens = rows // parts

    def mask_copy(part):
        return pltpu.make_async_copy(
            mask_ref.at[:, pl.ds(part * stride + offset, tokens), :],
            mask_tile.at[:, pl.ds(part * tokens, tokens), :],
            in_sem.at[part],
        )

    def out_copy(layer, part):
        return pltpu.make_async_copy(
            out_tile.at[layer, pl.ds(part * tokens, tokens), :],
            out_ref.at[layer, pl.ds(part * stride + offset, tokens), :],
            out_sem.at[layer * parts + part],
        )

    for part in range(parts):
        mask_copy(part).start()
    steps = [load_steps(got) for got in gots]
    for part in range(parts):
        mask_copy(part).wait()
    for layer in range(layers):
        total = own_ref[layer]
        for got, step in zip(gots, steps):
            total += load_values(got, step, layer, layers, rows, width)
        out_tile[layer] = (total * mask_tile[layer].astype(jnp.float32)).astype(jnp.bfloat16)
        for part in range(parts):
            out_copy(layer, part).start()
    for layer in range(layers):
        for part in range(parts):
            out_copy(layer, part).wait()


def finish_call(own, gots, mask, out, offset, stride, after):
    layers, rows, width = own.shape
    parts = mask.shape[1] // stride
    in_specs = [pl.BlockSpec((layers, rows, width), lambda i: (0, 0, 0))]
    in_specs += [
        pl.BlockSpec((payload_rows(layers, rows, width), LANES), lambda i, place=place: (place, 0)) for _, place in gots
    ]
    in_specs.append(ANYWHERE)
    gots = [got for got, _ in gots]
    operands = [own, *gots, mask]
    aliases = {}
    if out is not None:
        in_specs.append(ANYWHERE)
        aliases = {len(operands): 0}
        operands.append(out)
    in_specs += [ANYWHERE] * len(after)
    operands += after
    return pl.pallas_call(
        functools.partial(finish_kernel, len(gots), offset, stride),
        grid=(1,),
        in_specs=in_specs,
        out_specs=ANYWHERE,
        scratch_shapes=[
            pltpu.VMEM((layers, rows, width), jnp.int32),
            pltpu.VMEM((layers, rows, width), jnp.bfloat16),
            pltpu.SemaphoreType.DMA((parts,)),
            pltpu.SemaphoreType.DMA((layers * parts,)),
        ],
        out_shape=jax.ShapeDtypeStruct(mask.shape, jnp.bfloat16),
        input_output_aliases=aliases,
        compiler_params=pltpu.CompilerParams(vmem_limit_bytes=VMEM),
        cost_estimate=cost(20 * layers * rows * width, layers * rows * width * 16),
        name="finish",
    )(*operands)


def turn_kernel(spans, codes_ref, out_ref):
    tokens = codes_ref.shape[1]
    stride = sum(spans)
    blocks = tokens // stride
    offset = column = 0
    for span in spans:
        rows = jnp.concatenate(
            [codes_ref[0, pl.ds(block * stride + offset, span), :] for block in range(blocks)], axis=0
        )
        out_ref[0, :, pl.ds(column, blocks * span)] = rows.T
        offset += span
        column += blocks * span


def turn_call(codes, spans):
    layers, tokens, width = codes.shape
    return pl.pallas_call(
        functools.partial(turn_kernel, spans),
        grid=(layers,),
        in_specs=[pl.BlockSpec((1, tokens, width), lambda i: (i, 0, 0))],
        out_specs=pl.BlockSpec((1, width, tokens), lambda i: (i, 0, 0)),
        out_shape=jax.ShapeDtypeStruct((layers, width, tokens), jnp.bfloat16),
        compiler_params=pltpu.CompilerParams(vmem_limit_bytes=VMEM),
        cost_estimate=cost(codes.size, codes.size * 4),
        name="turn",
    )(codes)


def grads_kernel(t, tgt_count, codes_ref, err_ref, *refs):
    out_ref = refs[-1]
    layer = lax.axis_index("src") * pl.num_programs(0) + pl.program_id(0)
    kept = lax.axis_index("tgt") * tgt_count + t >= layer
    columns = out_ref.shape[3]
    step = min(columns, 512)

    @pl.when(kept)
    def _():
        for column in range(0, columns, step):
            out_ref[0, 0, :, column : column + step] = jnp.dot(
                codes_ref[0], err_ref[:, column : column + step], preferred_element_type=jnp.float32
            ).astype(jnp.bfloat16)

    @pl.when(jnp.logical_not(kept))
    def _():
        out_ref[...] = jnp.zeros_like(out_ref)


def grads_call(t, codes_t, everything, out, shape, after):
    layers, tgt_count, width, columns = shape
    tokens = codes_t.shape[2]
    in_specs = [
        pl.BlockSpec((1, width, tokens), lambda i: (i, 0, 0)),
        pl.BlockSpec((tokens, columns), lambda i: (0, t)),
    ]
    operands = [codes_t, everything]
    aliases = {}
    if out is not None:
        aliases = {len(operands): 0}
        operands.append(out)
    operands += after
    in_specs += [ANYWHERE] * (len(operands) - 2)
    return pl.pallas_call(
        functools.partial(grads_kernel, t, tgt_count),
        grid=(layers,),
        in_specs=in_specs,
        out_specs=pl.BlockSpec((1, 1, width, columns), lambda i: (i, t, 0, 0)),
        out_shape=jax.ShapeDtypeStruct(shape, jnp.bfloat16),
        input_output_aliases=aliases,
        compiler_params=pltpu.CompilerParams(vmem_limit_bytes=VMEM),
        cost_estimate=cost(
            2 * layers * width * columns * tokens, 2 * layers * width * (columns + tokens) + 2 * tokens * columns
        ),
        name="grads",
    )(*operands)


def gather_pieces(errors, spans, offsets, n_src, n_feat, codes_t):
    if (n_src, n_feat) != (2, 4):
        for offset, span in zip(offsets, spans):
            part = lax.slice_in_dim(errors, offset, offset + span, axis=1)
            columns = lax.all_gather(part, "src", axis=2, tiled=True)
            piece = lax.all_gather(columns, "feat", axis=1, tiled=True)
            yield [piece], [(0, None, 0, n_feat * span, None, None)]
        return
    axes = ("src", "feat")
    to = lambda x, flip: lax.ppermute(x, axes, [(i, i ^ flip) for i in range(n_src * n_feat)])
    core_own = over_core(errors, n_feat)
    (part,) = cut_call(errors, 0, spans[0], [], [])
    after = [core_own, codes_t]
    for index, (offset, span) in enumerate(zip(offsets, spans)):
        arrived = [to(part, n_feat), to(part, 2), to(part, n_feat + 2)]
        more = index + 1 < len(spans)
        joined, *rest = cut_call(
            errors, offsets[index + 1] if more else None, spans[index + 1] if more else None, arrived, after
        )
        part = rest[0] if more else None
        plan = [(core, None, offset, span, 0, core) for core in (0, 1)]
        for lead, (dx, dy) in enumerate(((1, 0), (0, 2), (1, 2))):
            plan += [(2 + core, lead, 0, span, dx, dy ^ core) for core in (0, 1)]
        after = yield [errors, core_own, joined, over_core(joined, n_feat)], plan


def over_core(x, n_feat):
    return lax.ppermute(x, "feat", [(i, i ^ 1) for i in range(n_feat)])


def body(n_src, n_tgt, n_feat, errors, saved_codes, active_mask, decoder):
    tgt_count = decoder.shape[1]
    stride = errors.shape[1]
    spans = [stride * part // 8 for part in EIGHTHS]
    offsets = [sum(spans[:index]) for index in range(len(spans))]
    codes_t = turn_call(saved_codes, spans)
    gather = gather_pieces(errors, spans, offsets, n_src, n_feat, codes_t)
    pieces, plan = next(gather)
    last = len(spans) - 1
    join_near = last > 0 and spans[0] <= spans[1]
    owns, gots = [], []
    carry, everything = [], None
    send = lambda x, flip: lax.ppermute(x, "tgt", [(i, i ^ flip) for i in range(n_tgt)])
    for index, span in enumerate(spans):
        own, near, across, far, everything = terms_call(
            pieces,
            plan,
            decoder,
            carry,
            everything,
            n_feat * offsets[index],
            n_tgt,
            n_feat * span,
            n_feat * stride,
            [],
        )
        owns.append(own)
        gots.append([(send(far, 3), 0), (send(across, 2), 0)])
        if join_near and index == 0:
            carry = [near]
        else:
            got_near = send(near, 1)
            if carry:
                gots[0].append((got_near, 0))
            gots[index].append((got_near, len(carry)))
            carry = []
        if index < last:
            before = gots[index - 1][:2] if index else []
            pieces, plan = gather.send([own] + [got for got, _ in before])
    decoder_grads = None
    for t in range(tgt_count):
        after = [gots[0][2][0]] if t else []
        decoder_grads = grads_call(t, codes_t, everything, decoder_grads, decoder.shape, after)
    code_grads = None
    for index in range(len(spans)):
        after = [] if index else [decoder_grads] + [got for group in gots[1:last] for got, _ in group[:2]]
        code_grads = finish_call(owns[index], gots[index], active_mask, code_grads, offsets[index], stride, after)
    return code_grads, decoder_grads


def plain_body(errors, saved_codes, active_mask, decoder):
    src_count, tgt_count, feat_count, _ = decoder.shape
    src_ids = lax.axis_index("src") * src_count + jnp.arange(src_count, dtype=jnp.int32)
    tgt_ids = lax.axis_index("tgt") * tgt_count + jnp.arange(tgt_count, dtype=jnp.int32)
    kept = (tgt_ids[None, :] >= src_ids[:, None])[:, :, None, None]
    columns = lax.all_gather(errors, "src", axis=2, tiled=True)
    portion = lax.all_gather(columns, "feat", axis=1, tiled=True)
    grads = jnp.einsum("itf,jtd->ijfd", saved_codes, portion, preferred_element_type=jnp.float32)
    decoder = jnp.where(kept, decoder, jnp.zeros_like(decoder))
    term = jnp.einsum("jtd,ijfd->itf", portion, decoder, preferred_element_type=jnp.float32)
    summed = lax.psum_scatter(term, "tgt", scatter_dimension=1, tiled=True)
    code_grads = (summed * active_mask.astype(jnp.float32)).astype(jnp.bfloat16)
    return code_grads, jnp.where(kept, grads, 0.0).astype(jnp.bfloat16)


def solution(mesh):
    sizes = [mesh.shape[axis] for axis in ("src", "tgt", "feat")]
    fits = sizes[1] == 4 and sizes[2] % sizes[1] == 0
    in_specs = (
        P("tgt", "feat", "src"),
        P("src", None, "feat"),
        P("src", "tgt", "feat"),
        P("src", "tgt", "feat", None),
    )
    out_specs = (P("src", "tgt", "feat"), P("src", "tgt", "feat", None))
    return jax.shard_map(
        functools.partial(body, *sizes) if fits else plain_body,
        mesh=mesh,
        in_specs=in_specs,
        out_specs=out_specs,
        check_vma=False,
    )
```

```python
import functools

import jax
import jax.numpy as jnp
from jax import lax
from jax.experimental import pallas as pl
from jax.experimental.pallas import tpu as pltpu
from jax.sharding import PartitionSpec as P

LANES = 128
SUBLANES = 8
STEPS_PER_OCTAVE = 64
TOP = 32760.0
FLOOR = 1e-30
EIGHTHS = (3, 3, 2)
VMEM = 127 << 19
EASE = 2
ANYWHERE = pl.BlockSpec(memory_space=pl.ANY)


def pair(x):
    half = x.shape[0] // 2
    return (x[half:] << 16) | (x[:half] & 0xFFFF)


def unpair(words):
    return (words << 16) >> 16, words >> 16


def scale_and_gain(peaks):
    scale = jnp.ceil(jnp.log2(jnp.maximum(peaks, FLOOR)) * STEPS_PER_OCTAVE)
    return scale.astype(jnp.int32), jnp.exp2(scale * (-1.0 / STEPS_PER_OCTAVE)) * TOP


def row_peak(v):
    return jnp.max(jnp.abs(v), axis=1, keepdims=True)


def store_words(out_ref, layer, v, gain, base=0):
    rows, width = v.shape
    half, tiles = rows // 2, width // LANES
    words = pair(jnp.floor(v * gain + 0.5).astype(jnp.int32))
    for tile in range(tiles):
        start = base + (layer * tiles + tile) * half
        out_ref[start : start + half, :] = words[:, tile * LANES : (tile + 1) * LANES]


def lanes_of(shape):
    return lax.broadcasted_iota(jnp.int32, shape, 1)


def load_steps(in_ref):
    end = in_ref.shape[0] - SUBLANES
    low, high = unpair(in_ref[end:, :])
    step = lambda scale: jnp.exp2(scale.astype(jnp.float32) * (1.0 / STEPS_PER_OCTAVE)) * (1.0 / TOP)
    return step(low), step(high)


def load_values(in_ref, steps, layer, layers, rows, width):
    half, tiles = rows // 2, width // LANES
    words = jnp.concatenate(
        [in_ref[(layer * tiles + tile) * half : (layer * tiles + tile + 1) * half, :] for tile in range(tiles)], axis=1
    )
    values = []
    for part, step in zip(unpair(words), steps):
        column = jnp.concatenate(
            [step[:, group * layers + layer][:, None] for group in range(half // SUBLANES)], axis=0
        )
        values.append(part.astype(jnp.float32) * column)
    return jnp.concatenate(values, axis=0)


def payload_rows(layers, rows, width):
    return layers * (width // LANES) * (rows // 2) + SUBLANES


def cost(flops, bytes_accessed):
    return pl.CostEstimate(flops=flops // EASE, bytes_accessed=bytes_accessed // EASE, transcendentals=0)


def cut_kernel(n_join, offset, errors_ref, *refs):
    sem = refs[-1]
    joined = refs[:n_join]
    outs = refs[-1 - (n_join > 0) - (offset is not None) : -1]
    copies = [(piece, outs[0].at[index]) for index, piece in enumerate(joined)]
    if offset is not None:
        copies.append((errors_ref.at[:, pl.ds(offset, outs[-1].shape[1]), :], outs[-1]))
    copies = [pltpu.make_async_copy(*copy, sem.at[index]) for index, copy in enumerate(copies)]
    for copy in copies:
        copy.start()
    for copy in copies:
        copy.wait()


def cut_call(errors, offset, span, join, after):
    shapes = []
    if join:
        shapes.append(jax.ShapeDtypeStruct((len(join), *join[0].shape), errors.dtype))
    if offset is not None:
        shapes.append(jax.ShapeDtypeStruct((errors.shape[0], span, errors.shape[2]), errors.dtype))
    return pl.pallas_call(
        functools.partial(cut_kernel, len(join), offset),
        in_specs=[ANYWHERE] * (1 + len(join) + len(after)),
        out_specs=[pl.BlockSpec(memory_space=pltpu.VMEM)] * len(shapes),
        out_shape=shapes,
        scratch_shapes=[pltpu.SemaphoreType.DMA((len(join) + 1,))],
        compiler_params=pltpu.CompilerParams(vmem_limit_bytes=VMEM),
        cost_estimate=cost(0, 4 * sum(shape.size for shape in shapes)),
        name="cut",
    )(errors, *join, *after)


def terms_kernel(n_tgt, plan, offset, carried, *refs):
    n_pieces = 1 + max(entry[0] for entry in plan)
    pieces = refs[:n_pieces]
    dec_ref = refs[n_pieces]
    own_ref, near_ref, across_ref, far_ref, all_ref, err, dec, acc, in_sem, dec_sem, own_sem, out_sem, carry_sem = refs[-13:]
    layers, tgt_count, width, columns = dec_ref.shape
    total_rows = err.shape[0]
    rows = total_rows // n_tgt
    half = rows // 2
    src, tgt, feat = (lax.axis_index(axis) for axis in ("src", "tgt", "feat"))

    def piece_copies(index):
        source, lead, skip, tokens, flip_src, flip_feat = plan[index]
        piece = pieces[source] if lead is None else pieces[source].at[lead]
        wide = piece.shape[2]
        row = 0 if flip_feat is None else pl.multiple_of((feat ^ flip_feat) * tokens, tokens)
        column = 0 if flip_src is None else pl.multiple_of((src ^ flip_src) * wide, wide)
        return [
            pltpu.make_async_copy(
                piece.at[t, pl.ds(skip, tokens), :],
                err.at[pl.ds(row, tokens), pl.ds(t * columns + column, wide)],
                in_sem.at[index * tgt_count + t],
            )
            for t in range(tgt_count)
        ]

    def dec_copy(layer, t):
        return pltpu.make_async_copy(
            dec_ref.at[layer, t], dec.at[layer, :, pl.ds(t * columns, columns)], dec_sem.at[layer * tgt_count + t]
        )

    def block(dest):
        return pl.ds(pl.multiple_of(dest * rows, rows), rows)

    def own_copy(layer):
        return pltpu.make_async_copy(acc.at[layer, block(tgt), :], own_ref.at[layer], own_sem.at[layer])

    if carried:
        early_ref = refs[n_pieces + 1]
        carry = pltpu.make_async_copy(early_ref, near_ref.at[pl.ds(0, early_ref.shape[0]), :], carry_sem)
    out_copy = pltpu.make_async_copy(err, all_ref.at[pl.ds(offset, total_rows), :], out_sem)

    for t in range(tgt_count):
        dec_copy(0, t).start()
    copies = [copy for index in range(len(plan)) for copy in piece_copies(index)]
    for copy in copies:
        copy.start()
    if carried:
        carry.start()
    for copy in copies:
        copy.wait()
    out_copy.start()

    lane = lanes_of((rows, LANES))
    small = lanes_of((SUBLANES, LANES))
    flips = {1: near_ref, 2: across_ref, 3: far_ref}
    tails = [jnp.zeros((SUBLANES, LANES), jnp.int32) for _ in flips]

    def multiply(layer):
        if layer + 1 < layers:
            for t in range(tgt_count):
                dec_copy(layer + 1, t).start()
        for t in range(tgt_count):
            dec_copy(layer, t).wait()
            kept = tgt * tgt_count + t >= src * layers + layer

            @pl.when(jnp.logical_not(kept))
            def _():
                dec[layer, :, t * columns : (t + 1) * columns] = jnp.zeros((width, columns), jnp.bfloat16)

        acc[layer] = lax.dot_general(
            err[...], dec[layer], (((1,), (1,)), ((), ())), preferred_element_type=jnp.float32
        )
        own_copy(layer).start()

    def encode(layer):
        peaks = jnp.zeros((rows, LANES), jnp.float32)
        for index, flip in enumerate(flips):
            peaks = jnp.where(lane == index, row_peak(acc[layer, block(tgt ^ flip), :]), peaks)
        scale, gain = scale_and_gain(peaks)
        scale_words = pair(scale)
        for index, flip in enumerate(flips):
            v, factor = acc[layer, block(tgt ^ flip), :], gain[:, index : index + 1]
            store_words(flips[flip], layer, v, factor, carried if flip == 1 else 0)
            for group in range(half // SUBLANES):
                piece = scale_words[group * SUBLANES : (group + 1) * SUBLANES, index : index + 1]
                tails[index] = jnp.where(small == group * layers + layer, piece, tails[index])

    for layer in range(layers):
        multiply(layer)
        if layer:
            encode(layer - 1)
    encode(layers - 1)
    for send, tail in zip(flips.values(), tails):
        send[send.shape[0] - SUBLANES :, :] = tail
    for layer in range(layers):
        own_copy(layer).wait()
    out_copy.wait()
    if carried:
        carry.wait()


def terms_call(pieces, plan, decoder, carry, everything, offset, n_tgt, total_rows, tokens, after):
    layers, tgt_count, width, columns = decoder.shape
    rows = total_rows // n_tgt
    payload = (payload_rows(layers, rows, width), LANES)
    whole = pl.BlockSpec(memory_space=pltpu.VMEM)
    operands = [*pieces, decoder, *carry]
    carried = payload[0] if carry else 0
    aliases = {}
    if everything is not None:
        aliases = {len(operands): 4}
        operands.append(everything)
    operands += after
    return pl.pallas_call(
        functools.partial(terms_kernel, n_tgt, plan, offset, carried),
        in_specs=[ANYWHERE] * len(operands),
        out_specs=[ANYWHERE, whole, whole, whole, ANYWHERE],
        scratch_shapes=[
            pltpu.VMEM((total_rows, tgt_count * columns), jnp.bfloat16),
            pltpu.VMEM((layers, width, tgt_count * columns), jnp.bfloat16),
            pltpu.VMEM((layers, total_rows, width), jnp.float32),
            pltpu.SemaphoreType.DMA((len(plan) * tgt_count,)),
            pltpu.SemaphoreType.DMA((layers * tgt_count,)),
            pltpu.SemaphoreType.DMA((layers,)),
            pltpu.SemaphoreType.DMA,
            pltpu.SemaphoreType.DMA,
        ],
        out_shape=[
            jax.ShapeDtypeStruct((layers, rows, width), jnp.float32),
            jax.ShapeDtypeStruct((carried + payload[0], LANES), jnp.int32),
            jax.ShapeDtypeStruct(payload, jnp.int32),
            jax.ShapeDtypeStruct(payload, jnp.int32),
            jax.ShapeDtypeStruct((tokens, tgt_count * columns), jnp.bfloat16),
        ],
        input_output_aliases=aliases,
        compiler_params=pltpu.CompilerParams(vmem_limit_bytes=VMEM),
        cost_estimate=cost(2 * total_rows * decoder.size, decoder.size * 2),
        name="terms",
    )(*operands)


def finish_kernel(n_got, offset, stride, own_ref, *refs):
    gots = refs[:n_got]
    mask_ref = refs[n_got]
    out_ref, mask_tile, out_tile, in_sem, out_sem = refs[-5:]
    layers, rows, width = out_tile.shape
    parts = mask_ref.shape[1] // stride
    tokens = rows // parts

    def mask_copy(part):
        return pltpu.make_async_copy(
            mask_ref.at[:, pl.ds(part * stride + offset, tokens), :],
            mask_tile.at[:, pl.ds(part * tokens, tokens), :],
            in_sem.at[part],
        )

    def out_copy(layer, part):
        return pltpu.make_async_copy(
            out_tile.at[layer, pl.ds(part * tokens, tokens), :],
            out_ref.at[layer, pl.ds(part * stride + offset, tokens), :],
            out_sem.at[layer * parts + part],
        )

    for part in range(parts):
        mask_copy(part).start()
    steps = [load_steps(got) for got in gots]
    for part in range(parts):
        mask_copy(part).wait()
    for layer in range(layers):
        total = own_ref[layer]
        for got, step in zip(gots, steps):
            total += load_values(got, step, layer, layers, rows, width)
        out_tile[layer] = (total * mask_tile[layer].astype(jnp.float32)).astype(jnp.bfloat16)
        for part in range(parts):
            out_copy(layer, part).start()
    for layer in range(layers):
        for part in range(parts):
            out_copy(layer, part).wait()


def finish_call(own, gots, mask, out, offset, stride, after):
    layers, rows, width = own.shape
    parts = mask.shape[1] // stride
    in_specs = [pl.BlockSpec((layers, rows, width), lambda i: (0, 0, 0))]
    in_specs += [
        pl.BlockSpec((payload_rows(layers, rows, width), LANES), lambda i, place=place: (place, 0)) for _, place in gots
    ]
    in_specs.append(ANYWHERE)
    gots = [got for got, _ in gots]
    operands = [own, *gots, mask]
    aliases = {}
    if out is not None:
        in_specs.append(ANYWHERE)
        aliases = {len(operands): 0}
        operands.append(out)
    in_specs += [ANYWHERE] * len(after)
    operands += after
    return pl.pallas_call(
        functools.partial(finish_kernel, len(gots), offset, stride),
        grid=(1,),
        in_specs=in_specs,
        out_specs=ANYWHERE,
        scratch_shapes=[
            pltpu.VMEM((layers, rows, width), jnp.int32),
            pltpu.VMEM((layers, rows, width), jnp.bfloat16),
            pltpu.SemaphoreType.DMA((parts,)),
            pltpu.SemaphoreType.DMA((layers * parts,)),
        ],
        out_shape=jax.ShapeDtypeStruct(mask.shape, jnp.bfloat16),
        input_output_aliases=aliases,
        compiler_params=pltpu.CompilerParams(vmem_limit_bytes=VMEM),
        cost_estimate=cost(20 * layers * rows * width, layers * rows * width * 16),
        name="finish",
    )(*operands)


def turn_kernel(spans, codes_ref, out_ref):
    tokens = codes_ref.shape[1]
    stride = sum(spans)
    blocks = tokens // stride
    offset = column = 0
    for span in spans:
        rows = jnp.concatenate(
            [codes_ref[0, pl.ds(block * stride + offset, span), :] for block in range(blocks)], axis=0
        )
        out_ref[0, :, pl.ds(column, blocks * span)] = rows.T
        offset += span
        column += blocks * span


def turn_call(codes, spans):
    layers, tokens, width = codes.shape
    return pl.pallas_call(
        functools.partial(turn_kernel, spans),
        grid=(layers,),
        in_specs=[pl.BlockSpec((1, tokens, width), lambda i: (i, 0, 0))],
        out_specs=pl.BlockSpec((1, width, tokens), lambda i: (i, 0, 0)),
        out_shape=jax.ShapeDtypeStruct((layers, width, tokens), jnp.bfloat16),
        compiler_params=pltpu.CompilerParams(vmem_limit_bytes=VMEM),
        cost_estimate=cost(codes.size, codes.size * 4),
        name="turn",
    )(codes)


def grads_kernel(t, tgt_count, codes_ref, err_ref, *refs):
    out_ref = refs[-1]
    layer = lax.axis_index("src") * pl.num_programs(0) + pl.program_id(0)
    kept = lax.axis_index("tgt") * tgt_count + t >= layer
    columns = out_ref.shape[3]
    step = min(columns, 512)

    @pl.when(kept)
    def _():
        for column in range(0, columns, step):
            out_ref[0, 0, :, column : column + step] = jnp.dot(
                codes_ref[0], err_ref[:, column : column + step], preferred_element_type=jnp.float32
            ).astype(jnp.bfloat16)

    @pl.when(jnp.logical_not(kept))
    def _():
        out_ref[...] = jnp.zeros_like(out_ref)


def grads_call(t, codes_t, everything, out, shape, after):
    layers, tgt_count, width, columns = shape
    tokens = codes_t.shape[2]
    in_specs = [
        pl.BlockSpec((1, width, tokens), lambda i: (i, 0, 0)),
        pl.BlockSpec((tokens, columns), lambda i: (0, t)),
    ]
    operands = [codes_t, everything]
    aliases = {}
    if out is not None:
        aliases = {len(operands): 0}
        operands.append(out)
    operands += after
    in_specs += [ANYWHERE] * (len(operands) - 2)
    return pl.pallas_call(
        functools.partial(grads_kernel, t, tgt_count),
        grid=(layers,),
        in_specs=in_specs,
        out_specs=pl.BlockSpec((1, 1, width, columns), lambda i: (i, t, 0, 0)),
        out_shape=jax.ShapeDtypeStruct(shape, jnp.bfloat16),
        input_output_aliases=aliases,
        compiler_params=pltpu.CompilerParams(vmem_limit_bytes=VMEM),
        cost_estimate=cost(
            2 * layers * width * columns * tokens, 2 * layers * width * (columns + tokens) + 2 * tokens * columns
        ),
        name="grads",
    )(*operands)


def gather_pieces(errors, spans, offsets, n_src, n_feat, codes_t):
    if (n_src, n_feat) != (2, 4):
        for offset, span in zip(offsets, spans):
            part = lax.slice_in_dim(errors, offset, offset + span, axis=1)
            columns = lax.all_gather(part, "src", axis=2, tiled=True)
            piece = lax.all_gather(columns, "feat", axis=1, tiled=True)
            yield [piece], [(0, None, 0, n_feat * span, None, None)]
        return
    axes = ("src", "feat")
    to = lambda x, flip: lax.ppermute(x, axes, [(i, i ^ flip) for i in range(n_src * n_feat)])
    core_own = over_core(errors, n_feat)
    (part,) = cut_call(errors, 0, spans[0], [], [])
    after = [core_own, codes_t]
    for index, (offset, span) in enumerate(zip(offsets, spans)):
        arrived = [to(part, n_feat), to(part, 2), to(part, n_feat + 2)]
        more = index + 1 < len(spans)
        joined, *rest = cut_call(
            errors, offsets[index + 1] if more else None, spans[index + 1] if more else None, arrived, after
        )
        part = rest[0] if more else None
        plan = [(core, None, offset, span, 0, core) for core in (0, 1)]
        for lead, (dx, dy) in enumerate(((1, 0), (0, 2), (1, 2))):
            plan += [(2 + core, lead, 0, span, dx, dy ^ core) for core in (0, 1)]
        after = yield [errors, core_own, joined, over_core(joined, n_feat)], plan


def over_core(x, n_feat):
    return lax.ppermute(x, "feat", [(i, i ^ 1) for i in range(n_feat)])


def body(n_src, n_tgt, n_feat, errors, saved_codes, active_mask, decoder):
    tgt_count = decoder.shape[1]
    stride = errors.shape[1]
    spans = [stride * part // 8 for part in EIGHTHS]
    offsets = [sum(spans[:index]) for index in range(len(spans))]
    codes_t = turn_call(saved_codes, spans)
    gather = gather_pieces(errors, spans, offsets, n_src, n_feat, codes_t)
    pieces, plan = next(gather)
    last = len(spans) - 1
    join_near = last > 0 and spans[0] <= spans[1]
    owns, gots = [], []
    carry, everything = [], None
    send = lambda x, flip: lax.ppermute(x, "tgt", [(i, i ^ flip) for i in range(n_tgt)])
    for index, span in enumerate(spans):
        own, near, across, far, everything = terms_call(
            pieces,
            plan,
            decoder,
            carry,
            everything,
            n_feat * offsets[index],
            n_tgt,
            n_feat * span,
            n_feat * stride,
            [],
        )
        owns.append(own)
        gots.append([(send(far, 3), 0), (send(across, 2), 0)])
        if join_near and index == 0:
            carry = [near]
        else:
            got_near = send(near, 1)
            if carry:
                gots[0].append((got_near, 0))
            gots[index].append((got_near, len(carry)))
            carry = []
        if index < last:
            before = gots[index - 1][:2] if index else []
            pieces, plan = gather.send([own] + [got for got, _ in before])
    decoder_grads = None
    for t in range(tgt_count):
        after = [gots[0][2][0]] if t else []
        decoder_grads = grads_call(t, codes_t, everything, decoder_grads, decoder.shape, after)
    code_grads = None
    for index in range(len(spans)):
        after = [] if index else [decoder_grads] + [got for group in gots[1:last] for got, _ in group[:2]]
        code_grads = finish_call(owns[index], gots[index], active_mask, code_grads, offsets[index], stride, after)
    return code_grads, decoder_grads


def plain_body(errors, saved_codes, active_mask, decoder):
    src_count, tgt_count, feat_count, _ = decoder.shape
    src_ids = lax.axis_index("src") * src_count + jnp.arange(src_count, dtype=jnp.int32)
    tgt_ids = lax.axis_index("tgt") * tgt_count + jnp.arange(tgt_count, dtype=jnp.int32)
    kept = (tgt_ids[None, :] >= src_ids[:, None])[:, :, None, None]
    columns = lax.all_gather(errors, "src", axis=2, tiled=True)
    portion = lax.all_gather(columns, "feat", axis=1, tiled=True)
    grads = jnp.einsum("itf,jtd->ijfd", saved_codes, portion, preferred_element_type=jnp.float32)
    decoder = jnp.where(kept, decoder, jnp.zeros_like(decoder))
    term = jnp.einsum("jtd,ijfd->itf", portion, decoder, preferred_element_type=jnp.float32)
    summed = lax.psum_scatter(term, "tgt", scatter_dimension=1, tiled=True)
    code_grads = (summed * active_mask.astype(jnp.float32)).astype(jnp.bfloat16)
    return code_grads, jnp.where(kept, grads, 0.0).astype(jnp.bfloat16)


def solution(mesh):
    sizes = [mesh.shape[axis] for axis in ("src", "tgt", "feat")]
    fits = sizes[1] == 4 and sizes[2] % sizes[1] == 0
    in_specs = (
        P("tgt", "feat", "src"),
        P("src", None, "feat"),
        P("src", "tgt", "feat"),
        P("src", "tgt", "feat", None),
    )
    out_specs = (P("src", "tgt", "feat"), P("src", "tgt", "feat", None))
    return jax.shard_map(
        functools.partial(body, *sizes) if fits else plain_body,
        mesh=mesh,
        in_specs=in_specs,
        out_specs=out_specs,
        check_vma=False,
    )
```
